128 devices in a mesh: dp: 32 (over x, z, y_lo), tensor: 4 (over y_hi, core).
Axes of the slice: x: 4, y: 4 (y_hi: 2, y_lo: 2; y = y_hi * 2 + y_lo), z: 4, core: 2. Of those that a mesh axis runs over, the one named last changes fastest.
Arguments:
- entering_activations: bfloat16 [32768, 768], P('dp'), may hold values from -6 to 6
- sample_sizes: int32 [32, 16], P('dp'), may hold values from 0 to 1024, as said below
- initial_layernorm_scale: float32 [768], replicated, may hold values from 0.5 to 1.5
- initial_layernorm_offset: float32 [768], replicated, may hold values from -3 to 3
- temporal_lookup_fraction: float32 [768], replicated, may hold values from 0 to 1
- temporal_content_fraction: float32 [768], replicated, may hold values from 0 to 1
- temporal_gating_fraction: float32 [768], replicated, may hold values from 0 to 1
- fading_speed_logarithm: float32 [768], replicated, may hold values from -9 to -1.5
- present_reward: float32 [768], replicated, may hold values from -1 to 1
- temporal_gating_matrix: bfloat16 [768, 768], replicated, may hold values from -0.21875 to 0.21875
- temporal_lookup_matrix: bfloat16 [768, 768], replicated, may hold values from -0.21875 to 0.21875
- temporal_content_matrix: bfloat16 [768, 768], replicated, may hold values from -0.21875 to 0.21875
- temporal_emission_matrix: bfloat16 [768, 768], replicated, may hold values from -0.875 to 0.875
- latter_layernorm_scale: float32 [768], replicated, may hold values from 0.5 to 1.5
- latter_layernorm_offset: float32 [768], replicated, may hold values from -3 to 3
- feedforward_lookup_fraction: float32 [768], replicated, may hold values from 0 to 1
- feedforward_gating_fraction: float32 [768], replicated, may hold values from 0 to 1
- feedforward_gating_matrix: bfloat16 [768, 768], replicated, may hold values from -0.21875 to 0.21875
- feedforward_lookup_matrix: bfloat16 [768, 3072], P(None, 'tensor'), may hold values from -0.21875 to 0.21875
- feedforward_content_matrix: bfloat16 [3072, 768], P('tensor'), may hold values from -0.109375 to 0.109375
- upstream_adjoint: bfloat16 [32768, 768], P('dp'), may hold values from -6 to 6
Outputs:
- out: bfloat16 [32768, 768], P('dp')
- grad_inputs: float32 [32768, 768], P('dp')
- grad_norm1_gain: float32 [768], replicated
- grad_norm1_bias: float32 [768], replicated
- grad_mix_key: float32 [768], replicated
- grad_mix_value: float32 [768], replicated
- grad_mix_recept: float32 [768], replicated
- gradient_log_decay: float32 [768], replicated
- present_reward_derivative: float32 [768], replicated
- grad_recept_weight: float32 [768, 768], replicated
- grad_key_weight: float32 [768, 768], replicated
- grad_value_weight: float32 [768, 768], replicated
- grad_output_weight: float32 [768, 768], replicated
- grad_norm2_gain: float32 [768], replicated
- grad_norm2_bias: float32 [768], replicated
- grad_chan_mix_key: float32 [768], replicated
- grad_chan_mix_recept: float32 [768], replicated
- grad_chan_recept: float32 [768, 768], replicated
- grad_chan_key: float32 [768, 3072], P(None, 'tensor')
- grad_chan_value: float32 [3072, 768], P('tensor')
The draws below stay inside these ranges and needn't reach their ends.
Inputs may be any that keep to these rules, and one draw needn't show every extreme that they name: `sample_sizes`: row g lists, in order from position 0, the lengths of the sequences packed into the 1024 positions of data device g. Every length is a multiple of 64; nonzero lengths come first, and their sum lies between 512 and 1024; positions after it are padding. On one device, drawn from the seed, a single sequence fills all 1024 positions.
All inputs are finite; a program needn't handle non-finite values.
Results may differ from the reference program's by a relative error of at most 0.0095.
Values sent between devices are 32-bit elements; how exact they have to be, the bound alone decides.
A program may use at most 192 MiB of HBM per device.

```python
import jax
import jax.numpy as jnp
from jax import lax

FEATURE_DIM = 768
FF = 3072
TOK_DEV = 1024
COUNT_RANGE = 64
GROUPS = 32
TOKENS = 32768


def draw_sample_sizes(key, part):
    key = jax.random.fold_in(key, 7)
    subkeys = jax.random.split(key, 4)
    units = TOK_DEV // COUNT_RANGE
    budget = jax.random.randint(subkeys[0], (GROUPS,), units // 2, units + 1)
    chosen = jax.random.randint(subkeys[1], (), 0, GROUPS)
    owner = jnp.arange(GROUPS) == chosen
    budget = jnp.where(owner, units, budget)
    first_pick = jax.random.randint(subkeys[2], (GROUPS, units), 0, 5)
    second_pick = jax.random.randint(subkeys[3], (GROUPS, units), 0, 5)
    wanted = jnp.minimum(jnp.power(2, jnp.minimum(first_pick, second_pick)), units)
    leading = (jnp.arange(units) == 0)[None, :] & owner[:, None]
    wanted = jnp.where(leading, units, wanted)
    before = jnp.cumsum(wanted, axis=1) - wanted
    taken = jnp.clip(budget[:, None] - before, 0, wanted)
    return (taken * COUNT_RANGE).astype(jnp.int32)


def block_levels(rng, shape, cuts, low, largest):
    level = 1.0
    for axis_at, blocks in cuts:
        draws = jax.random.uniform(jax.random.fold_in(jax.random.fold_in(rng, 6), axis_at), (blocks,), jnp.float32, low / len(cuts), largest / len(cuts))
        level = level * jnp.repeat(jnp.exp(draws), shape[axis_at] // blocks).reshape((-1,) + (1,) * (len(shape) - 1 - axis_at))
    return level


def bell_draw(own_key, extent, scale, reach, pieces=(), kind=jnp.bfloat16):
    drawn = jax.random.normal(own_key, extent, jnp.float32) * scale
    if len(pieces) > 0:
        drawn = block_levels(own_key, extent, pieces, -0.22, 0.18) * drawn
    return jnp.clip(drawn, min=-reach, max=reach).astype(kind)


def setup_inputs(seed: int = 0) -> dict:
    seeds = jax.random.split(jax.random.key(seed), 22)
    entering_activations = bell_draw(seeds[0], (TOKENS, FEATURE_DIM), 1.0, 6.0, ((0, 32),))
    sample_sizes = draw_sample_sizes(jax.random.fold_in(seeds[21], 71), 0)
    initial_layernorm_scale = jnp.clip(1.0 + 0.1 * jax.random.normal(seeds[2], (FEATURE_DIM,), jnp.float32), 0.5, 1.5)
    initial_layernorm_offset = bell_draw(seeds[3], (FEATURE_DIM,), 0.3, 3.0, (), jnp.float32)
    temporal_lookup_fraction = jnp.clip(jax.random.uniform(seeds[4], (FEATURE_DIM,), jnp.float32, 0.0, 1.0), 0.0, 1.0)
    temporal_content_fraction = jnp.clip(jax.random.uniform(seeds[5], (FEATURE_DIM,), jnp.float32, 0.0, 1.0), 0.0, 1.0)
    temporal_gating_fraction = jnp.clip(jax.random.uniform(seeds[6], (FEATURE_DIM,), jnp.float32, 0.0, 1.0), 0.0, 1.0)
    fading_speed_logarithm = jnp.clip(jax.random.uniform(seeds[7], (FEATURE_DIM,), jnp.float32, -9.0, -1.5), -9.0, -1.5)
    present_reward = jnp.clip(jax.random.uniform(seeds[8], (FEATURE_DIM,), jnp.float32, -1.0, 1.0), -1.0, 1.0)
    temporal_gating_matrix = bell_draw(seeds[9], (FEATURE_DIM, FEATURE_DIM), FEATURE_DIM ** -0.5, 0.21875)
    temporal_lookup_matrix = bell_draw(seeds[10], (FEATURE_DIM, FEATURE_DIM), FEATURE_DIM ** -0.5, 0.21875)
    temporal_content_matrix = bell_draw(seeds[11], (FEATURE_DIM, FEATURE_DIM), FEATURE_DIM ** -0.5, 0.21875)
    temporal_emission_matrix = bell_draw(seeds[12], (FEATURE_DIM, FEATURE_DIM), (FEATURE_DIM // 16) ** -0.5, 0.875)
    latter_layernorm_scale = jnp.clip(1.0 + 0.1 * jax.random.normal(seeds[13], (FEATURE_DIM,), jnp.float32), 0.5, 1.5)
    latter_layernorm_offset = bell_draw(seeds[14], (FEATURE_DIM,), 0.3, 3.0, (), jnp.float32)
    feedforward_lookup_fraction = jnp.clip(jax.random.uniform(seeds[15], (FEATURE_DIM,), jnp.float32, 0.0, 1.0), 0.0, 1.0)
    feedforward_gating_fraction = jnp.clip(jax.random.uniform(seeds[16], (FEATURE_DIM,), jnp.float32, 0.0, 1.0), 0.0, 1.0)
    feedforward_gating_matrix = bell_draw(seeds[17], (FEATURE_DIM, FEATURE_DIM), FEATURE_DIM ** -0.5, 0.21875)
    feedforward_lookup_matrix = bell_draw(seeds[18], (FEATURE_DIM, FF), FEATURE_DIM ** -0.5, 0.21875, ((1, 4),))
    feedforward_content_matrix = bell_draw(seeds[19], (FF, FEATURE_DIM), FF ** -0.5, 0.109375, ((0, 4),))
    upstream_adjoint = bell_draw(seeds[20], (TOKENS, FEATURE_DIM), 1.0, 6.0, ((0, 32),))
    return {"entering_activations": entering_activations, "sample_sizes": sample_sizes, "initial_layernorm_scale": initial_layernorm_scale, "initial_layernorm_offset": initial_layernorm_offset, "temporal_lookup_fraction": temporal_lookup_fraction, "temporal_content_fraction": temporal_content_fraction, "temporal_gating_fraction": temporal_gating_fraction, "fading_speed_logarithm": fading_speed_logarithm, "present_reward": present_reward, "temporal_gating_matrix": temporal_gating_matrix, "temporal_lookup_matrix": temporal_lookup_matrix, "temporal_content_matrix": temporal_content_matrix, "temporal_emission_matrix": temporal_emission_matrix, "latter_layernorm_scale": latter_layernorm_scale, "latter_layernorm_offset": latter_layernorm_offset, "feedforward_lookup_fraction": feedforward_lookup_fraction, "feedforward_gating_fraction": feedforward_gating_fraction, "feedforward_gating_matrix": feedforward_gating_matrix, "feedforward_lookup_matrix": feedforward_lookup_matrix, "feedforward_content_matrix": feedforward_content_matrix, "upstream_adjoint": upstream_adjoint}


@jax.custom_vjp
def reduced_accuracy(v):
    return lax.optimization_barrier(v.astype(jnp.bfloat16)).astype(jnp.float32)

@jax.custom_vjp
def low_back(v):
    return v

def low_keep(v):
    return (reduced_accuracy(v), None)

def low_pass(kept, grad):
    return (grad,)

def back_keep(v):
    return (v, None)

def back_low(kept, grad):
    return (reduced_accuracy(grad),)
reduced_accuracy.defvjp(low_keep, low_pass)
low_back.defvjp(back_keep, back_low)
EPSILON = 1e-05
HIGHEST = lax.Precision.HIGHEST

def product(left, right):
    return jnp.dot(left, right, precision=HIGHEST, preferred_element_type=jnp.float32)

def norm_rows(values, gain_vec, offset):
    row_mean = lax.optimization_barrier(jnp.mean(values, axis=-1, keepdims=True))
    centered = values - row_mean
    variance = lax.optimization_barrier(jnp.mean(centered * centered, axis=-1, keepdims=True))
    return centered * lax.rsqrt(variance + EPSILON) * gain_vec + offset

def shift_rows(values, resets):
    earlier = jnp.concatenate([jnp.zeros_like(values[:1]), values[:-1]], axis=0)
    return earlier * (1.0 - resets)[:, None]

def layout(lengths_row, row_count, segment_size):
    lengths_row = lengths_row.astype(jnp.int32)
    seq_ends = jnp.cumsum(lengths_row).astype(jnp.int32)
    begins = seq_ends - lengths_row
    block_marks = jnp.arange(row_count // segment_size, dtype=jnp.int32) * segment_size
    matches = (begins[None, :] == block_marks[:, None]) & (lengths_row[None, :] > 0)
    segment_beginnings = jnp.any(matches, axis=1).astype(jnp.float32)
    places = jnp.arange(row_count, dtype=jnp.int32)
    at_heads = (places % segment_size == 0).astype(jnp.float32)
    resets = jnp.repeat(segment_beginnings, segment_size) * at_heads
    valid_rows = (places < seq_ends[-1]).astype(jnp.float32)
    return (resets, segment_beginnings, valid_rows)

def exponentiated_lookups(mapped_lookup_vectors, mapped_content_vectors, fading_speed_logarithm, present_reward, segment_beginnings, segment_size):
    decay_rate = jnp.exp(fading_speed_logarithm)
    offsets = jnp.arange(segment_size, dtype=jnp.int32).astype(jnp.float32)[:, None]
    fading_multiplier = jnp.exp(-offsets * decay_rate)
    rising = jnp.exp((offsets + 1.0) * decay_rate)
    through = jnp.exp(-segment_size * decay_rate)
    number_blocks = mapped_lookup_vectors.shape[0] // segment_size
    channels = mapped_lookup_vectors.shape[1]

    def one_block(carry_state, block_items):
        segment_lookup_vectors, segment_content_vectors, fresh_flag = block_items
        dividend_carry = carry_state[0] * (1.0 - fresh_flag)
        divisor_carry = carry_state[1] * (1.0 - fresh_flag)
        lifted = rising * jnp.exp(segment_lookup_vectors)
        carried = lifted * segment_content_vectors
        zero_row = jnp.zeros_like(lifted[:1])
        dividend_earlier = jnp.concatenate([zero_row, jnp.cumsum(carried, axis=0)[:-1]], axis=0)
        divisor_earlier = jnp.concatenate([zero_row, jnp.cumsum(lifted, axis=0)[:-1]], axis=0)
        reward_multiples = jnp.exp(present_reward + segment_lookup_vectors)
        accumulated_dividend = fading_multiplier * (dividend_carry + dividend_earlier) + reward_multiples * segment_content_vectors
        accumulated_divisor = fading_multiplier * (divisor_carry + divisor_earlier) + reward_multiples
        following = (through * (dividend_carry + lax.optimization_barrier(jnp.sum(carried, axis=0))), through * (divisor_carry + lax.optimization_barrier(jnp.sum(lifted, axis=0))))
        return (following, accumulated_dividend / accumulated_divisor)
    initial = (jnp.zeros((channels,), jnp.float32), jnp.zeros((channels,), jnp.float32))
    block_data = (mapped_lookup_vectors.reshape(number_blocks, segment_size, channels), mapped_content_vectors.reshape(number_blocks, segment_size, channels), segment_beginnings)
    last_state, outputs = lax.scan(jax.checkpoint(one_block), initial, block_data)
    return outputs.reshape(number_blocks * segment_size, channels)

def layer(entering_activations, softmax_scores, resets, segment_beginnings, valid_rows):
    initial_layernorm_scale, initial_layernorm_offset, temporal_lookup_fraction, temporal_content_fraction, temporal_gating_fraction, fading_speed_logarithm, present_reward, temporal_gating_matrix, temporal_lookup_matrix, temporal_content_matrix, temporal_emission_matrix, latter_layernorm_scale, latter_layernorm_offset, feedforward_lookup_fraction, feedforward_gating_fraction, feedforward_gating_matrix, feedforward_lookup_matrix, feedforward_content_matrix = softmax_scores
    normed = norm_rows(entering_activations, initial_layernorm_scale, initial_layernorm_offset)
    shifted = shift_rows(normed, resets)
    keyed = reduced_accuracy(normed * temporal_lookup_fraction + shifted * (1.0 - temporal_lookup_fraction))
    valued = reduced_accuracy(normed * temporal_content_fraction + shifted * (1.0 - temporal_content_fraction))
    recepted = reduced_accuracy(normed * temporal_gating_fraction + shifted * (1.0 - temporal_gating_fraction))
    gating_preactivation = low_back(product(recepted, temporal_gating_matrix))
    mapped_lookup_vectors = low_back(product(keyed, temporal_lookup_matrix))
    mapped_content_vectors = low_back(product(valued, temporal_content_matrix))
    interpolated_tokens = reduced_accuracy(jax.nn.sigmoid(gating_preactivation) * exponentiated_lookups(mapped_lookup_vectors, mapped_content_vectors, fading_speed_logarithm, present_reward, segment_beginnings, COUNT_RANGE))
    after = entering_activations + low_back(product(interpolated_tokens, temporal_emission_matrix))
    normed_two = norm_rows(after, latter_layernorm_scale, latter_layernorm_offset)
    shifted_two = shift_rows(normed_two, resets)
    chan_keyed = reduced_accuracy(normed_two * feedforward_lookup_fraction + shifted_two * (1.0 - feedforward_lookup_fraction))
    chan_recepted = reduced_accuracy(normed_two * feedforward_gating_fraction + shifted_two * (1.0 - feedforward_gating_fraction))
    hidden_pre = low_back(product(chan_keyed, feedforward_lookup_matrix))
    hidden = reduced_accuracy(jnp.square(jnp.maximum(hidden_pre, 0.0)))
    channel_out = low_back(product(hidden, feedforward_content_matrix))
    gate_rows = jax.nn.sigmoid(low_back(product(chan_recepted, feedforward_gating_matrix)))
    return (after + gate_rows * channel_out) * valid_rows[:, None]

def reference(entering_activations, sample_sizes, initial_layernorm_scale, initial_layernorm_offset, temporal_lookup_fraction, temporal_content_fraction, temporal_gating_fraction, fading_speed_logarithm, present_reward, temporal_gating_matrix, temporal_lookup_matrix, temporal_content_matrix, temporal_emission_matrix, latter_layernorm_scale, latter_layernorm_offset, feedforward_lookup_fraction, feedforward_gating_fraction, feedforward_gating_matrix, feedforward_lookup_matrix, feedforward_content_matrix, upstream_adjoint):
    softmax_scores = tuple((segment_membership.astype(jnp.float32) for segment_membership in (initial_layernorm_scale, initial_layernorm_offset, temporal_lookup_fraction, temporal_content_fraction, temporal_gating_fraction, fading_speed_logarithm, present_reward, temporal_gating_matrix, temporal_lookup_matrix, temporal_content_matrix, temporal_emission_matrix, latter_layernorm_scale, latter_layernorm_offset, feedforward_lookup_fraction, feedforward_gating_fraction, feedforward_gating_matrix, feedforward_lookup_matrix, feedforward_content_matrix)))
    row_count = TOK_DEV
    input_blocks = entering_activations.astype(jnp.float32).reshape(GROUPS, row_count, FEATURE_DIM)
    cot_blocks = upstream_adjoint.astype(jnp.float32).reshape(GROUPS, row_count, FEATURE_DIM)

    def one_group(totals, group_items):
        group_inputs, group_cot, group_lengths = group_items
        resets, segment_beginnings, valid_rows = layout(group_lengths, row_count, COUNT_RANGE)

        def forward(values, params):
            return layer(values, params, resets, segment_beginnings, valid_rows)
        result, pullback = jax.vjp(forward, group_inputs, softmax_scores)
        grad_values, grad_params = pullback(group_cot)
        totals = jax.tree.map(jnp.add, totals, grad_params)
        return (totals, (result.astype(jnp.bfloat16), grad_values))
    zero_grads = tuple((jnp.zeros_like(segment_membership) for segment_membership in softmax_scores))
    totals, (results, grad_blocks) = lax.scan(one_group, zero_grads, (input_blocks, cot_blocks, sample_sizes))
    out = results.reshape(GROUPS * row_count, FEATURE_DIM)
    grad_inputs = grad_blocks.reshape(GROUPS * row_count, FEATURE_DIM)
    return (out, grad_inputs, totals[0], totals[1], totals[2], totals[3], totals[4], totals[5], totals[6], totals[7], totals[8], totals[9], totals[10], totals[11], totals[12], totals[13], totals[14], totals[15], totals[16], totals[17])
```

```python
import functools

import jax
import jax.numpy as jnp
from jax import lax
from jax.experimental import pallas as pl
from jax.experimental.pallas import tpu as pltpu
from jax.sharding import PartitionSpec as P

F32 = jnp.float32
BF16 = jnp.bfloat16
EPSILON = 1e-05
SEG = 64
D = 768
T = 1024
HALF = 512
HALF_D = D // 2
BLK = 128
SUB = 16
NSEG = T // SEG


def nn(left, right):
    return jnp.dot(left, right, preferred_element_type=F32)


def nt(left, right):
    return lax.dot_general(left, right, (((1,), (1,)), ((), ())), preferred_element_type=F32)


def tn(left, right):
    return lax.dot_general(left, right, (((0,), (0,)), ((), ())), preferred_element_type=F32)


def normalize(v):
    c = v - jnp.mean(v, axis=-1, keepdims=True)
    r = lax.rsqrt(jnp.mean(c * c, axis=-1, keepdims=True) + EPSILON)
    return c * r, r


def roll_down(v, first):
    row = lax.broadcasted_iota(jnp.int32, v.shape, 0)
    return jnp.where(row == 0, first, pltpu.roll(v, 1, 0))


def two_parts(v):
    hi = v.astype(BF16)
    return hi, (v - hi.astype(F32)).astype(BF16)


def triangle(upper):
    row = lax.broadcasted_iota(jnp.int32, (SEG, 2 * SEG), 0)
    col = lax.broadcasted_iota(jnp.int32, (SEG, 2 * SEG), 1)
    col = jnp.where(col >= SEG, col - SEG, col)
    keep = (col > row) if upper else (col < row)
    return jnp.where(keep, 1.0, 0.0).astype(BF16)


def running(tri, first, second):
    both = jnp.concatenate([first, second], axis=1)
    hi, lo = two_parts(both)
    return nn(tri, jnp.concatenate([hi, lo], axis=0)), both


def decay_tables(dec, rise, fade):
    rate = jnp.exp(dec)
    offs = lax.broadcasted_iota(jnp.int32, (SEG, D), 0).astype(F32)
    rise[...] = jnp.exp((offs + 1.0) * rate)
    fade[...] = jnp.exp(-offs * rate)
    return jnp.exp(-float(SEG) * rate)


def front_kernel(
    half_ref, len_ref, x_ref, adj_ref, g1, b1, fk, fv, fr, dec, rew, g2, b2, ck, cr,
    wr, wk, wv, wo, wg, wfk, wfv,
    flags, pq, grads, n1_o, dh1_o, a_o, v_o, sr_o, w_o, rd_o, sn_o, sd_o, after_o, gate_o, n2_o, dh2_o,
    r1_o, r2_o, keyed_o, valued_o, recepted_o, mixed_o, chrec_o,
    rise, fade, through, expu, nc, dc, p1, p2, kb, vb, rb, hb, rs, mx, cks, hid, gch, gpr,
    b_key, b_val, b_rec, b_crec, t_n1, t_dh1, t_r1,
):
    i = pl.program_id(0)
    own = (i // 4) == half_ref[0]

    @pl.when(i == 0)
    def _():
        for b in range(NSEG):
            flags[0, b] = 0.0
        begin = jnp.int32(0)
        for j in range(NSEG):
            size = len_ref[0, j]
            at = lax.shift_right_logical(begin, 6)

            @pl.when(size > 0)
            def _():
                flags[0, at] = 1.0

            begin = begin + size
        for b in range(NSEG):
            flags[1, b] = jnp.where(b * SEG < begin, 1.0, 0.0)
        through[...] = decay_tables(dec[...], rise, fade)
        expu[...] = jnp.exp(rew[...])
        nc[...] = jnp.zeros_like(nc)
        dc[...] = jnp.zeros_like(dc)
        p1[...] = jnp.zeros_like(p1)
        p2[...] = jnp.zeros_like(p2)

    fresh = [flags[0, i * (BLK // SEG) + s] for s in range(BLK // SEG)]
    live = [flags[1, i * (BLK // SEG) + s] for s in range(BLK // SEG)]

    for s in range(BLK // SUB):
        at = pl.ds(s * SUB, SUB)
        n1, r1 = normalize(x_ref[at, :].astype(F32))
        h1 = n1 * g1[...] + b1[...]
        before = p1[...]
        if (s * SUB) % SEG == 0:
            before = before * (1.0 - fresh[s * SUB // SEG])
        sh = roll_down(h1, before)
        p1[...] = h1[SUB - 1 :, :]
        dh1 = h1 - sh
        b_key[at, :] = (sh + dh1 * fk[...]).astype(BF16)
        b_val[at, :] = (sh + dh1 * fv[...]).astype(BF16)
        b_rec[at, :] = (sh + dh1 * fr[...]).astype(BF16)
        t_n1[at, :] = n1
        t_dh1[at, :] = dh1
        t_r1[at, :] = jnp.broadcast_to(r1, (SUB, 128))

    kb[...] = nn(b_key[...], wk[...])
    vb[...] = nn(b_val[...], wv[...])
    rb[...] = nn(b_rec[...], wr[...])

    tri = triangle(False)
    for s in range(BLK // SEG):
        at = pl.ds(s * SEG, SEG)
        keep = 1.0 - fresh[s]
        for c in range(D // 128):
            cols = pl.ds(c * 128, 128)
            a = jnp.exp(kb[at, cols])
            v = vb[at, cols]
            lift = rise[:, cols] * a
            cum, both = running(tri, lift * v, lift)
            ncar = nc[:, cols] * keep
            dcar = dc[:, cols] * keep
            sn = fade[:, cols] * (ncar + cum[:, :128])
            sd = fade[:, cols] * (dcar + cum[:, 128:])
            th = through[:, cols]
            nc[:, cols] = th * (ncar + (cum[SEG - 1 :, :128] + both[SEG - 1 :, :128]))
            dc[:, cols] = th * (dcar + (cum[SEG - 1 :, 128:] + both[SEG - 1 :, 128:]))
            e = expu[:, cols] * a
            rd = 1.0 / (sd + e)
            w = (sn + e * v) * rd
            sr = jax.nn.sigmoid(rb[at, cols])
            mx[at, cols] = (sr * w).astype(BF16)

            @pl.when(own)
            def _():
                a_o[at, cols] = a
                v_o[at, cols] = v
                sr_o[at, cols] = sr
                w_o[at, cols] = w
                rd_o[at, cols] = rd
                sn_o[at, cols] = sn
                sd_o[at, cols] = sd

    hb[...] = nn(mx[...], wo[...])

    rows0 = pl.multiple_of(i * BLK, BLK)
    for s in range(BLK // SUB):
        at = pl.ds(s * SUB, SUB)
        after = x_ref[at, :].astype(F32) + hb[at, :]
        n2, r2 = normalize(after)
        h2 = n2 * g2[...] + b2[...]
        before = p2[...]
        if (s * SUB) % SEG == 0:
            before = before * (1.0 - fresh[s * SUB // SEG])
        sh = roll_down(h2, before)
        p2[...] = h2[SUB - 1 :, :]
        dh2 = h2 - sh
        cks[pl.ds(rows0 + s * SUB, SUB), :] = (sh + dh2 * ck[...]).astype(BF16)
        b_crec[at, :] = (sh + dh2 * cr[...]).astype(BF16)

        @pl.when(own)
        def _():
            after_o[at, :] = after
            n2_o[at, :] = n2
            dh2_o[at, :] = dh2
            r2_o[at, :] = jnp.broadcast_to(r2, (SUB, 128))

    rows = pl.ds(rows0, BLK)
    hb[...] = nn(cks[rows, :], wfk[...])
    rs[...] = nn(b_crec[...], wg[...])
    for s in range(BLK // SUB):
        at = pl.ds(s * SUB, SUB)
        hp = jnp.maximum(hb[at, :], 0.0)
        hid[pl.ds(rows0 + s * SUB, SUB), :] = (hp * hp).astype(BF16)
        gate = jax.nn.sigmoid(rs[at, :])
        rs[at, :] = gate
        go = adj_ref[at, :].astype(F32) * live[s * SUB // SEG]
        gch[pl.ds(rows0 + s * SUB, SUB), :] = (go * gate).astype(BF16)
    pq[:, :D] = nn(hid[rows, :], wfv[...])
    kb[...] = nt(gch[rows, :], wfv[...])
    for s in range(BLK // SUB):
        at = pl.ds(s * SUB, SUB)
        gpr[pl.ds(rows0 + s * SUB, SUB), :] = (2.0 * jnp.maximum(hb[at, :], 0.0) * kb[at, :]).astype(BF16)
    pq[:, D:] = nt(gpr[rows, :], wfk[...])

    @pl.when(own)
    def _():
        gate_o[...] = rs[...]
        n1_o[...] = t_n1[...]
        dh1_o[...] = t_dh1[...]
        r1_o[...] = t_r1[...]
        keyed_o[...] = b_key[...]
        valued_o[...] = b_val[...]
        recepted_o[...] = b_rec[...]
        mixed_o[...] = mx[...]
        chrec_o[...] = b_crec[...]

    @pl.when(i == T // BLK - 1)
    def _():
        for c in range(D // 256):
            cols = pl.ds(c * 256, 256)
            grads[:D, cols] = tn(cks[...], gpr[:, cols])
            grads[D:, cols] = tn(hid[...], gch[:, cols])


def front(half, sizes, x, adj, vecs, mats):
    steps = T // BLK
    blk = lambda w: pl.BlockSpec((BLK, w), lambda i, h: (i, 0))
    own = lambda w: pl.BlockSpec((BLK, w), lambda i, h: (jnp.clip(i - 4 * h[0], 0, 3), 0))
    vec = pl.BlockSpec((1, D), lambda i, h: (0, 0))
    mat = pl.BlockSpec((D, D), lambda i, h: (0, 0), pipeline_mode=pl.Buffered(1))
    sds = jax.ShapeDtypeStruct
    vm = pltpu.VMEM
    return pl.pallas_call(
        front_kernel,
        grid_spec=pltpu.PrefetchScalarGridSpec(
            num_scalar_prefetch=1,
            grid=(steps,),
            in_specs=[pl.BlockSpec(memory_space=pltpu.SMEM), blk(D), blk(D)] + [vec] * 11 + [mat] * 7,
            out_specs=[pl.BlockSpec(memory_space=pltpu.SMEM), blk(2 * D),
                       pl.BlockSpec((2 * D, D), lambda i, h: (0, 0), pipeline_mode=pl.Buffered(1))]
            + [own(D)] * 13 + [own(128)] * 2 + [own(D)] * 5,
            scratch_shapes=[vm((SEG, D), F32)] * 2 + [vm((1, D), F32)] * 6 + [vm((BLK, D), F32)] * 5
            + [vm((BLK, D), BF16)] + [vm((T, D), BF16)] * 4
            + [vm((BLK, D), BF16)] * 4 + [vm((BLK, D), F32)] * 2 + [vm((BLK, 128), F32)],
        ),
        out_shape=[sds((2, NSEG), F32), sds((T, 2 * D), F32), sds((2 * D, D), F32)]
        + [sds((HALF, D), F32)] * 13 + [sds((HALF, 128), F32)] * 2 + [sds((HALF, D), BF16)] * 5,
        compiler_params=pltpu.CompilerParams(dimension_semantics=("arbitrary",), vmem_limit_bytes=60 * 2**20),
        cost_estimate=pl.CostEstimate(flops=11 * 2 * T * D * D, bytes_accessed=60 * 2**20, transcendentals=4 * T * D),
        name="front",
    )(half, sizes, x, adj, *vecs, *mats)


MESH = pl.DeviceIdType.MESH
COPIES = 160
FF_ROWS = 2 * D
R_ROWS = 2048
VEC_ROW = 5 * HALF_D
NVEC = 11


def rows(start, size):
    return pl.ds(pl.multiple_of(start, 8), size)


def each(count, step, body, reverse=False):
    def run(k, carry):
        body((count - 1 - k) * step if reverse else k * step)
        return carry

    lax.fori_loop(0, count, run, 0)


class Links:
    def __init__(self, sends, recvs):
        self.sends, self.recvs, self.used, self.open = sends, recvs, 0, []

    def send(self, src, dst, device):
        k = self.used
        self.used += 1
        copy = pltpu.make_async_remote_copy(
            src_ref=src, dst_ref=dst, send_sem=self.sends.at[k], recv_sem=self.recvs.at[k],
            device_id=device, device_id_type=MESH,
        )
        copy.start()
        self.open.append(copy)
        return copy

    def sent(self, copy):
        self.open = [kept for kept in self.open if kept is not copy]
        copy.wait_send()

    def finish(self):
        for copy in self.open:
            copy.wait_send()


def add_into(dst, dst_at, terms, size, step=16):
    if size % step:
        step = 8

    def body(r):
        total = dst[rows(dst_at + r, step), :]
        for ref, start in terms:
            total = total + ref[rows(start + r, step), :]
        dst[rows(dst_at + r, step), :] = total

    each(size // step, step, body)


def ring_reduce(links, data, base, size, place, up, down, land, land_at):
    s = size // 4
    q = s // 2
    mine = base + place * s
    nxt = base + lax.rem(place + 1, 4) * s
    opp = base + lax.rem(place + 2, 4) * s
    prv = base + lax.rem(place + 3, 4) * s
    spot = [land.at[pl.ds(land_at + k * q, q), :] for k in range(6)]
    fwd_a = links.send(data.at[rows(opp, q), :], spot[0], up)
    fwd_b = links.send(data.at[rows(opp + q, q), :], spot[1], down)
    dir_b = links.send(data.at[rows(nxt + q, q), :], spot[2], up)
    dir_a = links.send(data.at[rows(prv, q), :], spot[3], down)
    yield
    for copy in (fwd_a, fwd_b, dir_b, dir_a):
        links.sent(copy)
    fwd_a.wait_recv()
    add_into(land, land_at, [(data, nxt)], q)
    cmb_a = links.send(spot[0], spot[4], up)
    fwd_b.wait_recv()
    add_into(land, land_at + q, [(data, prv + q)], q)
    cmb_b = links.send(spot[1], spot[5], down)
    yield
    dir_a.wait_recv()
    dir_b.wait_recv()
    cmb_a.wait_recv()
    cmb_b.wait_recv()
    add_into(data, mine, [(land, land_at + 3 * q), (land, land_at + 4 * q)], q)
    add_into(data, mine + q, [(land, land_at + 2 * q), (land, land_at + 5 * q)], q)


def ring_gather(links, data, base, size, place, up, down):
    s = size // 4
    q = s // 2
    mine = base + place * s
    nxt = base + lax.rem(place + 1, 4) * s
    prv = base + lax.rem(place + 3, 4) * s
    own = data.at[rows(mine, s), :]
    to_up = links.send(own, own, up)
    to_down = links.send(own, own, down)
    yield
    to_up.wait_recv()
    half_a = data.at[rows(prv, q), :]
    on_a = links.send(half_a, half_a, up)
    to_down.wait_recv()
    half_b = data.at[rows(nxt + q, q), :]
    on_b = links.send(half_b, half_b, down)
    yield
    on_a.wait_recv()
    on_b.wait_recv()


def all_reduce(links, data, base, size, axes, land, land_at):
    spans = []
    for axis in axes:
        spans.append((base, size))
        if axis[0] == "ring":
            yield from ring_reduce(links, data, base, size, axis[1], axis[2], axis[3], land, land_at)
            land_at += 6 * (size // 8)
            size = size // 4
        else:
            whole = data.at[rows(base, size), :]
            copy = links.send(whole, land.at[pl.ds(land_at, size), :], axis[2])
            yield
            links.sent(copy)
            copy.wait_recv()
            add_into(data, base, [(land, land_at)], size, 8)
            land_at += size
            continue
        base = base + axis[1] * size
    for axis, (lo, span) in zip(reversed(axes), reversed(spans)):
        if axis[0] == "ring":
            yield from ring_gather(links, data, lo, span, axis[1], axis[2], axis[3])


def step(*jobs):
    for job in jobs:
        next(job, None)


def drain(*jobs):
    live = list(jobs)
    while live:
        live = [job for job in live if next(job, job) is not job]


def back_kernel(
    flags, pq, grads, n1_h, dh1_h, a_h, v_h, sr_h, w_h, rd_h, sn_h, sd_h, after_h, gate_h, n2_h, dh2_h,
    r1_h, r2_h, keyed_h, valued_h, recepted_h, mixed_h, chrec_h, adj_h,
    g1, fk, fv, fr, dec, rew, g2, ck, cr, wr_h, wk_h, wv_h, wo_h, wg_h,
    out_o, gi_o, vec_o, recw_o, keyw_o, valw_o, outw_o, chrec_o, chkey_o, chval_o,
    slots, front4, r1, r2, keyed, valued, recepted, mixed, chrec, adj, wr, wk, wv, wo, wg,
    fin, part, arecv, crecv, brecv, gg, gb, gk, gv, gp, t0, t1, t2, other, og,
    ff, ffland, rland, urow, urow2, gsend, grecv, acc, rise, fade, through, expu, sums, gc,
    sends, recvs, local, fill,
):
    dp = lax.axis_index("dp")
    tensor = lax.axis_index("tensor")
    x, z, yl = dp // 8, lax.rem(dp // 2, 4), lax.rem(dp, 2)
    h, c = tensor // 2, lax.rem(tensor, 2)
    y = 2 * h + yl

    def chip(cx, cz, cy, core):
        cx, cz, cy = lax.rem(cx + 4, 4), lax.rem(cz + 4, 4), lax.rem(cy + 4, 4)
        return {"dp": (cx * 4 + cz) * 2 + lax.rem(cy, 2), "tensor": (cy // 2) * 2 + core}

    xp, xm = chip(x + 1, z, y, c), chip(x - 1, z, y, c)
    zp, zm = chip(x, z + 1, y, c), chip(x, z - 1, y, c)
    yp, ym = chip(x, z, y + 1, c), chip(x, z, y - 1, c)
    opp = {"dp": dp, "tensor": (1 - h) * 2 + c}
    sib = {"dp": dp, "tensor": h * 2 + (1 - c)}
    pair = {"dp": dp + 1 - 2 * yl, "tensor": tensor}
    own_at, other_at = h * HALF, (1 - h) * HALF

    fills = []

    def bring(src, dst):
        copy = pltpu.make_async_copy(src, dst, fill.at[len(fills)])
        copy.start()
        fills.append(copy)
        return copy

    part_in = [bring(pq.at[rows(other_at + 128 * j + 64 * c, 64), :], part.at[pl.ds(64 * j, 64), :]) for j in range(4)]
    ff_in = bring(grads, ff)
    fin_in = [
        bring(pq.at[rows(own_at + 128 * j + 64 * c, 64), :], fin.at[rows(128 * j + 64 * c, 64), :]) for j in range(4)
    ]
    AFTER, GATE, N2, DH2 = (HALF * k for k in range(4))
    A, V, SR, W, RD, SN, SD = (HALF * k for k in range(7))
    first_in = [bring(s, front4.at[pl.ds(HALF * k, HALF), :]) for k, s in enumerate((after_h, gate_h, n2_h, dh2_h))]
    first_in += [bring(adj_h.at[rows(own_at, HALF), :], adj), bring(wg_h, wg), bring(r2_h, r2), bring(wo_h, wo)]
    second_in = [
        bring(s, slots.at[pl.ds(HALF * k, HALF), :])
        for k, s in enumerate((a_h, v_h, sr_h, w_h, rd_h, sn_h, sd_h))
    ]
    third_in = [
        bring(s, d)
        for s, d in (
            (mixed_h, mixed), (chrec_h, chrec), (keyed_h, keyed), (valued_h, valued), (recepted_h, recepted),
            (wr_h, wr), (wk_h, wk), (wv_h, wv), (r1_h, r1),
        )
    ]

    barrier = pltpu.get_barrier_semaphore()
    partners = (xp, xm, zp, zm, yp, ym, opp, sib)
    for device in partners:
        pl.semaphore_signal(barrier, inc=1, device_id=device, device_id_type=MESH)
    pl.semaphore_wait(barrier, len(partners))

    links = Links(sends, recvs)
    a_in = [
        links.send(pq.at[rows(other_at + 128 * j + 64 * (1 - c), 64), :], arecv.at[pl.ds(64 * j, 64), :], sib)
        for j in range(4)
    ]
    ff_in.wait()
    ax = ("ring", x, xp, xm)
    az = ("ring", z, zp, zm)
    ay = ("ring", y, yp, ym)
    ap = ("pair", yl, pair)
    ff_a = all_reduce(links, ff, 0, D, (ax, az, ap), ffland, 0)
    ff_b = all_reduce(links, ff, D, D, (az, ax, ap), ffland, FF_ROWS // 2)
    step(ff_a, ff_b)
    c_in = [
        links.send(pq.at[rows(own_at + 128 * j + 64 * (1 - c), 64), :], crecv.at[pl.ds(64 * j, 64), :], sib)
        for j in range(4)
    ]
    b_in = []
    for j in range(4):
        part_in[j].wait()
        a_in[j].wait_recv()
        add_into(part, 64 * j, [(arecv, 64 * j)], 64, 8)
        b_in.append(links.send(part.at[pl.ds(64 * j, 64), :], brecv.at[pl.ds(64 * j, 64), :], opp))

    through[...] = decay_tables(dec[...], rise, fade)
    expu[...] = jnp.exp(rew[...])
    acc[...] = jnp.zeros_like(acc)
    seg0 = h * (HALF // SEG)
    not_last = (1 - h).astype(F32)

    def fold(v):
        return jnp.sum(v.reshape(-1, 8, D), axis=0)

    def tally(k, v):
        acc[pl.ds(8 * k, 8), :] += fold(v)

    MIXK, MIXV, MIXR, GAIN1, BIAS1, LOGD, REW, GAIN2, BIAS2, CMIXK, CMIXR = 2, 3, 4, 0, 1, 5, 6, 7, 8, 9, 10

    step(ff_a, ff_b)
    for copy in first_in:
        copy.wait()

    def take(j):
        fin_in[j].wait()
        c_in[j].wait_recv()
        b_in[j].wait_recv()
        add_into(fin, 128 * j + 64 * c, [(crecv, 64 * j), (brecv, 64 * j)], 64, 8)
        mine = fin.at[rows(128 * j + 64 * c, 64), :]
        return links.send(mine, mine, sib)

    def gate_part(j):
        lo = 128 * j
        for seg in range(2):
            live = flags[1, seg0 + 2 * j + seg]

            def body(r, seg=seg, live=live):
                at = rows(lo + SEG * seg + r, SUB)
                gate = front4[rows(GATE + lo + SEG * seg + r, SUB), :]
                co = fin[at, :D]
                res = live * (front4[rows(AFTER + lo + SEG * seg + r, SUB), :] + gate * co)
                front4[rows(AFTER + lo + SEG * seg + r, SUB), :] = res.astype(BF16).astype(F32)
                go = adj[at, :].astype(F32) * live
                gg[at, :] = (go * co * gate * (1.0 - gate)).astype(BF16)

            each(SEG // SUB, SUB, body)
        t0[...] = nt(gg[pl.ds(lo, 128), :], wg[...])

        def body2(r):
            at = rows(lo + r, SUB)
            qk = fin[at, D:]
            qr = t0[rows(r, SUB), :]
            dh2 = front4[rows(DH2 + lo + r, SUB), :]
            tally(CMIXK, qk * dh2)
            tally(CMIXR, qr * dh2)
            base = qk * ck[...] + qr * cr[...]
            fin[at, :D] = base
            fin[at, D:] = (qk + qr) - base

        each(128 // SUB, SUB, body2)

    e_in = []
    out_in = None
    for j in range(4):
        e_in.append(take(j))
        if j == 1:
            step(ff_a, ff_b)
        e_in[j].wait_recv()
        links.sent(e_in[j])
        gate_part(j)
        if j == 0:
            gsend[...] = fin[:8, D:]
            u_in = links.send(gsend, urow, opp)
        step(ff_a, ff_b)
    half_at = AFTER + 256 * c
    out_in = links.send(front4.at[rows(half_at, 256), :], other.at[rows(256 * c, 256), :], opp)
    u_in.wait_recv()
    step(ff_a, ff_b)

    def lifted(ref_row, nxt, u):
        row = lax.broadcasted_iota(jnp.int32, u.shape, 0)
        return jnp.where(row == u.shape[0] - 1, nxt, pltpu.roll(u, u.shape[0] - 1, 0))

    def norm_back(e, n, r, gain):
        f = e * gain
        return r * (f - jnp.mean(f, axis=-1, keepdims=True) - n * jnp.mean(f * n, axis=-1, keepdims=True))

    def keep_next(seg):
        return 1.0 - flags[0, jnp.minimum(seg0 + seg + 1, NSEG - 1)]

    def walk_rows(sub_body, after_chunk=None):
        for j in reversed(range(4)):
            for seg in (1, 0):
                s = 2 * j + seg
                live = flags[1, seg0 + s]
                for k in reversed(range(SEG // SUB)):
                    lo = SEG * s + SUB * k
                    if lo + SUB == HALF:
                        nxt = urow_now[0:1, :] * (not_last * keep_next(s))
                    else:
                        nxt = fin[lo + SUB : lo + SUB + 1, D:]
                        if k == SEG // SUB - 1:
                            nxt = nxt * keep_next(s)
                    sub_body(lo, live, nxt)
            if after_chunk is not None:
                after_chunk(j)

    for copy in second_in:
        copy.wait()

    def after_rows(lo, live, nxt):
        at = pl.ds(lo, SUB)
        e = fin[at, :D] + lifted(None, nxt, fin[at, D:])
        n = front4[pl.ds(N2 + lo, SUB), :]
        tally(GAIN2, e * n)
        tally(BIAS2, e)
        go = adj[at, :].astype(F32) * live
        ga = go + norm_back(e, n, r2[at, 0:1], g2[...])
        front4[pl.ds(N2 + lo, SUB), :] = ga
        gb[at, :] = ga.astype(BF16)

    def mixed_chunk(j):
        t0[...] = nt(gb[pl.ds(128 * j, 128), :], wo[...])

        def body(r):
            at = 128 * j + r
            gm = t0[rows(r, SUB), :]
            sr = slots[rows(SR + at, SUB), :]
            w = slots[rows(W + at, SUB), :]
            gw = gm * sr
            q = gw * slots[rows(RD + at, SUB), :]
            slots[rows(RD + at, SUB), :] = q
            gp[rows(at, SUB), :] = (gw * w * (1.0 - sr)).astype(BF16)
            fq = fade[rows(lax.rem(r, SEG), SUB), :] * q
            total[0:8, :] = total[0:8, :] + fold(fq)
            total[8:16, :] = total[8:16, :] + fold(fq * w)

        for seg in (1, 0):
            total = sums.at[pl.ds(16 * (2 * j + seg), 16), :]
            total[...] = jnp.zeros((16, D), F32)
            each(SEG // SUB, SUB, lambda r, seg=seg: body(r + SEG * seg))

    urow_now = urow
    walk_rows(after_rows, mixed_chunk)
    step(ff_a, ff_b)

    def seg_sum(s):
        q = jnp.sum(sums[pl.ds(16 * s, 8), :], axis=0, keepdims=True)
        return q, jnp.sum(sums[pl.ds(16 * s + 8, 8), :], axis=0, keepdims=True)

    first = jnp.zeros((1, D), F32)
    second = jnp.zeros((1, D), F32)
    th = through[...]
    for s in reversed(range(8)):
        q, qw = seg_sum(s)
        keep = keep_next(s) if s < 7 else 0.0
        first = q + th * (first * keep)
        second = qw + th * (second * keep)
    gsend2 = sums.at[pl.ds(0, 8), :]
    gsend2[0:1, :] = first
    gsend2[1:2, :] = second
    g_in = links.send(gsend2, grecv, opp)
    n1_in = bring(n1_h, front4.at[pl.ds(GATE, HALF), :])
    dh1_in = bring(dh1_h, front4.at[pl.ds(DH2, HALF), :])
    for copy in third_in:
        copy.wait()
    g_in.wait_recv()
    edge = not_last * keep_next(7)
    gc[0:1, :] = grecv[0:1, :] * edge
    gc[1:2, :] = grecv[1:2, :] * edge
    tri = triangle(True)

    def key_value(k, carry):
        s = 7 - k
        lo = SEG * s
        keep = 1.0 - flags[0, seg0 + s]
        for col in range(D // 128):
            cols = pl.ds(col * 128, 128)
            at = rows(lo, SEG)
            q = slots[rows(RD + lo, SEG), cols]
            w = slots[rows(W + lo, SEG), cols]
            a = slots[rows(A + lo, SEG), cols]
            v = slots[rows(V + lo, SEG), cols]
            fq = fade[:, cols] * q
            cum, both = running(tri, fq, fq * w)
            cn = through[:, cols] * gc[0:1, cols]
            cd = through[:, cols] * gc[1:2, cols]
            gn = rise[:, cols] * (cum[:, :128] + cn)
            gd = rise[:, cols] * (cum[:, 128:] + cd)
            gc[0:1, cols] = (both[0:1, :128] + cum[0:1, :128] + cn) * keep
            gc[1:2, cols] = (both[0:1, 128:] + cum[0:1, 128:] + cd) * keep
            eq = expu[:, cols] * a * q
            gvv = a * gn + eq
            gv[at, cols] = gvv.astype(BF16)
            gk[at, cols] = (v * gvv - (a * gd + eq * w)).astype(BF16)
            up = eq * (v - w)
            down = gn * slots[rows(SN + lo, SEG), cols] - gd * slots[rows(SD + lo, SEG), cols]
            acc[pl.ds(8 * REW, 8), cols] += jnp.sum(up.reshape(-1, 8, 128), axis=0)
            acc[pl.ds(8 * LOGD, 8), cols] += jnp.sum(down.reshape(-1, 8, 128), axis=0)
        return carry

    lax.fori_loop(0, 8, key_value, 0)
    step(ff_a, ff_b)

    n1_in.wait()
    dh1_in.wait()

    def front_chunk(j):
        at0 = pl.ds(128 * j, 128)
        t0[...] = nt(gk[at0, :], wk[...])
        t1[...] = nt(gv[at0, :], wv[...])
        t2[...] = nt(gp[at0, :], wr[...])

        def body(r):
            at = rows(128 * j + r, SUB)
            pk, pv, pr = (t[rows(r, SUB), :] for t in (t0, t1, t2))
            dh1 = front4[rows(DH2 + 128 * j + r, SUB), :]
            tally(MIXK, pk * dh1)
            tally(MIXV, pv * dh1)
            tally(MIXR, pr * dh1)
            base = pk * fk[...] + pv * fv[...] + pr * fr[...]
            fin[at, :D] = base
            fin[at, D:] = (pk + pv + pr) - base

        each(128 // SUB, SUB, body)

    for j in range(4):
        front_chunk(j)
        if j == 0:
            u2_in = links.send(fin.at[pl.ds(0, 8), pl.ds(D, D)], urow2, opp)
    u2_in.wait_recv()
    step(ff_a, ff_b)

    def input_rows(lo, live, nxt):
        at = pl.ds(lo, SUB)
        e = fin[at, :D] + lifted(None, nxt, fin[at, D:])
        n = front4[pl.ds(GATE + lo, SUB), :]
        tally(GAIN1, e * n)
        tally(BIAS1, e)
        front4[pl.ds(N2 + lo, SUB), :] = front4[pl.ds(N2 + lo, SUB), :] + norm_back(e, n, r1[at, 0:1], g1[...])

    urow_now = urow2
    walk_rows(input_rows)
    gi_rows = gi_o.at[rows(own_at + 256 * c, 256), :]
    gi_in = links.send(front4.at[rows(N2 + 256 * c, 256), :], gi_rows, opp)
    keeps = []

    def put(src, dst):
        copy = pltpu.make_async_copy(src, dst, local.at[len(keeps)])
        copy.start()
        keeps.append(copy)

    put(front4.at[pl.ds(N2, HALF), :], gi_o.at[rows(own_at, HALF), :])

    lanes = pl.ds(pl.multiple_of(c * HALF_D, 128), HALF_D)
    red = slots
    for k, (left, right) in enumerate(((recepted, gp), (keyed, gk), (valued, gv), (mixed, gb), (chrec, gg))):
        for col in range(D // 256):
            cols = pl.ds(256 * col, 256)
            red[pl.ds(HALF_D * k, HALF_D), cols] = tn(left[:, lanes], right[:, cols])
    red[pl.ds(VEC_ROW, R_ROWS - VEC_ROW), :] = jnp.zeros((R_ROWS - VEC_ROW, D), F32)
    scale = -jnp.exp(dec[...]) * jnp.exp(-jnp.exp(dec[...]))
    for k in range(NVEC):
        total = jnp.sum(acc[pl.ds(8 * k, 8), :], axis=0, keepdims=True)
        red[VEC_ROW + k : VEC_ROW + k + 1, :] = total * scale if k == LOGD else total

    red_a = all_reduce(links, red, 0, R_ROWS // 2, (ax, az, ay), rland, 0)
    red_b = all_reduce(links, red, R_ROWS // 2, R_ROWS // 2, (az, ax, ay), rland, R_ROWS // 2)
    step(red_a, red_b)
    step(ff_a, ff_b)
    out_in.wait_recv()
    theirs = other.at[rows(256 * c, 256), :]
    out_on = links.send(theirs, theirs, sib)
    step(red_a, red_b)
    drain(ff_a, ff_b)
    put(ff.at[pl.ds(0, D), :], chkey_o)
    put(ff.at[pl.ds(D, D), :], chval_o)
    step(red_a, red_b)
    gi_in.wait_recv()
    gi_theirs = gi_o.at[rows(other_at + 256 * c, 256), :]
    gi_on = links.send(gi_theirs, gi_theirs, sib)
    out_on.wait_recv()

    def cast_rows(r):
        og[rows(own_at + r, SUB), :] = front4[rows(AFTER + r, SUB), :].astype(BF16)
        og[rows(other_at + r, SUB), :] = other[rows(r, SUB), :].astype(BF16)

    each(HALF // SUB, SUB, cast_rows)
    put(og, out_o)
    drain(red_a, red_b)
    mats = (recw_o, keyw_o, valw_o, outw_o, chrec_o)
    spots = [m.at[rows(c * HALF_D, HALF_D), :] for m in mats]
    on = [links.send(red.at[pl.ds(HALF_D * k, HALF_D), :], spots[k], sib) for k in range(5)]
    for k in range(5):
        put(red.at[pl.ds(HALF_D * k, HALF_D), :], spots[k])
    put(red.at[pl.ds(VEC_ROW, 16), :], vec_o)
    gi_on.wait_recv()
    for copy in on:
        copy.wait_recv()
    for copy in keeps:
        copy.wait()
    links.finish()


def back(front_outs, adj, vecs, mats):
    g1, b1, fk, fv, fr, dec, rew, g2, b2, ck, cr = vecs
    flags, rest = front_outs[0], front_outs[1:]
    sds = jax.ShapeDtypeStruct
    vm = pltpu.VMEM
    anywhere = pl.BlockSpec(memory_space=pl.ANY)
    vmem = pl.BlockSpec(memory_space=pltpu.VMEM)
    half = lambda dt: vm((HALF, D), dt)
    return pl.pallas_call(
        back_kernel,
        in_specs=[pl.BlockSpec(memory_space=pltpu.SMEM)] + [anywhere] * len(rest) + [anywhere]
        + [vmem] * 9 + [anywhere] * 5,
        out_specs=[anywhere] * 10,
        out_shape=[sds((T, D), BF16), sds((T, D), F32), sds((16, D), F32)] + [sds((D, D), F32)] * 7,
        scratch_shapes=[vm((7 * HALF, D), F32), vm((4 * HALF, D), F32), vm((HALF, 128), F32), vm((HALF, 128), F32)]
        + [half(BF16)] * 6 + [vm((D, D), BF16)] * 5
        + [vm((HALF, 2 * D), F32)] + [vm((256, 2 * D), F32)] * 4
        + [half(BF16)] * 5 + [vm((128, D), F32)] * 3 + [half(F32), vm((T, D), BF16)]
        + [vm((FF_ROWS, D), F32)] * 2 + [vm((R_ROWS, D), F32)]
        + [vm((8, D), F32)] * 4 + [vm((8 * NVEC, D), F32)] + [vm((SEG, D), F32)] * 2
        + [vm((1, D), F32)] * 2 + [vm((128, D), F32), vm((8, D), F32)]
        + [pltpu.SemaphoreType.DMA((COPIES,)), pltpu.SemaphoreType.DMA((COPIES,)),
           pltpu.SemaphoreType.DMA((16,)), pltpu.SemaphoreType.DMA((48,))],
        compiler_params=pltpu.CompilerParams(collective_id=1, has_side_effects=True, vmem_limit_bytes=63 * 2**20),
        cost_estimate=pl.CostEstimate(flops=14 * T * D * D, bytes_accessed=60 * 2**20, transcendentals=0),
        name="back",
    )(flags, *rest, adj, g1, fk, fv, fr, dec, rew, g2, ck, cr, *mats[:5])


def body(
    entering_activations, sample_sizes, initial_layernorm_scale, initial_layernorm_offset, temporal_lookup_fraction,
    temporal_content_fraction, temporal_gating_fraction, fading_speed_logarithm, present_reward,
    temporal_gating_matrix, temporal_lookup_matrix, temporal_content_matrix, temporal_emission_matrix,
    latter_layernorm_scale, latter_layernorm_offset, feedforward_lookup_fraction, feedforward_gating_fraction,
    feedforward_gating_matrix, feedforward_lookup_matrix, feedforward_content_matrix, upstream_adjoint,
):
    vecs = [
        v.reshape(1, D)
        for v in (
            initial_layernorm_scale, initial_layernorm_offset, temporal_lookup_fraction, temporal_content_fraction,
            temporal_gating_fraction, fading_speed_logarithm, present_reward, latter_layernorm_scale,
            latter_layernorm_offset, feedforward_lookup_fraction, feedforward_gating_fraction,
        )
    ]
    mats = (
        temporal_gating_matrix, temporal_lookup_matrix, temporal_content_matrix, temporal_emission_matrix,
        feedforward_gating_matrix, feedforward_lookup_matrix, feedforward_content_matrix,
    )
    half = (lax.axis_index("tensor") // 2).astype(jnp.int32).reshape(1)
    fronts = front(half, sample_sizes, entering_activations, upstream_adjoint, vecs, mats)
    out, grad_inputs, vec, recw, keyw, valw, outw, chrec, chkey, chval = back(fronts, upstream_adjoint, vecs, mats)
    g = [vec[k] for k in range(NVEC)]
    return (
        out, grad_inputs, g[0], g[1], g[2], g[3], g[4], g[5], g[6], recw, keyw, valw, outw,
        g[7], g[8], g[9], g[10], chrec, chkey, chval,
    )


def solution(mesh):
    split = P("dp", None)
    in_specs = (split, split) + (P(),) * 16 + (P(None, "tensor"), P("tensor", None), split)
    out_specs = (split, split) + (P(),) * 16 + (P(None, "tensor"), P("tensor", None))
    return jax.shard_map(body, mesh=mesh, in_specs=in_specs, out_specs=out_specs, check_vma=False)
```

```python
import functools

import jax
import jax.numpy as jnp
from jax import lax
from jax.experimental import pallas as pl
from jax.experimental.pallas import tpu as pltpu
from jax.sharding import PartitionSpec as P

F32 = jnp.float32
BF16 = jnp.bfloat16
EPSILON = 1e-05
SEG = 64
D = 768
T = 1024
HALF = 512
HALF_D = D // 2
BLK = 256
SUB = 32
NSEG = T // SEG
PER = HALF // BLK


def nn(left, right):
    return jnp.dot(left, right, preferred_element_type=F32)


def nt(left, right):
    return lax.dot_general(left, right, (((1,), (1,)), ((), ())), preferred_element_type=F32)


def tn(left, right):
    return lax.dot_general(left, right, (((0,), (0,)), ((), ())), preferred_element_type=F32)


def normalize(v):
    c = v - jnp.mean(v, axis=-1, keepdims=True)
    r = lax.rsqrt(jnp.mean(c * c, axis=-1, keepdims=True) + EPSILON)
    return c * r, r


def roll_down(v, first):
    row = lax.broadcasted_iota(jnp.int32, v.shape, 0)
    return jnp.where(row == 0, first, pltpu.roll(v, 1, 0))


def two_parts(v):
    hi = v.astype(BF16)
    return hi, (v - hi.astype(F32)).astype(BF16)


def triangle(upper):
    row = lax.broadcasted_iota(jnp.int32, (SEG, 2 * SEG), 0)
    col = lax.broadcasted_iota(jnp.int32, (SEG, 2 * SEG), 1)
    col = jnp.where(col >= SEG, col - SEG, col)
    keep = (col > row) if upper else (col < row)
    return jnp.where(keep, 1.0, 0.0).astype(BF16)


def running(tri, first, second):
    both = jnp.concatenate([first, second], axis=1)
    hi, lo = two_parts(both)
    return nn(tri, jnp.concatenate([hi, lo], axis=0)), both


def decay_tables(dec, rise, fade):
    rate = jnp.exp(dec)
    offs = lax.broadcasted_iota(jnp.int32, (SEG, D), 0).astype(F32)
    rise[...] = jnp.exp((offs + 1.0) * rate)
    fade[...] = jnp.exp(-offs * rate)
    return jnp.exp(-float(SEG) * rate)


def spread(dst, first, v):
    for s in range(v.shape[0] // SEG):
        dst[2 * SEG * s + first : 2 * SEG * s + first + SEG, :] = v[SEG * s : SEG * (s + 1), :]


def front_kernel(
    _, len_ref, x_ref, adj_ref, g1_h, b1_h, fk_h, fv_h, fr_h, dec_h, rew_h, g2_h, b2_h, ck_h, cr_h,
    wr, wk, wv, wo, wg, wfk, wfv,
    flags, pq, grads, n1_o, dh1_o, a_o, v_o, sr_o, w_o, rd_o, sn_o, sd_o, after_o, gate_o, n2_o, dh2_o,
    r1_o, r2_o, keyed_o, valued_o, recepted_o, mixed_o, chrec_o,
    rise, fade, through, expu, nc, dc, p1, p2, kb, vb, rb, hb, cks, hid, gch, gpr, pv,
):
    i = pl.program_id(0)
    given = (g1_h, b1_h, fk_h, fv_h, fr_h, dec_h, rew_h, g2_h, b2_h, ck_h, cr_h)
    g1, b1, fk, fv, fr, dec, rew, g2, b2, ck, cr = (pv.at[k : k + 1, :] for k in range(len(given)))

    @pl.when(i == 0)
    def _():
        for b in range(NSEG):
            flags[0, b] = 0.0
        begin = jnp.int32(0)
        for j in range(NSEG):
            size = len_ref[0, j]
            at = lax.shift_right_logical(begin, 6)

            @pl.when(size > 0)
            def _():
                flags[0, at] = 1.0

            begin = begin + size
        for b in range(NSEG):
            flags[1, b] = jnp.where(b * SEG < begin, 1.0, 0.0)
        for k, v in enumerate(given):
            pv[k : k + 1, :] = v[...].reshape(1, D)
        through[...] = decay_tables(dec[...], rise, fade)
        expu[...] = jnp.exp(rew[...])
        nc[...] = jnp.zeros_like(nc)
        dc[...] = jnp.zeros_like(dc)
        p1[...] = jnp.zeros_like(p1)
        p2[...] = jnp.zeros_like(p2)

    fresh = [flags[0, i * (BLK // SEG) + s] for s in range(BLK // SEG)]
    live = [flags[1, i * (BLK // SEG) + s] for s in range(BLK // SEG)]

    for s in range(BLK // SUB):
        at = pl.ds(s * SUB, SUB)
        n1, r1 = normalize(x_ref[at, :].astype(F32))
        h1 = n1 * g1[...] + b1[...]
        before = p1[...]
        if (s * SUB) % SEG == 0:
            before = before * (1.0 - fresh[s * SUB // SEG])
        sh = roll_down(h1, before)
        p1[...] = h1[SUB - 1 :, :]
        dh1 = h1 - sh
        keyed_o[at, :] = (sh + dh1 * fk[...]).astype(BF16)
        valued_o[at, :] = (sh + dh1 * fv[...]).astype(BF16)
        recepted_o[at, :] = (sh + dh1 * fr[...]).astype(BF16)
        n1_o[at, :] = n1
        dh1_o[at, :] = dh1
        r1_o[at, :] = jnp.broadcast_to(r1, (SUB, 128))

    kb[...] = nn(keyed_o[...], wk[...])
    vb[...] = nn(valued_o[...], wv[...])
    rb[...] = nn(recepted_o[...], wr[...])

    tri = triangle(False)
    for s in range(BLK // SEG):
        at = pl.ds(s * SEG, SEG)
        keep = 1.0 - fresh[s]
        for c in range(D // 128):
            cols = pl.ds(c * 128, 128)
            a = jnp.exp(kb[at, cols])
            v = vb[at, cols]
            lift = rise[:, cols] * a
            cum, both = running(tri, lift * v, lift)
            ncar = nc[:, cols] * keep
            dcar = dc[:, cols] * keep
            sn = fade[:, cols] * (ncar + cum[:, :128])
            sd = fade[:, cols] * (dcar + cum[:, 128:])
            th = through[:, cols]
            nc[:, cols] = th * (ncar + (cum[SEG - 1 :, :128] + both[SEG - 1 :, :128]))
            dc[:, cols] = th * (dcar + (cum[SEG - 1 :, 128:] + both[SEG - 1 :, 128:]))
            e = expu[:, cols] * a
            rd = 1.0 / (sd + e)
            w = (sn + e * v) * rd
            sr = jax.nn.sigmoid(rb[at, cols])
            mixed_o[at, cols] = (sr * w).astype(BF16)

            a_o[at, cols] = a
            v_o[at, cols] = v
            sr_o[at, cols] = sr
            w_o[at, cols] = w
            rd_o[at, cols] = rd
            sn_o[at, cols] = sn
            sd_o[at, cols] = sd

    hb[...] = nn(mixed_o[...], wo[...])

    rows0 = pl.multiple_of(i * BLK, BLK)
    for s in range(BLK // SUB):
        at = pl.ds(s * SUB, SUB)
        after = x_ref[at, :].astype(F32) + hb[at, :]
        n2, r2 = normalize(after)
        h2 = n2 * g2[...] + b2[...]
        before = p2[...]
        if (s * SUB) % SEG == 0:
            before = before * (1.0 - fresh[s * SUB // SEG])
        sh = roll_down(h2, before)
        p2[...] = h2[SUB - 1 :, :]
        dh2 = h2 - sh
        cks[pl.ds(rows0 + s * SUB, SUB), :] = (sh + dh2 * ck[...]).astype(BF16)
        chrec_o[at, :] = (sh + dh2 * cr[...]).astype(BF16)
        after_o[at, :] = after
        n2_o[at, :] = n2
        dh2_o[at, :] = dh2
        r2_o[at, :] = jnp.broadcast_to(r2, (SUB, 128))

    rows = pl.ds(rows0, BLK)
    hb[...] = nn(cks[rows, :], wfk[...])
    gate_o[...] = nn(chrec_o[...], wg[...])
    for s in range(BLK // SUB):
        at = pl.ds(s * SUB, SUB)
        hp = jnp.maximum(hb[at, :], 0.0)
        hid[pl.ds(rows0 + s * SUB, SUB), :] = (hp * hp).astype(BF16)
        gate = jax.nn.sigmoid(gate_o[at, :])
        gate_o[at, :] = gate
        go = adj_ref[at, :].astype(F32) * live[s * SUB // SEG]
        gch[pl.ds(rows0 + s * SUB, SUB), :] = (go * gate).astype(BF16)
    spread(pq, 0, nn(hid[rows, :], wfv[...]))
    kb[...] = nt(gch[rows, :], wfv[...])
    for s in range(BLK // SUB):
        at = pl.ds(s * SUB, SUB)
        gpr[pl.ds(rows0 + s * SUB, SUB), :] = (2.0 * jnp.maximum(hb[at, :], 0.0) * kb[at, :]).astype(BF16)
    spread(pq, SEG, nt(gpr[rows, :], wfk[...]))

    @pl.when(i == T // BLK - 1)
    def _():
        for c in range(D // 256):
            cols = pl.ds(c * 256, 256)
            grads[:D, cols] = tn(cks[...], gpr[:, cols])
            grads[D:, cols] = tn(hid[...], gch[:, cols])


def front(half, sizes, x, adj, vecs, mats):
    steps = T // BLK
    blk = lambda w: pl.BlockSpec((BLK, w), lambda i, h: (i, 0))
    own = lambda w: pl.BlockSpec((BLK, w), lambda i, h: (jnp.where(i // PER == h[0], lax.rem(i, PER), PER), 0))
    vec = pl.BlockSpec((D,), lambda i, h: (0,))
    mat = pl.BlockSpec((D, D), lambda i, h: (0, 0), pipeline_mode=pl.Buffered(1))
    sds = jax.ShapeDtypeStruct
    vm = pltpu.VMEM
    return pl.pallas_call(
        front_kernel,
        grid_spec=pltpu.PrefetchScalarGridSpec(
            num_scalar_prefetch=1,
            grid=(steps,),
            in_specs=[pl.BlockSpec(memory_space=pltpu.SMEM), blk(D), blk(D)] + [vec] * 11 + [mat] * 7,
            out_specs=[pl.BlockSpec(memory_space=pltpu.SMEM), pl.BlockSpec((2 * BLK, D), lambda i, h: (i, 0)),
                       pl.BlockSpec((2 * D, D), lambda i, h: (0, 0), pipeline_mode=pl.Buffered(1))]
            + [own(D)] * 13 + [own(128)] * 2 + [own(D)] * 5,
            scratch_shapes=[vm((SEG, D), F32)] * 2 + [vm((1, D), F32)] * 6 + [vm((BLK, D), F32)] * 4
            + [vm((T, D), BF16)] * 4 + [vm((16, D), F32)],
        ),
        out_shape=[sds((2, NSEG), F32), sds((2 * T, D), F32), sds((2 * D, D), F32)]
        + [sds((HALF + BLK, D), F32)] * 13 + [sds((HALF + BLK, 128), F32)] * 2 + [sds((HALF + BLK, D), BF16)] * 5,
        compiler_params=pltpu.CompilerParams(dimension_semantics=("arbitrary",), vmem_limit_bytes=60 * 2**20),
        cost_estimate=pl.CostEstimate(flops=11 * 2 * T * D * D, bytes_accessed=60 * 2**20, transcendentals=4 * T * D),
        name="front",
    )(half, sizes, x, adj, *vecs, *mats)


MESH = pl.DeviceIdType.MESH
COPIES = 256
FF_ROWS = 2 * D
R_ROWS = 2048
MATS = 5
BACK_VMEM = 39
FINISH_VMEM = 2
NVEC = 11


def rows(start, size):
    return pl.ds(pl.multiple_of(start, 8), size)


def each(count, step, body, reverse=False):
    def run(k, carry):
        body((count - 1 - k) * step if reverse else k * step)
        return carry

    lax.fori_loop(0, count, run, 0)


class Links:
    def __init__(self, sends, recvs):
        self.sends, self.recvs, self.used, self.open = sends, recvs, 0, []

    def send(self, src, dst, device):
        k = self.used
        self.used += 1
        copy = pltpu.make_async_remote_copy(
            src_ref=src, dst_ref=dst, send_sem=self.sends.at[k], recv_sem=self.recvs.at[k],
            device_id=device, device_id_type=MESH,
        )
        copy.start()
        self.open.append(copy)
        return copy

    def sent(self, copy):
        self.open = [kept for kept in self.open if kept is not copy]
        copy.wait_send()

    def finish(self):
        for copy in self.open:
            copy.wait_send()


def add_into(dst, dst_at, terms, size, step=16):
    if size % step:
        step = 8

    def body(r):
        total = dst[rows(dst_at + r, step), :]
        for ref, start in terms:
            total = total + ref[rows(start + r, step), :]
        dst[rows(dst_at + r, step), :] = total

    each(size // step, step, body)


def ring_reduce(links, data, base, size, place, up, down, land, land_at, source, loaded):
    s = size // 4
    qa = (s // 2 + 7) // 8 * 8
    qb = s - qa
    mine = base + place * s
    nxt = base + lax.rem(place + 1, 4) * s
    opp = base + lax.rem(place + 2, 4) * s
    prv = base + lax.rem(place + 3, 4) * s
    starts = [land_at]
    for size_k in (qa, qb, qb, qa, qa, qb):
        starts.append(starts[-1] + size_k)
    spot = [land.at[pl.ds(a, b - a), :] for a, b in zip(starts, starts[1:])]
    fwd_a = links.send(source.at[rows(opp, qa), :], spot[0], up)
    fwd_b = links.send(source.at[rows(opp + qa, qb), :], spot[1], down)
    dir_b = links.send(source.at[rows(nxt + qa, qb), :], spot[2], up)
    dir_a = links.send(source.at[rows(prv, qa), :], spot[3], down)
    yield
    if loaded is not None:
        loaded()
    fwd_a.wait_recv()
    add_into(land, starts[0], [(data, nxt)], qa)
    cmb_a = links.send(spot[0], spot[4], up)
    fwd_b.wait_recv()
    add_into(land, starts[1], [(data, prv + qa)], qb)
    for copy in (fwd_a, fwd_b, dir_b, dir_a):
        links.sent(copy)
    cmb_b = links.send(spot[1], spot[5], down)
    yield
    dir_a.wait_recv()
    dir_b.wait_recv()
    cmb_a.wait_recv()
    cmb_b.wait_recv()
    add_into(data, mine, [(land, starts[3]), (land, starts[4])], qa)
    add_into(data, mine + qa, [(land, starts[2]), (land, starts[5])], qb)


def ring_gather(links, data, base, size, place, up, down, share):
    s = size // 4
    qa = (s // 2 + 7) // 8 * 8
    qb = s - qa
    mine = base + place * s
    nxt = base + lax.rem(place + 1, 4) * s
    opp = base + lax.rem(place + 2, 4) * s
    prv = base + lax.rem(place + 3, 4) * s
    own = data.at[rows(mine, s), :]
    to_up = links.send(own, own, up)
    to_down = links.send(own, own, down)
    share(own)
    yield
    to_up.wait_recv()
    half_a = data.at[rows(prv, qa), :]
    on_a = links.send(half_a, half_a, up)
    to_down.wait_recv()
    half_b = data.at[rows(nxt + qa, qb), :]
    on_b = links.send(half_b, half_b, down)
    share(data.at[rows(prv, s), :])
    share(data.at[rows(nxt, s), :])
    yield
    on_a.wait_recv()
    on_b.wait_recv()
    share(data.at[rows(opp, s), :])


def sum_of_four(links, data, base, size, place, others, land, land_at):
    mine = rows(land_at + place * size, size)
    land[mine, :] = data[rows(base, size), :]
    copies = [links.send(land.at[mine, :], land.at[mine, :], device) for device in others]
    yield
    for copy in copies:
        copy.wait_recv()

    def body(r):
        a, b, c, d = (land[rows(land_at + k * size + r, 8), :] for k in range(4))
        data[rows(base + r, 8), :] = (a + b) + (c + d)

    each(size // 8, 8, body)


def all_reduce(links, data, base, size, axes, land, land_at, last, last_land, last_at, source, loaded, share):
    spans = []
    for place, up, down in axes:
        spans.append((base, size))
        yield from ring_reduce(links, data, base, size, place, up, down, land, land_at, source, loaded)
        source, loaded = data, None
        land_at += 3 * (size // 4)
        size = size // 4
        base = base + place * size
    yield from last(links, data, base, size, last_land, last_at)
    for k in (1, 0):
        place, up, down = axes[k]
        yield from ring_gather(links, data, *spans[k], place, up, down, share if k == 0 else lambda ref: None)


def step(*jobs):
    for job in jobs:
        next(job, None)


def drain(*jobs):
    live = list(jobs)
    while live:
        live = [job for job in live if next(job, job) is not job]


def back_kernel(
    flags, pq, grads, n1_h, dh1_h, a_h, v_h, sr_h, w_h, rd_h, sn_h, sd_h, after_h, gate_h, n2_h, dh2_h,
    r1_h, r2_h, keyed_h, valued_h, recepted_h, mixed_h, chrec_h, adj_h,
    g1_h, fk_h, fv_h, fr_h, dec_h, rew_h, g2_h, ck_h, cr_h, wr_h, wk_h, wv_h, wo_h, wg_h,
    out_o, gi, vec_o, red, ff,
    front4, r1, r2, keyed, valued, recepted, mixed, chrec, adj, wr, wo, wg,
    fin, xb, gg, gb, gk, gv, gp, t0, t1, t2, other, ffland, yland, vland,
    urow, urow2, gsend, grecv, acc, rise, fade, through, expu, sums, gc, pv,
    sends, recvs, fill, ready_ring, ready_sib,
):
    dp = lax.axis_index("dp")
    tensor = lax.axis_index("tensor")
    x, z, yl = dp // 8, lax.rem(dp // 2, 4), lax.rem(dp, 2)
    h, c = tensor // 2, lax.rem(tensor, 2)
    y = 2 * h + yl

    def chip(cx, cz, cy):
        cx, cz, cy = lax.rem(cx + 4, 4), lax.rem(cz + 4, 4), lax.rem(cy + 4, 4)
        return {"dp": (cx * 4 + cz) * 2 + lax.rem(cy, 2), "tensor": (cy // 2) * 2 + c}

    xp, xo, xm = (chip(x + k, z, y) for k in (1, 2, 3))
    zp, zo, zm = (chip(x, z + k, y) for k in (1, 2, 3))
    yp, opp, ym = (chip(x, z, y + k) for k in (1, 2, 3))
    sib = {"dp": dp, "tensor": h * 2 + (1 - c)}
    pair = {"dp": dp + 1 - 2 * yl, "tensor": tensor}
    own_at, other_at = h * HALF, (1 - h) * HALF
    mine_at = c * R_ROWS

    given = (g1_h, fk_h, fv_h, fr_h, dec_h, rew_h, g2_h, ck_h, cr_h)
    g1, fk, fv, fr, dec, rew, g2, ck, cr = (pv.at[k : k + 1, :] for k in range(len(given)))
    fills = []

    def bring(src, dst):
        copy = pltpu.make_async_copy(src, dst, fill.at[len(fills)])
        copy.start()
        fills.append(copy)
        return copy

    def group(start):
        return rows(2 * start, 2 * SEG)

    PART, ARECV, CRECV, BRECV = (512 * k for k in range(4))
    part_in = [
        bring(pq.at[group(other_at + 128 * j + SEG * c), :], xb.at[pl.ds(PART + 128 * j, 128), :]) for j in range(4)
    ]
    ff_in = bring(grads, ff)
    fin_in = [
        bring(pq.at[group(own_at + 128 * j + SEG * c), :], fin.at[group(128 * j + SEG * c), :]) for j in range(4)
    ]
    half = pl.ds(0, HALF)
    AFTER, GATE, N2, DH2 = (HALF * k for k in range(4))
    A, V, SR, W, RD, SN, SD = (HALF * k for k in range(7))
    first_in = [
        bring(s.at[half, :], front4.at[pl.ds(HALF * k, HALF), :]) for k, s in enumerate((after_h, gate_h, n2_h, dh2_h))
    ]
    first_in += [bring(adj_h.at[rows(own_at, HALF), :], adj), bring(wg_h, wg), bring(r2_h.at[half, :], r2)]
    first_in += [bring(wo_h, wo)]
    second_in = [
        bring(s.at[half, :], red.at[pl.ds(HALF * k, HALF), :])
        for k, s in enumerate((a_h, v_h, sr_h, w_h, rd_h, sn_h, sd_h))
    ]
    lanes = pl.ds(pl.multiple_of(c * HALF_D, 128), HALF_D)
    third_in = [
        bring(s.at[half, lanes], d)
        for s, d in (
            (mixed_h, mixed), (chrec_h, chrec), (keyed_h, keyed), (valued_h, valued), (recepted_h, recepted),
        )
    ]
    third_in += [bring(r1_h.at[half, :], r1), bring(wr_h, wr)]

    barrier = pltpu.get_barrier_semaphore()
    partners = (xp, xo, xm, zp, zo, zm, yp, ym, opp, sib)
    for device in partners:
        pl.semaphore_signal(barrier, inc=1, device_id=device, device_id_type=MESH)
    pl.semaphore_wait(barrier, len(partners))

    links = Links(sends, recvs)
    ax, az = (x, xp, xm), (z, zp, zm)

    def with_pair(links, data, base, size, land, land_at):
        whole = data.at[rows(base, size), :]
        copy = links.send(whole, land.at[pl.ds(land_at, size), :], pair)
        yield
        links.sent(copy)
        copy.wait_recv()
        add_into(data, base, [(land, land_at)], size, 8)

    def with_y(links, data, base, size, land, land_at):
        yield from sum_of_four(links, data, base, size, y, (yp, opp, ym), land, land_at)

    waited = []

    def ff_loaded():
        if not waited:
            ff_in.wait()
            waited.append(True)

    n = FF_ROWS // 4
    ffs = [
        all_reduce(
            links, ff, n * k, n, (ax, az) if k < 2 else (az, ax), ffland, n * k,
            with_pair, ffland, n * k + 15 * n // 16, grads, ff_loaded, lambda ref: None,
        )
        for k in range(4)
    ]

    def one():
        step(ffs[0], ffs[2])

    def two():
        step(ffs[1], ffs[3])

    a_in = [
        links.send(pq.at[group(other_at + 128 * j + SEG * (1 - c)), :], xb.at[pl.ds(ARECV + 128 * j, 128), :], sib)
        for j in range(4)
    ]
    one()
    c_in = [
        links.send(pq.at[group(own_at + 128 * j + SEG * (1 - c)), :], xb.at[pl.ds(CRECV + 128 * j, 128), :], sib)
        for j in range(4)
    ]
    b_in = []
    for j in range(4):
        part_in[j].wait()
        a_in[j].wait_recv()
        add_into(xb, PART + 128 * j, [(xb, ARECV + 128 * j)], 128)
        b_in.append(
            links.send(xb.at[pl.ds(PART + 128 * j, 128), :], xb.at[pl.ds(BRECV + 128 * j, 128), :], opp)
        )
    one()
    two()

    for k, v in enumerate(given):
        pv[k : k + 1, :] = v[...].reshape(1, D)
    through[...] = decay_tables(dec[...], rise, fade)
    expu[...] = jnp.exp(rew[...])
    acc[...] = jnp.zeros_like(acc)
    seg0 = h * (HALF // SEG)
    not_last = (1 - h).astype(F32)

    def fold(v):
        return jnp.sum(v.reshape(-1, 8, D), axis=0)

    def tally(k, v):
        acc[pl.ds(8 * k, 8), :] += fold(v)

    GAIN1, BIAS1, MIXK, MIXV, MIXR, LOGD, REW, GAIN2, BIAS2, CMIXK, CMIXR = range(NVEC)

    for copy in first_in:
        copy.wait()

    def take(j):
        fin_in[j].wait()
        c_in[j].wait_recv()
        b_in[j].wait_recv()
        add_into(fin, 2 * (128 * j + SEG * c), [(xb, CRECV + 128 * j), (xb, BRECV + 128 * j)], 128)
        mine = fin.at[group(128 * j + SEG * c), :]
        copy = links.send(mine, mine, sib)
        links.sent(b_in[j])
        copy.wait_recv()
        links.sent(copy)

    def gate_part(j):
        lo = 128 * j
        for seg in range(2):
            live = flags[1, seg0 + 2 * j + seg]

            def body(r, seg=seg, live=live):
                at = lo + SEG * seg + r
                gate = front4[rows(GATE + at, SUB), :]
                co = fin[rows(2 * (lo + SEG * seg) + r, SUB), :]
                res = live * (front4[rows(AFTER + at, SUB), :] + gate * co)
                front4[rows(AFTER + at, SUB), :] = res.astype(BF16).astype(F32)
                go = adj[rows(at, SUB), :].astype(F32) * live
                gg[rows(at, SUB), :] = (go * co * gate * (1.0 - gate)).astype(BF16)

            each(SEG // SUB, SUB, body)
        t0[...] = nt(gg[pl.ds(lo, 128), :], wg[...])
        for seg in range(2):

            def body2(r, seg=seg):
                at = 2 * (lo + SEG * seg) + r
                qk = fin[rows(at + SEG, SUB), :]
                qr = t0[rows(SEG * seg + r, SUB), :]
                dh2 = front4[rows(DH2 + lo + SEG * seg + r, SUB), :]
                tally(CMIXK, qk * dh2)
                tally(CMIXR, qr * dh2)
                base = qk * ck[...] + qr * cr[...]
                fin[rows(at, SUB), :] = base
                fin[rows(at + SEG, SUB), :] = (qk + qr) - base

            each(SEG // SUB, SUB, body2)

    one()
    two()
    take(0)
    gate_part(0)
    gsend[...] = fin[SEG : SEG + 8, :]
    u_in = links.send(gsend, urow, opp)
    one()
    two()
    one()
    two()
    take(1)
    gate_part(1)
    one()
    two()
    one()
    two()
    one()
    two()
    two()
    take(2)
    gate_part(2)
    one()
    take(3)
    for device in (xp, xm, zp, zm):
        pl.semaphore_signal(ready_ring, inc=1, device_id=device, device_id_type=MESH)
    two()
    gate_part(3)
    wk = wg
    wk_in = bring(wk_h, wk)
    half_at = AFTER + 256 * c
    out_in = links.send(front4.at[rows(half_at, 256), :], other.at[rows(256 * c, 256), :], opp)
    u_in.wait_recv()

    def lifted(nxt, u):
        row = lax.broadcasted_iota(jnp.int32, u.shape, 0)
        return jnp.where(row == u.shape[0] - 1, nxt, pltpu.roll(u, u.shape[0] - 1, 0))

    def norm_back(e, n, r, gain):
        f = e * gain
        return r * (f - jnp.mean(f, axis=-1, keepdims=True) - n * jnp.mean(f * n, axis=-1, keepdims=True))

    def keep_next(seg):
        return 1.0 - flags[0, jnp.minimum(seg0 + seg + 1, NSEG - 1)]

    def walk_rows(edge_row, sub_body, after_chunk=None):
        for j in reversed(range(4)):
            for seg in (1, 0):
                s = 2 * j + seg
                live = flags[1, seg0 + s]
                for k in reversed(range(SEG // SUB)):
                    lo = SEG * s + SUB * k
                    at = 2 * SEG * s + SUB * k
                    if lo + SUB == HALF:
                        nxt = edge_row[0:1, :] * (not_last * keep_next(s))
                    elif k == SEG // SUB - 1:
                        nxt = fin[2 * SEG * (s + 1) + SEG : 2 * SEG * (s + 1) + SEG + 1, :] * keep_next(s)
                    else:
                        nxt = fin[at + SEG + SUB : at + SEG + SUB + 1, :]
                    sub_body(lo, at, live, nxt)
            if after_chunk is not None:
                after_chunk(j)

    for copy in second_in:
        copy.wait()

    def after_rows(lo, at, live, nxt):
        e = fin[pl.ds(at, SUB), :] + lifted(nxt, fin[pl.ds(at + SEG, SUB), :])
        n = front4[pl.ds(N2 + lo, SUB), :]
        tally(GAIN2, e * n)
        tally(BIAS2, e)
        go = adj[pl.ds(lo, SUB), :].astype(F32) * live
        ga = go + norm_back(e, n, r2[pl.ds(lo, SUB), 0:1], g2[...])
        front4[pl.ds(N2 + lo, SUB), :] = ga
        gb[pl.ds(lo, SUB), :] = ga.astype(BF16)

    def mixed_chunk(j):
        t0[...] = nt(gb[pl.ds(128 * j, 128), :], wo[...])
        for seg in (1, 0):
            total = 16 * (2 * j + seg)
            sums[pl.ds(total, 16), :] = jnp.zeros((16, D), F32)

            def body(r, seg=seg, total=total):
                at = 128 * j + SEG * seg + r
                gm = t0[rows(SEG * seg + r, SUB), :]
                sr = red[rows(SR + at, SUB), :]
                w = red[rows(W + at, SUB), :]
                gw = gm * sr
                q = gw * red[rows(RD + at, SUB), :]
                red[rows(RD + at, SUB), :] = q
                gp[rows(at, SUB), :] = (gw * w * (1.0 - sr)).astype(BF16)
                fq = fade[rows(r, SUB), :] * q
                sums[pl.ds(total, 8), :] += fold(fq)
                sums[pl.ds(total + 8, 8), :] += fold(fq * w)

            each(SEG // SUB, SUB, body)

    walk_rows(urow, after_rows, mixed_chunk)
    wv = wo
    wv_in = bring(wv_h, wv)
    one()
    two()

    first = jnp.zeros((1, D), F32)
    second = jnp.zeros((1, D), F32)
    th = through[...]
    for s in reversed(range(8)):
        q = jnp.sum(sums[pl.ds(16 * s, 8), :], axis=0, keepdims=True)
        qw = jnp.sum(sums[pl.ds(16 * s + 8, 8), :], axis=0, keepdims=True)
        if s < 7:
            q = q + th * (first * keep_next(s))
            qw = qw + th * (second * keep_next(s))
        first, second = q, qw
    sums[0:1, :] = first
    sums[1:2, :] = second
    g_in = links.send(sums.at[pl.ds(0, 8), :], grecv, opp)
    n1_in = bring(n1_h.at[half, :], front4.at[pl.ds(GATE, HALF), :])
    dh1_in = bring(dh1_h.at[half, :], front4.at[pl.ds(DH2, HALF), :])
    for copy in third_in:
        copy.wait()
    g_in.wait_recv()
    edge = not_last * keep_next(7)
    gc[0:1, :] = grecv[0:1, :] * edge
    gc[1:2, :] = grecv[1:2, :] * edge
    tri = triangle(True)

    def key_value(k, carry):
        s = 7 - k
        lo = SEG * s
        keep = 1.0 - flags[0, seg0 + s]
        for col in range(D // 128):
            cols = pl.ds(col * 128, 128)
            at = rows(lo, SEG)
            q = red[rows(RD + lo, SEG), cols]
            w = red[rows(W + lo, SEG), cols]
            a = red[rows(A + lo, SEG), cols]
            v = red[rows(V + lo, SEG), cols]
            fq = fade[:, cols] * q
            cum, both = running(tri, fq, fq * w)
            cn = through[:, cols] * gc[0:1, cols]
            cd = through[:, cols] * gc[1:2, cols]
            gn = rise[:, cols] * (cum[:, :128] + cn)
            gd = rise[:, cols] * (cum[:, 128:] + cd)
            gc[0:1, cols] = (both[0:1, :128] + cum[0:1, :128] + cn) * keep
            gc[1:2, cols] = (both[0:1, 128:] + cum[0:1, 128:] + cd) * keep
            eq = expu[:, cols] * a * q
            gvv = a * gn + eq
            gv[at, cols] = gvv.astype(BF16)
            gk[at, cols] = (v * gvv - (a * gd + eq * w)).astype(BF16)
            up = eq * (v - w)
            down = gn * red[rows(SN + lo, SEG), cols] - gd * red[rows(SD + lo, SEG), cols]
            acc[pl.ds(8 * REW, 8), cols] += jnp.sum(up.reshape(-1, 8, 128), axis=0)
            acc[pl.ds(8 * LOGD, 8), cols] += jnp.sum(down.reshape(-1, 8, 128), axis=0)
        return carry

    lax.fori_loop(0, 8, key_value, 0)
    pl.semaphore_signal(ready_sib, inc=1, device_id=sib, device_id_type=MESH)

    for k, (left, right) in enumerate(((recepted, gp), (keyed, gk), (valued, gv), (mixed, gb), (chrec, gg))):
        for col in range(D // 256):
            cols = pl.ds(256 * col, 256)
            red[rows(mine_at + HALF_D * k, HALF_D), cols] = tn(left[...], right[:, cols])
    red[rows(mine_at + HALF_D * MATS, R_ROWS - HALF_D * MATS), :] = jnp.zeros((R_ROWS - HALF_D * MATS, D), F32)

    shared = []

    def share(ref):
        if not shared:
            pl.semaphore_wait(ready_sib, 1)
        shared.append(links.send(ref, ref, sib))

    pl.semaphore_wait(ready_ring, 4)
    n = R_ROWS // 4
    reds = [
        all_reduce(
            links, red, mine_at + n * k, n, (ax, az) if k < 2 else (az, ax), xb, n * k,
            with_y, yland, n // 4 * k, red, None, share,
        )
        for k in range(4)
    ]

    def three():
        step(reds[0], reds[2])

    def four():
        step(reds[1], reds[3])

    three()
    for copy in (n1_in, dh1_in, wk_in, wv_in):
        copy.wait()

    def front_chunk(j):
        at0 = pl.ds(128 * j, 128)
        t0[...] = nt(gk[at0, :], wk[...])
        t1[...] = nt(gv[at0, :], wv[...])
        t2[...] = nt(gp[at0, :], wr[...])
        for seg in range(2):

            def body(r, seg=seg):
                lo = 128 * j + SEG * seg
                pk, pv_, pr = (t[rows(SEG * seg + r, SUB), :] for t in (t0, t1, t2))
                dh1 = front4[rows(DH2 + lo + r, SUB), :]
                tally(MIXK, pk * dh1)
                tally(MIXV, pv_ * dh1)
                tally(MIXR, pr * dh1)
                base = pk * fk[...] + pv_ * fv[...] + pr * fr[...]
                fin[rows(2 * lo + r, SUB), :] = base
                fin[rows(2 * lo + SEG + r, SUB), :] = (pk + pv_ + pr) - base

            each(SEG // SUB, SUB, body)

    for j in range(4):
        front_chunk(j)
        if j == 0:
            u2_in = links.send(fin.at[pl.ds(SEG, 8), :], urow2, opp)
        if j == 1:
            three()
            four()
    u2_in.wait_recv()
    drain(*ffs)

    def input_rows(lo, at, live, nxt):
        e = fin[pl.ds(at, SUB), :] + lifted(nxt, fin[pl.ds(at + SEG, SUB), :])
        n = front4[pl.ds(GATE + lo, SUB), :]
        tally(GAIN1, e * n)
        tally(BIAS1, e)
        gi[rows(own_at + lo, SUB), :] = front4[pl.ds(N2 + lo, SUB), :] + norm_back(e, n, r1[pl.ds(lo, SUB), 0:1], g1[...])

    walk_rows(urow2, input_rows)
    gi_rows = gi.at[rows(own_at + 256 * c, 256), :]
    gi_in = links.send(gi_rows, gi_rows, opp)
    scale = -jnp.exp(dec[...]) * jnp.exp(-jnp.exp(dec[...]))
    vec_o[...] = jnp.zeros_like(vec_o)
    for k in range(NVEC):
        total = jnp.sum(acc[pl.ds(8 * k, 8), :], axis=0, keepdims=True)
        vec_o[k : k + 1, :] = total * scale if k == LOGD else total

    def vectors():
        for k, (place, others) in enumerate(((x, (xp, xo, xm)), (z, (zp, zo, zm)), (y, (yp, opp, ym)))):
            yield from sum_of_four(links, vec_o, 0, 16, place, others, vland, 64 * k)

    vecs = vectors()
    step(vecs)
    out_in.wait_recv()
    theirs = other.at[rows(256 * c, 256), :]
    out_on = links.send(theirs, theirs, sib)
    three()
    four()
    step(vecs)
    three()
    four()
    step(vecs)

    def cast_rows(r):
        out_o[rows(own_at + r, SUB), :] = front4[rows(AFTER + r, SUB), :].astype(BF16)
        out_o[rows(other_at + r, SUB), :] = other[rows(r, SUB), :].astype(BF16)

    out_on.wait_recv()
    each(HALF // SUB, SUB, cast_rows)
    three()
    four()
    drain(vecs)
    three()
    four()
    gi_in.wait_recv()
    gi_theirs = gi.at[rows(other_at + 256 * c, 256), :]
    gi_on = links.send(gi_theirs, gi_theirs, sib)
    drain(*reds)
    gi_on.wait_recv()
    for copy in shared:
        copy.wait_recv()
    links.finish()


def back(front_outs, adj, vecs, mats):
    g1, b1, fk, fv, fr, dec, rew, g2, b2, ck, cr = vecs
    flags, rest = front_outs[0], front_outs[1:]
    vm = pltpu.VMEM
    anywhere = pl.BlockSpec(memory_space=pl.ANY)
    vmem = pl.BlockSpec(memory_space=pltpu.VMEM)
    half = lambda dt: vm((HALF, D), dt)
    return pl.pallas_call(
        back_kernel,
        in_specs=[pl.BlockSpec(memory_space=pltpu.SMEM)] + [anywhere] * len(rest) + [anywhere]
        + [vmem] * 9 + [anywhere] * 5,
        out_specs=[vmem] * 5,
        out_shape=[vm((T, D), BF16), vm((T, D), F32), vm((16, D), F32), vm((2 * R_ROWS, D), F32), vm((FF_ROWS, D), F32)],
        scratch_shapes=[vm((4 * HALF, D), F32), vm((HALF, 128), F32), vm((HALF, 128), F32)]
        + [vm((HALF, HALF_D), BF16)] * 5 + [half(BF16)] + [vm((D, D), BF16)] * 3
        + [vm((2 * HALF, D), F32), vm((R_ROWS, D), F32)]
        + [half(BF16)] * 5 + [vm((128, D), F32)] * 3 + [half(F32)]
        + [vm((FF_ROWS, D), F32), vm((R_ROWS // 4, D), F32), vm((192, D), F32)]
        + [vm((8, D), F32)] * 4 + [vm((8 * NVEC, D), F32)] + [vm((SEG, D), F32)] * 2
        + [vm((1, D), F32)] * 2 + [vm((128, D), F32), vm((8, D), F32), vm((16, D), F32)]
        + [pltpu.SemaphoreType.DMA((COPIES,)), pltpu.SemaphoreType.DMA((COPIES,)),
           pltpu.SemaphoreType.DMA((48,)), pltpu.SemaphoreType.REGULAR, pltpu.SemaphoreType.REGULAR],
        compiler_params=pltpu.CompilerParams(collective_id=1, has_side_effects=True, vmem_limit_bytes=BACK_VMEM * 2**20),
        cost_estimate=pl.CostEstimate(flops=14 * T * D * D, bytes_accessed=60 * 2**20, transcendentals=0),
        name="back",
    )(flags, *rest, adj, g1, fk, fv, fr, dec, rew, g2, ck, cr, *mats[:5])


def finish_kernel(out, gi, vec, red, ff, *refs):
    out_o, gi_o, mats, ck_o, cv_o, vecs, sems = refs[0], refs[1], refs[2:7], refs[7], refs[8], refs[9:20], refs[20]
    pairs = [(gi, gi_o), (ff.at[pl.ds(0, D), :], ck_o), (ff.at[pl.ds(D, D), :], cv_o), (out, out_o)]
    for k in range(MATS):
        for core in range(2):
            src = red.at[pl.ds(core * R_ROWS + HALF_D * k, HALF_D), :]
            pairs.append((src, mats[k].at[pl.ds(HALF_D * core, HALF_D), :]))
    copies = [pltpu.make_async_copy(src, dst, sems.at[k]) for k, (src, dst) in enumerate(pairs)]
    for copy in copies:
        copy.start()
    for k in range(NVEC):
        vecs[k][...] = vec[k : k + 1, :].reshape(D)
    for copy in copies:
        copy.wait()


def finish(out, gi, vec, red, ff):
    sds = jax.ShapeDtypeStruct
    anywhere = pl.BlockSpec(memory_space=pl.ANY)
    vmem = pl.BlockSpec(memory_space=pltpu.VMEM)
    return pl.pallas_call(
        finish_kernel,
        in_specs=[vmem] * 5,
        out_specs=[anywhere] * 9 + [vmem] * NVEC,
        out_shape=[sds((T, D), BF16), sds((T, D), F32)] + [sds((D, D), F32)] * 7 + [sds((D,), F32)] * NVEC,
        scratch_shapes=[pltpu.SemaphoreType.DMA((16,))],
        compiler_params=pltpu.CompilerParams(vmem_limit_bytes=FINISH_VMEM * 2**20),
        name="finish",
    )(out, gi, vec, red, ff)


def body(
    entering_activations, sample_sizes, initial_layernorm_scale, initial_layernorm_offset, temporal_lookup_fraction,
    temporal_content_fraction, temporal_gating_fraction, fading_speed_logarithm, present_reward,
    temporal_gating_matrix, temporal_lookup_matrix, temporal_content_matrix, temporal_emission_matrix,
    latter_layernorm_scale, latter_layernorm_offset, feedforward_lookup_fraction, feedforward_gating_fraction,
    feedforward_gating_matrix, feedforward_lookup_matrix, feedforward_content_matrix, upstream_adjoint,
):
    vecs = (
        initial_layernorm_scale, initial_layernorm_offset, temporal_lookup_fraction, temporal_content_fraction,
        temporal_gating_fraction, fading_speed_logarithm, present_reward, latter_layernorm_scale,
        latter_layernorm_offset, feedforward_lookup_fraction, feedforward_gating_fraction,
    )
    mats = (
        temporal_gating_matrix, temporal_lookup_matrix, temporal_content_matrix, temporal_emission_matrix,
        feedforward_gating_matrix, feedforward_lookup_matrix, feedforward_content_matrix,
    )
    half = (lax.axis_index("tensor") // 2).astype(jnp.int32).reshape(1)
    fronts = front(half, sample_sizes, entering_activations, upstream_adjoint, vecs, mats)
    out, grad_inputs, recw, keyw, valw, outw, chrec, chkey, chval, *g = finish(*back(fronts, upstream_adjoint, vecs, mats))
    return (
        out, grad_inputs, g[0], g[1], g[2], g[3], g[4], g[5], g[6], recw, keyw, valw, outw,
        g[7], g[8], g[9], g[10], chrec, chkey, chval,
    )


def solution(mesh):
    split = P("dp", None)
    in_specs = (split, split) + (P(),) * 16 + (P(None, "tensor"), P("tensor", None), split)
    out_specs = (split, split) + (P(),) * 16 + (P(None, "tensor"), P("tensor", None))
    return jax.shard_map(body, mesh=mesh, in_specs=in_specs, out_specs=out_specs, check_vma=False)
```

```python
import functools

import jax
import jax.numpy as jnp
from jax import lax
from jax.experimental import pallas as pl
from jax.experimental.pallas import tpu as pltpu
from jax.sharding import PartitionSpec as P

F32 = jnp.float32
BF16 = jnp.bfloat16
EPSILON = 1e-05
SEG = 64
D = 768
T = 1024
HALF = 512
HALF_D = D // 2
BLK = 256
SUB = 32
NSEG = T // SEG
PER = HALF // BLK


def nn(left, right):
    return jnp.dot(left, right, preferred_element_type=F32)


def nt(left, right):
    return lax.dot_general(left, right, (((1,), (1,)), ((), ())), preferred_element_type=F32)


def tn(left, right):
    return lax.dot_general(left, right, (((0,), (0,)), ((), ())), preferred_element_type=F32)


def normalize(v):
    c = v - jnp.mean(v, axis=-1, keepdims=True)
    r = lax.rsqrt(jnp.mean(c * c, axis=-1, keepdims=True) + EPSILON)
    return c * r, r


def roll_down(v, first):
    row = lax.broadcasted_iota(jnp.int32, v.shape, 0)
    return jnp.where(row == 0, first, pltpu.roll(v, 1, 0))


def two_parts(v):
    hi = v.astype(BF16)
    return hi, (v - hi.astype(F32)).astype(BF16)


def triangle(upper):
    row = lax.broadcasted_iota(jnp.int32, (SEG, 2 * SEG), 0)
    col = lax.broadcasted_iota(jnp.int32, (SEG, 2 * SEG), 1)
    col = jnp.where(col >= SEG, col - SEG, col)
    keep = (col > row) if upper else (col < row)
    return jnp.where(keep, 1.0, 0.0).astype(BF16)


def running(tri, first, second):
    both = jnp.concatenate([first, second], axis=1)
    hi, lo = two_parts(both)
    return nn(tri, jnp.concatenate([hi, lo], axis=0)), both


def decay_tables(dec, rise, fade):
    rate = jnp.exp(dec)
    offs = lax.broadcasted_iota(jnp.int32, (SEG, D), 0).astype(F32)
    rise[...] = jnp.exp((offs + 1.0) * rate)
    fade[...] = jnp.exp(-offs * rate)
    return jnp.exp(-float(SEG) * rate)


def spread(dst, first, v):
    for s in range(v.shape[0] // SEG):
        dst[2 * SEG * s + first : 2 * SEG * s + first + SEG, :] = v[SEG * s : SEG * (s + 1), :]


def front_kernel(
    _, len_ref, x_ref, adj_ref, g1_h, b1_h, fk_h, fv_h, fr_h, dec_h, rew_h, g2_h, b2_h, ck_h, cr_h,
    wr, wk, wv, wo, wg, wfk, wfv,
    flags, pq, grads, n1_o, dh1_o, a_o, v_o, sr_o, w_o, rd_o, sn_o, sd_o, after_o, gate_o, n2_o, dh2_o,
    r1_o, r2_o, keyed_o, valued_o, recepted_o, mixed_o, chrec_o,
    rise, fade, through, expu, nc, dc, p1, p2, kb, vb, rb, hb, cks, hid, gch, gpr, pv,
):
    i = pl.program_id(0)
    given = (g1_h, b1_h, fk_h, fv_h, fr_h, dec_h, rew_h, g2_h, b2_h, ck_h, cr_h)
    g1, b1, fk, fv, fr, dec, rew, g2, b2, ck, cr = (pv.at[k : k + 1, :] for k in range(len(given)))

    @pl.when(i == 0)
    def _():
        for b in range(NSEG):
            flags[0, b] = 0.0
        begin = jnp.int32(0)
        for j in range(NSEG):
            size = len_ref[0, j]
            at = lax.shift_right_logical(begin, 6)

            @pl.when(size > 0)
            def _():
                flags[0, at] = 1.0

            begin = begin + size
        for b in range(NSEG):
            flags[1, b] = jnp.where(b * SEG < begin, 1.0, 0.0)
        for k, v in enumerate(given):
            pv[k : k + 1, :] = v[...].reshape(1, D)
        through[...] = decay_tables(dec[...], rise, fade)
        expu[...] = jnp.exp(rew[...])
        nc[...] = jnp.zeros_like(nc)
        dc[...] = jnp.zeros_like(dc)
        p1[...] = jnp.zeros_like(p1)
        p2[...] = jnp.zeros_like(p2)

    fresh = [flags[0, i * (BLK // SEG) + s] for s in range(BLK // SEG)]
    live = [flags[1, i * (BLK // SEG) + s] for s in range(BLK // SEG)]

    for s in range(BLK // SUB):
        at = pl.ds(s * SUB, SUB)
        n1, r1 = normalize(x_ref[at, :].astype(F32))
        h1 = n1 * g1[...] + b1[...]
        before = p1[...]
        if (s * SUB) % SEG == 0:
            before = before * (1.0 - fresh[s * SUB // SEG])
        sh = roll_down(h1, before)
        p1[...] = h1[SUB - 1 :, :]
        dh1 = h1 - sh
        keyed_o[at, :] = (sh + dh1 * fk[...]).astype(BF16)
        valued_o[at, :] = (sh + dh1 * fv[...]).astype(BF16)
        recepted_o[at, :] = (sh + dh1 * fr[...]).astype(BF16)
        n1_o[at, :] = n1
        dh1_o[at, :] = dh1
        r1_o[at, :] = jnp.broadcast_to(r1, (SUB, 128))

    kb[...] = nn(keyed_o[...], wk[...])
    vb[...] = nn(valued_o[...], wv[...])
    rb[...] = nn(recepted_o[...], wr[...])

    tri = triangle(False)
    for s in range(BLK // SEG):
        at = pl.ds(s * SEG, SEG)
        keep = 1.0 - fresh[s]
        for c in range(D // 128):
            cols = pl.ds(c * 128, 128)
            a = jnp.exp(kb[at, cols])
            v = vb[at, cols]
            lift = rise[:, cols] * a
            cum, both = running(tri, lift * v, lift)
            ncar = nc[:, cols] * keep
            dcar = dc[:, cols] * keep
            sn = fade[:, cols] * (ncar + cum[:, :128])
            sd = fade[:, cols] * (dcar + cum[:, 128:])
            th = through[:, cols]
            nc[:, cols] = th * (ncar + (cum[SEG - 1 :, :128] + both[SEG - 1 :, :128]))
            dc[:, cols] = th * (dcar + (cum[SEG - 1 :, 128:] + both[SEG - 1 :, 128:]))
            e = expu[:, cols] * a
            rd = 1.0 / (sd + e)
            w = (sn + e * v) * rd
            sr = jax.nn.sigmoid(rb[at, cols])
            mixed_o[at, cols] = (sr * w).astype(BF16)

            a_o[at, cols] = a
            v_o[at, cols] = v
            sr_o[at, cols] = sr
            w_o[at, cols] = w
            rd_o[at, cols] = rd
            sn_o[at, cols] = sn
            sd_o[at, cols] = sd

    hb[...] = nn(mixed_o[...], wo[...])

    rows0 = pl.multiple_of(i * BLK, BLK)
    for s in range(BLK // SUB):
        at = pl.ds(s * SUB, SUB)
        after = x_ref[at, :].astype(F32) + hb[at, :]
        n2, r2 = normalize(after)
        h2 = n2 * g2[...] + b2[...]
        before = p2[...]
        if (s * SUB) % SEG == 0:
            before = before * (1.0 - fresh[s * SUB // SEG])
        sh = roll_down(h2, before)
        p2[...] = h2[SUB - 1 :, :]
        dh2 = h2 - sh
        cks[pl.ds(rows0 + s * SUB, SUB), :] = (sh + dh2 * ck[...]).astype(BF16)
        chrec_o[at, :] = (sh + dh2 * cr[...]).astype(BF16)
        after_o[at, :] = after
        n2_o[at, :] = n2
        dh2_o[at, :] = dh2
        r2_o[at, :] = jnp.broadcast_to(r2, (SUB, 128))

    rows = pl.ds(rows0, BLK)
    hb[...] = nn(cks[rows, :], wfk[...])
    gate_o[...] = nn(chrec_o[...], wg[...])
    for s in range(BLK // SUB):
        at = pl.ds(s * SUB, SUB)
        hp = jnp.maximum(hb[at, :], 0.0)
        hid[pl.ds(rows0 + s * SUB, SUB), :] = (hp * hp).astype(BF16)
        gate = jax.nn.sigmoid(gate_o[at, :])
        gate_o[at, :] = gate
        go = adj_ref[at, :].astype(F32) * live[s * SUB // SEG]
        gch[pl.ds(rows0 + s * SUB, SUB), :] = (go * gate).astype(BF16)
    spread(pq, 0, nn(hid[rows, :], wfv[...]))
    kb[...] = nt(gch[rows, :], wfv[...])
    for s in range(BLK // SUB):
        at = pl.ds(s * SUB, SUB)
        gpr[pl.ds(rows0 + s * SUB, SUB), :] = (2.0 * jnp.maximum(hb[at, :], 0.0) * kb[at, :]).astype(BF16)
    spread(pq, SEG, nt(gpr[rows, :], wfk[...]))

    @pl.when(i == T // BLK - 1)
    def _():
        for c in range(D // 256):
            cols = pl.ds(c * 256, 256)
            grads[:D, cols] = tn(cks[...], gpr[:, cols])
            grads[D:, cols] = tn(hid[...], gch[:, cols])


def front(half, sizes, x, adj, vecs, mats):
    steps = T // BLK
    blk = lambda w: pl.BlockSpec((BLK, w), lambda i, h: (i, 0))
    own = lambda w: pl.BlockSpec((BLK, w), lambda i, h: (jnp.where(i // PER == h[0], lax.rem(i, PER), PER), 0))
    vec = pl.BlockSpec((D,), lambda i, h: (0,))
    mat = pl.BlockSpec((D, D), lambda i, h: (0, 0), pipeline_mode=pl.Buffered(1))
    sds = jax.ShapeDtypeStruct
    vm = pltpu.VMEM
    return pl.pallas_call(
        front_kernel,
        grid_spec=pltpu.PrefetchScalarGridSpec(
            num_scalar_prefetch=1,
            grid=(steps,),
            in_specs=[pl.BlockSpec(memory_space=pltpu.SMEM), blk(D), blk(D)] + [vec] * 11 + [mat] * 7,
            out_specs=[pl.BlockSpec(memory_space=pltpu.SMEM), pl.BlockSpec((2 * BLK, D), lambda i, h: (i, 0)),
                       pl.BlockSpec((2 * D, D), lambda i, h: (0, 0), pipeline_mode=pl.Buffered(1))]
            + [own(D)] * 13 + [own(128)] * 2 + [own(D)] * 5,
            scratch_shapes=[vm((SEG, D), F32)] * 2 + [vm((1, D), F32)] * 6 + [vm((BLK, D), F32)] * 4
            + [vm((T, D), BF16)] * 4 + [vm((16, D), F32)],
        ),
        out_shape=[sds((2, NSEG), F32), sds((2 * T, D), F32), sds((2 * D, D), F32)]
        + [sds((HALF + BLK, D), F32)] * 13 + [sds((HALF + BLK, 128), F32)] * 2 + [sds((HALF + BLK, D), BF16)] * 5,
        compiler_params=pltpu.CompilerParams(dimension_semantics=("arbitrary",), vmem_limit_bytes=60 * 2**20),
        cost_estimate=pl.CostEstimate(flops=11 * 2 * T * D * D, bytes_accessed=60 * 2**20, transcendentals=4 * T * D),
        name="front",
    )(half, sizes, x, adj, *vecs, *mats)


MESH = pl.DeviceIdType.MESH
COPIES = 256
FF_ROWS = 2 * D
R_ROWS = 2048
MATS = 5
BACK_VMEM = 39
FINISH_VMEM = 2
SETTLE = 24
ORDER = (
    "bBcaBBBMbcBdaMdBcbcBabBMMdMMbcdaMMdbacMOMMMMMpOM",
    "qMMOMMrqMtsMrMqaOsrpbtqMdMsrtMMGOqrGVspOOrtpqtGa",
    "psqVtGpsGtrVdpGOGsacqGGbrtpVOdsc",
)
NVEC = 11


def rows(start, size):
    return pl.ds(pl.multiple_of(start, 8), size)


def each(count, step, body, reverse=False):
    def run(k, carry):
        body((count - 1 - k) * step if reverse else k * step)
        return carry

    lax.fori_loop(0, count, run, 0)


class Links:
    def __init__(self, sends, recvs):
        self.sends, self.recvs, self.used, self.open, self.step = sends, recvs, 0, [], 0

    def send(self, src, dst, device):
        k = self.used
        self.used += 1
        copy = pltpu.make_async_remote_copy(
            src_ref=src, dst_ref=dst, send_sem=self.sends.at[k], recv_sem=self.recvs.at[k],
            device_id=device, device_id_type=MESH,
        )
        copy.start()
        self.open.append((self.step, copy))
        return copy

    def sent(self, copy):
        if all(kept[1] is not copy for kept in self.open):
            return
        self.open = [kept for kept in self.open if kept[1] is not copy]
        copy.wait_send()

    def settle(self, steps):
        while self.open and self.open[0][0] < self.step - steps:
            self.open.pop(0)[1].wait_send()
        self.step += 1

    def finish(self):
        for _, copy in self.open:
            copy.wait_send()


def add_into(dst, dst_at, terms, size, step=16):
    if size % step:
        step = 8

    def body(r):
        total = dst[rows(dst_at + r, step), :]
        for ref, start in terms:
            total = total + ref[rows(start + r, step), :]
        dst[rows(dst_at + r, step), :] = total

    each(size // step, step, body)


def ring_reduce(links, data, base, size, place, up, down, land, land_at, source, loaded):
    s = size // 4
    qa = (s // 2 + 7) // 8 * 8
    qb = s - qa
    mine = base + place * s
    nxt = base + lax.rem(place + 1, 4) * s
    opp = base + lax.rem(place + 2, 4) * s
    prv = base + lax.rem(place + 3, 4) * s
    starts = [land_at]
    for size_k in (qa, qb, qb, qa, qa, qb):
        starts.append(starts[-1] + size_k)
    spot = [land.at[pl.ds(a, b - a), :] for a, b in zip(starts, starts[1:])]
    fwd_a = links.send(source.at[rows(opp, qa), :], spot[0], up)
    fwd_b = links.send(source.at[rows(opp + qa, qb), :], spot[1], down)
    dir_b = links.send(source.at[rows(nxt + qa, qb), :], spot[2], up)
    dir_a = links.send(source.at[rows(prv, qa), :], spot[3], down)
    yield
    if loaded is not None:
        loaded()
    fwd_a.wait_recv()
    add_into(land, starts[0], [(data, nxt)], qa)
    cmb_a = links.send(spot[0], spot[4], up)
    fwd_b.wait_recv()
    add_into(land, starts[1], [(data, prv + qa)], qb)
    for copy in (fwd_a, fwd_b, dir_b, dir_a):
        links.sent(copy)
    cmb_b = links.send(spot[1], spot[5], down)
    yield
    dir_a.wait_recv()
    dir_b.wait_recv()
    cmb_a.wait_recv()
    cmb_b.wait_recv()
    add_into(data, mine, [(land, starts[3]), (land, starts[4])], qa)
    add_into(data, mine + qa, [(land, starts[2]), (land, starts[5])], qb)


def ring_gather(links, data, base, size, place, up, down, share):
    s = size // 4
    qa = (s // 2 + 7) // 8 * 8
    qb = s - qa
    mine = base + place * s
    nxt = base + lax.rem(place + 1, 4) * s
    opp = base + lax.rem(place + 2, 4) * s
    prv = base + lax.rem(place + 3, 4) * s
    own = data.at[rows(mine, s), :]
    to_up = links.send(own, own, up)
    to_down = links.send(own, own, down)
    share(own)
    yield
    to_up.wait_recv()
    half_a = data.at[rows(prv, qa), :]
    on_a = links.send(half_a, half_a, up)
    to_down.wait_recv()
    half_b = data.at[rows(nxt + qa, qb), :]
    on_b = links.send(half_b, half_b, down)
    share(data.at[rows(prv, s), :])
    share(data.at[rows(nxt, s), :])
    yield
    on_a.wait_recv()
    on_b.wait_recv()
    share(data.at[rows(opp, s), :])


def near_reduce(links, data, base, size, place, others, land, land_at, stage_at):
    s = size // 4
    copies = []
    for k, device in enumerate(others):
        theirs = base + lax.rem(place + 1 + k, 4) * s
        stage = stage_at + k * s

        def body(r, theirs=theirs, stage=stage):
            land[rows(stage + r, 8), :] = data[rows(theirs + r, 8), :]

        each(s // 8, 8, body)
        copies.append(links.send(land.at[pl.ds(stage, s), :], land.at[pl.ds(land_at + k * s, s), :], device))
    yield
    for copy in copies:
        copy.wait_recv()
    add_into(data, base + place * s, [(land, land_at + k * s) for k in range(3)], s, 8)


def near_gather(links, data, base, size, place, others):
    s = size // 4
    own = data.at[rows(base + place * s, s), :]
    copies = [links.send(own, own, device) for device in others]
    yield
    for copy in copies:
        copy.wait_recv()


def sum_of_four(links, data, base, size, place, others, land, land_at):
    mine = rows(land_at + place * size, size)
    land[mine, :] = data[rows(base, size), :]
    copies = [links.send(land.at[mine, :], land.at[mine, :], device) for device in others]
    yield
    for copy in copies:
        copy.wait_recv()

    def body(r):
        a, b, c, d = (land[rows(land_at + k * size + r, 8), :] for k in range(4))
        data[rows(base + r, 8), :] = (a + b) + (c + d)

    each(size // 8, 8, body)


def all_reduce(links, data, base, size, axes, land, land_at, last, last_land, last_at, source, loaded, share):
    (place, up, _, down), (place_2, *others) = axes
    yield from ring_reduce(links, data, base, size, place, up, down, land, land_at, source, loaded)
    part = size // 4
    at = base + place * part
    yield from near_reduce(links, data, at, part, place_2, others, land, land_at + 3 * part, land_at + part)
    yield from last(links, data, at + place_2 * (part // 4), part // 4, last_land, last_at)
    yield from near_gather(links, data, at, part, place_2, others)
    yield from ring_gather(links, data, base, size, place, up, down, share)


def back_kernel(
    flags, pq, grads, n1_h, dh1_h, a_h, v_h, sr_h, w_h, rd_h, sn_h, sd_h, after_h, gate_h, n2_h, dh2_h,
    r1_h, r2_h, keyed_h, valued_h, recepted_h, mixed_h, chrec_h, adj_h,
    g1_h, fk_h, fv_h, fr_h, dec_h, rew_h, g2_h, ck_h, cr_h, wr_h, wk_h, wv_h, wo_h, wg_h,
    out_o, gi, vec_o, red, ff,
    front4, r1, r2, keyed, valued, recepted, mixed, chrec, adj, wr, wo, wg,
    fin, xb, gg, gb, gk, gv, gp, t0, t1, t2, other, ffland, yland, vland,
    urow, urow2, gsend, grecv, acc, rise, fade, through, expu, sums, gc, pv,
    sends, recvs, fill, ready_ring, ready_sib,
):
    dp = lax.axis_index("dp")
    tensor = lax.axis_index("tensor")
    x, z, yl = dp // 8, lax.rem(dp // 2, 4), lax.rem(dp, 2)
    h, c = tensor // 2, lax.rem(tensor, 2)
    y = 2 * h + yl

    def chip(cx, cz, cy):
        cx, cz, cy = lax.rem(cx + 4, 4), lax.rem(cz + 4, 4), lax.rem(cy + 4, 4)
        return {"dp": (cx * 4 + cz) * 2 + lax.rem(cy, 2), "tensor": (cy // 2) * 2 + c}

    xp, xo, xm = (chip(x + k, z, y) for k in (1, 2, 3))
    zp, zo, zm = (chip(x, z + k, y) for k in (1, 2, 3))
    yp, opp, ym = (chip(x, z, y + k) for k in (1, 2, 3))
    sib = {"dp": dp, "tensor": h * 2 + (1 - c)}
    pair = {"dp": dp + 1 - 2 * yl, "tensor": tensor}
    own_at, other_at = h * HALF, (1 - h) * HALF
    mine_at = c * R_ROWS

    given = (g1_h, fk_h, fv_h, fr_h, dec_h, rew_h, g2_h, ck_h, cr_h)
    g1, fk, fv, fr, dec, rew, g2, ck, cr = (pv.at[k : k + 1, :] for k in range(len(given)))
    barrier = pltpu.get_barrier_semaphore()
    partners = (xp, xo, xm, zp, zo, zm, yp, ym, opp, sib)
    for device in partners:
        pl.semaphore_signal(barrier, inc=1, device_id=device, device_id_type=MESH)

    fills = []

    def bring(src, dst):
        copy = pltpu.make_async_copy(src, dst, fill.at[len(fills)])
        copy.start()
        fills.append(copy)
        return copy

    def group(start):
        return rows(2 * start, 2 * SEG)

    PART, ARECV, CRECV, BRECV = (512 * k for k in range(4))
    part_in = [
        bring(pq.at[group(other_at + 128 * j + SEG * c), :], xb.at[pl.ds(PART + 128 * j, 128), :]) for j in range(4)
    ]
    ff_in = bring(grads, ff)
    fin_in = [
        bring(pq.at[group(own_at + 128 * j + SEG * c), :], fin.at[group(128 * j + SEG * c), :]) for j in range(4)
    ]
    pl.semaphore_wait(barrier, len(partners))

    links = Links(sends, recvs)
    ax, az, ay = (x, xp, xo, xm), (z, zp, zo, zm), (y, yp, opp, ym)

    def with_pair(links, data, base, size, land, land_at):
        whole = data.at[rows(base, size), :]
        copy = links.send(whole, land.at[pl.ds(land_at, size), :], pair)
        yield
        links.sent(copy)
        copy.wait_recv()
        add_into(data, base, [(land, land_at)], size, 8)

    def with_ring(axis):
        def last(links, data, base, size, land, land_at):
            yield from sum_of_four(links, data, base, size, axis[0], axis[1:], land, land_at)

        return last

    waited = []

    def ff_loaded():
        if not waited:
            ff_in.wait()
            waited.append(True)

    n = FF_ROWS // 4
    ffs = [
        all_reduce(
            links, ff, n * k, n, (ax, az) if k % 2 == 0 else (az, ax), ffland, n * k,
            with_pair, ffland, n * k + 15 * n // 16, grads, ff_loaded, lambda ref: None,
        )
        for k in range(4)
    ]

    a_in = [
        links.send(pq.at[group(other_at + 128 * j + SEG * (1 - c)), :], xb.at[pl.ds(ARECV + 128 * j, 128), :], sib)
        for j in range(4)
    ]
    c_in = [
        links.send(pq.at[group(own_at + 128 * j + SEG * (1 - c)), :], xb.at[pl.ds(CRECV + 128 * j, 128), :], sib)
        for j in range(4)
    ]
    half = pl.ds(0, HALF)
    AFTER, GATE, N2, DH2 = (HALF * k for k in range(4))
    SR, W, RD, A, V, SN, SD = (lax.rem(mine_at + HALF * k, 2 * R_ROWS) for k in range(1, 8))
    first_in = [
        bring(s.at[half, :], front4.at[pl.ds(HALF * k, HALF), :]) for k, s in enumerate((after_h, gate_h, n2_h, dh2_h))
    ]
    first_in += [bring(adj_h.at[rows(own_at, HALF), :], adj), bring(wg_h, wg), bring(r2_h.at[half, :], r2)]
    first_in += [bring(wo_h, wo)]
    second_in = [
        bring(s.at[half, :], red.at[rows(spot, HALF), :])
        for s, spot in ((a_h, A), (v_h, V), (sr_h, SR), (w_h, W), (rd_h, RD), (sn_h, SN), (sd_h, SD))
    ]
    lanes = pl.ds(pl.multiple_of(c * HALF_D, 128), HALF_D)
    third_in = [
        bring(s.at[half, lanes], d)
        for s, d in (
            (mixed_h, mixed), (chrec_h, chrec), (keyed_h, keyed), (valued_h, valued), (recepted_h, recepted),
        )
    ]
    third_in += [bring(r1_h.at[half, :], r1), bring(wr_h, wr)]
    b_in = []

    def other_half():
        for j in range(4):
            part_in[j].wait()
            a_in[j].wait_recv()
            for at in (128 * j, 128 * j + SEG):
                add_into(xb, PART + at, [(xb, ARECV + at)], SEG)
                b_in.append(links.send(xb.at[pl.ds(PART + at, SEG), :], xb.at[pl.ds(BRECV + at, SEG), :], opp))
                yield

    seg0 = h * (HALF // SEG)
    not_last = (1 - h).astype(F32)

    def fold(v):
        return jnp.sum(v.reshape(-1, 8, D), axis=0)

    def tally(k, v):
        acc[pl.ds(8 * k, 8), :] += fold(v)

    GAIN1, BIAS1, MIXK, MIXV, MIXR, LOGD, REW, GAIN2, BIAS2, CMIXK, CMIXR = range(NVEC)

    def take(j):
        fin_in[j].wait()
        c_in[j].wait_recv()
        b_in[2 * j].wait_recv()
        b_in[2 * j + 1].wait_recv()
        add_into(fin, 2 * (128 * j + SEG * c), [(xb, CRECV + 128 * j), (xb, BRECV + 128 * j)], 128)
        mine = fin.at[group(128 * j + SEG * c), :]
        links.sent(b_in[2 * j])
        links.sent(b_in[2 * j + 1])
        return links.send(mine, mine, sib)

    def gate_part(j):
        lo = 128 * j
        for seg in range(2):
            live = flags[1, seg0 + 2 * j + seg]

            def body(r, seg=seg, live=live):
                at = lo + SEG * seg + r
                gate = front4[rows(GATE + at, SUB), :]
                co = fin[rows(2 * (lo + SEG * seg) + r, SUB), :]
                res = live * (front4[rows(AFTER + at, SUB), :] + gate * co)
                front4[rows(AFTER + at, SUB), :] = res.astype(BF16).astype(F32)
                go = adj[rows(at, SUB), :].astype(F32) * live
                gg[rows(at, SUB), :] = (go * co * gate * (1.0 - gate)).astype(BF16)

            each(SEG // SUB, SUB, body)
        t0[...] = nt(gg[pl.ds(lo, 128), :], wg[...])
        for seg in range(2):

            def body2(r, seg=seg):
                at = 2 * (lo + SEG * seg) + r
                qk = fin[rows(at + SEG, SUB), :]
                qr = t0[rows(SEG * seg + r, SUB), :]
                dh2 = front4[rows(DH2 + lo + SEG * seg + r, SUB), :]
                tally(CMIXK, qk * dh2)
                tally(CMIXR, qr * dh2)
                base = qk * ck[...] + qr * cr[...]
                fin[rows(at, SUB), :] = base
                fin[rows(at + SEG, SUB), :] = (qk + qr) - base

            each(SEG // SUB, SUB, body2)

    def lifted(nxt, u):
        row = lax.broadcasted_iota(jnp.int32, u.shape, 0)
        return jnp.where(row == u.shape[0] - 1, nxt, pltpu.roll(u, u.shape[0] - 1, 0))

    def norm_back(e, n, r, gain):
        f = e * gain
        return r * (f - jnp.mean(f, axis=-1, keepdims=True) - n * jnp.mean(f * n, axis=-1, keepdims=True))

    def keep_next(seg):
        return 1.0 - flags[0, jnp.minimum(seg0 + seg + 1, NSEG - 1)]

    def walk_rows(j, edge_row, sub_body):
        for seg in (1, 0):
            s = 2 * j + seg
            live = flags[1, seg0 + s]
            for k in reversed(range(SEG // SUB)):
                lo = SEG * s + SUB * k
                at = 2 * SEG * s + SUB * k
                if lo + SUB == HALF:
                    nxt = edge_row[0:1, :] * (not_last * keep_next(s))
                elif k == SEG // SUB - 1:
                    nxt = fin[2 * SEG * (s + 1) + SEG : 2 * SEG * (s + 1) + SEG + 1, :] * keep_next(s)
                else:
                    nxt = fin[at + SEG + SUB : at + SEG + SUB + 1, :]
                sub_body(lo, at, live, nxt)

    def after_rows(lo, at, live, nxt):
        e = fin[pl.ds(at, SUB), :] + lifted(nxt, fin[pl.ds(at + SEG, SUB), :])
        n = front4[pl.ds(N2 + lo, SUB), :]
        tally(GAIN2, e * n)
        tally(BIAS2, e)
        go = adj[pl.ds(lo, SUB), :].astype(F32) * live
        ga = go + norm_back(e, n, r2[pl.ds(lo, SUB), 0:1], g2[...])
        front4[pl.ds(N2 + lo, SUB), :] = ga
        gb[pl.ds(lo, SUB), :] = ga.astype(BF16)

    def mixed_chunk(j):
        t0[...] = nt(gb[pl.ds(128 * j, 128), :], wo[...])
        for seg in (1, 0):
            total = 16 * (2 * j + seg)
            sums[pl.ds(total, 16), :] = jnp.zeros((16, D), F32)

            def body(r, seg=seg, total=total):
                at = 128 * j + SEG * seg + r
                gm = t0[rows(SEG * seg + r, SUB), :]
                sr = red[rows(SR + at, SUB), :]
                w = red[rows(W + at, SUB), :]
                gw = gm * sr
                q = gw * red[rows(RD + at, SUB), :]
                red[rows(RD + at, SUB), :] = q
                gp[rows(at, SUB), :] = (gw * w * (1.0 - sr)).astype(BF16)
                fq = fade[rows(r, SUB), :] * q
                sums[pl.ds(total, 8), :] += fold(fq)
                sums[pl.ds(total + 8, 8), :] += fold(fq * w)

            each(SEG // SUB, SUB, body)

    def chain():
        first = jnp.zeros((1, D), F32)
        second = jnp.zeros((1, D), F32)
        th = through[...]
        for s in reversed(range(8)):
            q = jnp.sum(sums[pl.ds(16 * s, 8), :], axis=0, keepdims=True)
            qw = jnp.sum(sums[pl.ds(16 * s + 8, 8), :], axis=0, keepdims=True)
            if s < 7:
                q = q + th * (first * keep_next(s))
                qw = qw + th * (second * keep_next(s))
            first, second = q, qw
        sums[0:1, :] = first
        sums[1:2, :] = second

    tri = triangle(True)

    def key_value(k, carry):
        s = 7 - k
        lo = SEG * s
        keep = 1.0 - flags[0, seg0 + s]
        for col in range(D // 128):
            cols = pl.ds(col * 128, 128)
            at = rows(lo, SEG)
            q = red[rows(RD + lo, SEG), cols]
            w = red[rows(W + lo, SEG), cols]
            a = red[rows(A + lo, SEG), cols]
            v = red[rows(V + lo, SEG), cols]
            fq = fade[:, cols] * q
            cum, both = running(tri, fq, fq * w)
            cn = through[:, cols] * gc[0:1, cols]
            cd = through[:, cols] * gc[1:2, cols]
            gn = rise[:, cols] * (cum[:, :128] + cn)
            gd = rise[:, cols] * (cum[:, 128:] + cd)
            gc[0:1, cols] = (both[0:1, :128] + cum[0:1, :128] + cn) * keep
            gc[1:2, cols] = (both[0:1, 128:] + cum[0:1, 128:] + cd) * keep
            eq = expu[:, cols] * a * q
            gvv = a * gn + eq
            gv[at, cols] = gvv.astype(BF16)
            gk[at, cols] = (v * gvv - (a * gd + eq * w)).astype(BF16)
            up = eq * (v - w)
            down = gn * red[rows(SN + lo, SEG), cols] - gd * red[rows(SD + lo, SEG), cols]
            acc[pl.ds(8 * REW, 8), cols] += jnp.sum(up.reshape(-1, 8, 128), axis=0)
            acc[pl.ds(8 * LOGD, 8), cols] += jnp.sum(down.reshape(-1, 8, 128), axis=0)
        return carry

    def weights(k, left, right):
        for col in range(D // 256):
            cols = pl.ds(256 * col, 256)
            red[rows(mine_at + HALF_D * k, HALF_D), cols] = tn(left[...], right[:, cols])

    shared = []

    def share(ref):
        if not shared:
            pl.semaphore_wait(ready_sib, 1)
        shared.append(links.send(ref, ref, sib))

    orders = ((ax, az, ay), (az, ax, ay), (ax, az, ay), (az, ax, ay), (ay, ax, az))

    def reduce_weights(k):
        if k == 0:
            pl.semaphore_wait(ready_ring, 6)
        first, second, third = orders[k]
        yield from all_reduce(
            links, red, mine_at + HALF_D * k, HALF_D, (first, second), xb, HALF_D * k,
            with_ring(third), yland, HALF_D // 4 * k, red, None, share,
        )

    def front_chunk(j):
        at0 = pl.ds(128 * j, 128)
        t0[...] = nt(gk[at0, :], wk[...])
        t1[...] = nt(gv[at0, :], wv[...])
        t2[...] = nt(gp[at0, :], wr[...])
        for seg in range(2):

            def body(r, seg=seg):
                lo = 128 * j + SEG * seg
                pk, pv_, pr = (t[rows(SEG * seg + r, SUB), :] for t in (t0, t1, t2))
                dh1 = front4[rows(DH2 + lo + r, SUB), :]
                tally(MIXK, pk * dh1)
                tally(MIXV, pv_ * dh1)
                tally(MIXR, pr * dh1)
                base = pk * fk[...] + pv_ * fv[...] + pr * fr[...]
                fin[rows(2 * lo + r, SUB), :] = base
                fin[rows(2 * lo + SEG + r, SUB), :] = (pk + pv_ + pr) - base

            each(SEG // SUB, SUB, body)

    def input_rows(lo, at, live, nxt):
        e = fin[pl.ds(at, SUB), :] + lifted(nxt, fin[pl.ds(at + SEG, SUB), :])
        n = front4[pl.ds(GATE + lo, SUB), :]
        tally(GAIN1, e * n)
        tally(BIAS1, e)
        gi[rows(own_at + lo, SUB), :] = front4[pl.ds(N2 + lo, SUB), :] + norm_back(e, n, r1[pl.ds(lo, SUB), 0:1], g1[...])

    def vector_sums():
        scale = -jnp.exp(dec[...]) * jnp.exp(-jnp.exp(dec[...]))
        vec_o[...] = jnp.zeros_like(vec_o)
        for k in range(NVEC):
            total = jnp.sum(acc[pl.ds(8 * k, 8), :], axis=0, keepdims=True)
            vec_o[k : k + 1, :] = total * scale if k == LOGD else total

    def cast_rows(r):
        out_o[rows(own_at + r, SUB), :] = front4[rows(AFTER + r, SUB), :].astype(BF16)
        out_o[rows(other_at + r, SUB), :] = other[rows(r, SUB), :].astype(BF16)

    wk, wv = wg, wo

    def compute():
        for k, v in enumerate(given):
            pv[k : k + 1, :] = v[...].reshape(1, D)
        through[...] = decay_tables(dec[...], rise, fade)
        expu[...] = jnp.exp(rew[...])
        acc[...] = jnp.zeros_like(acc)
        for copy in first_in:
            copy.wait()
        yield
        for j in range(4):
            e_in = take(j)
            if j == 3:
                for device in (xp, xm, zp, zm, yp, ym):
                    pl.semaphore_signal(ready_ring, inc=1, device_id=device, device_id_type=MESH)
            yield
            e_in.wait_recv()
            links.sent(e_in)
            gate_part(j)
            if j == 0:
                gsend[...] = fin[SEG : SEG + 8, :]
                u_in = links.send(gsend, urow, opp)
            yield
        wk_in = bring(wk_h, wk)
        u_in.wait_recv()
        for copy in second_in:
            copy.wait()
        for j in reversed(range(4)):
            walk_rows(j, urow, after_rows)
            mixed_chunk(j)
            if j > 0:
                yield
        chain()
        g_in = links.send(sums.at[pl.ds(0, 8), :], grecv, opp)
        late = [wk_in, bring(wv_h, wv), bring(n1_h.at[half, :], front4.at[pl.ds(GATE, HALF), :])]
        late.append(bring(dh1_h.at[half, :], front4.at[pl.ds(DH2, HALF), :]))
        yield
        for copy in third_in:
            copy.wait()
        weights(0, mixed, gb)
        yield
        weights(1, chrec, gg)
        yield
        g_in.wait_recv()
        edge = not_last * keep_next(7)
        gc[0:1, :] = grecv[0:1, :] * edge
        gc[1:2, :] = grecv[1:2, :] * edge
        lax.fori_loop(0, 4, key_value, 0)
        yield
        lax.fori_loop(4, 8, key_value, 0)
        pl.semaphore_signal(ready_sib, inc=1, device_id=sib, device_id_type=MESH)
        yield
        weights(2, recepted, gp)
        yield
        weights(3, keyed, gk)
        yield
        weights(4, valued, gv)
        yield
        for copy in late:
            copy.wait()
        for j in range(4):
            front_chunk(j)
            if j == 0:
                u2_in = links.send(fin.at[pl.ds(SEG, 8), :], urow2, opp)
            yield
        u2_in.wait_recv()
        for j in reversed(range(4)):
            walk_rows(j, urow2, input_rows)
            if j == 2:
                yield
        vector_sums()

    def vectors():
        for k, (place, others) in enumerate(((x, (xp, xo, xm)), (z, (zp, zo, zm)), (y, (yp, opp, ym)))):
            yield from sum_of_four(links, vec_o, 0, 16, place, others, vland, 64 * k)

    def swap(src, src_at, dst, dst_at, back_at):
        there = []
        for k in range(4):
            there.append(
                links.send(src.at[rows(src_at + SEG * k, SEG), :], dst.at[rows(dst_at + SEG * k, SEG), :], opp)
            )
            yield
        onward = []
        for k in range(4):
            there[k].wait_recv()
            theirs = dst.at[rows(back_at + SEG * k, SEG), :]
            onward.append(links.send(theirs, theirs, sib))
            yield
        for copy in onward:
            copy.wait_recv()

    def result():
        yield from swap(front4, AFTER + 256 * c, other, 256 * c, 256 * c)
        each(HALF // SUB, SUB, cast_rows)

    def input_grads():
        yield from swap(gi, own_at + 256 * c, gi, own_at + 256 * c, other_at + 256 * c)

    jobs = dict(zip("abcd", ffs))
    jobs.update(zip("pqrst", (reduce_weights(k) for k in range(MATS))))
    jobs.update(M=compute(), B=other_half(), V=vectors(), O=result(), G=input_grads())
    for name in "".join(ORDER):
        next(jobs[name], None)
        links.settle(SETTLE)
    for copy in shared:
        copy.wait_recv()
    links.finish()


def back(front_outs, adj, vecs, mats):
    g1, b1, fk, fv, fr, dec, rew, g2, b2, ck, cr = vecs
    flags, rest = front_outs[0], front_outs[1:]
    vm = pltpu.VMEM
    anywhere = pl.BlockSpec(memory_space=pl.ANY)
    vmem = pl.BlockSpec(memory_space=pltpu.VMEM)
    half = lambda dt: vm((HALF, D), dt)
    return pl.pallas_call(
        back_kernel,
        in_specs=[pl.BlockSpec(memory_space=pltpu.SMEM)] + [anywhere] * len(rest) + [anywhere]
        + [vmem] * 9 + [anywhere] * 5,
        out_specs=[vmem] * 5,
        out_shape=[vm((T, D), BF16), vm((T, D), F32), vm((16, D), F32), vm((2 * R_ROWS, D), F32), vm((FF_ROWS, D), F32)],
        scratch_shapes=[vm((4 * HALF, D), F32), vm((HALF, 128), F32), vm((HALF, 128), F32)]
        + [vm((HALF, HALF_D), BF16)] * 5 + [half(BF16)] + [vm((D, D), BF16)] * 3
        + [vm((2 * HALF, D), F32), vm((R_ROWS, D), F32)]
        + [half(BF16)] * 5 + [vm((128, D), F32)] * 3 + [half(F32)]
        + [vm((FF_ROWS, D), F32), vm((R_ROWS // 4, D), F32), vm((192, D), F32)]
        + [vm((8, D), F32)] * 4 + [vm((8 * NVEC, D), F32)] + [vm((SEG, D), F32)] * 2
        + [vm((1, D), F32)] * 2 + [vm((128, D), F32), vm((8, D), F32), vm((16, D), F32)]
        + [pltpu.SemaphoreType.DMA((COPIES,)), pltpu.SemaphoreType.DMA((COPIES,)),
           pltpu.SemaphoreType.DMA((48,)), pltpu.SemaphoreType.REGULAR, pltpu.SemaphoreType.REGULAR],
        compiler_params=pltpu.CompilerParams(collective_id=1, has_side_effects=True, vmem_limit_bytes=BACK_VMEM * 2**20),
        cost_estimate=pl.CostEstimate(flops=14 * T * D * D, bytes_accessed=60 * 2**20, transcendentals=0),
        name="back",
    )(flags, *rest, adj, g1, fk, fv, fr, dec, rew, g2, ck, cr, *mats[:5])


def finish_kernel(out, gi, vec, red, ff, *refs):
    out_o, gi_o, mats, ck_o, cv_o, vecs, sems = refs[0], refs[1], refs[2:7], refs[7], refs[8], refs[9:20], refs[20]
    pairs = [(gi, gi_o), (ff.at[pl.ds(0, D), :], ck_o), (ff.at[pl.ds(D, D), :], cv_o), (out, out_o)]
    for k in range(MATS):
        for core in range(2):
            src = red.at[pl.ds(core * R_ROWS + HALF_D * k, HALF_D), :]
            pairs.append((src, mats[(3, 4, 0, 1, 2)[k]].at[pl.ds(HALF_D * core, HALF_D), :]))
    copies = [pltpu.make_async_copy(src, dst, sems.at[k]) for k, (src, dst) in enumerate(pairs)]
    for copy in copies:
        copy.start()
    for k in range(NVEC):
        vecs[k][...] = vec[k : k + 1, :].reshape(D)
    for copy in copies:
        copy.wait()


def finish(out, gi, vec, red, ff):
    sds = jax.ShapeDtypeStruct
    anywhere = pl.BlockSpec(memory_space=pl.ANY)
    vmem = pl.BlockSpec(memory_space=pltpu.VMEM)
    return pl.pallas_call(
        finish_kernel,
        in_specs=[vmem] * 5,
        out_specs=[anywhere] * 9 + [vmem] * NVEC,
        out_shape=[sds((T, D), BF16), sds((T, D), F32)] + [sds((D, D), F32)] * 7 + [sds((D,), F32)] * NVEC,
        scratch_shapes=[pltpu.SemaphoreType.DMA((16,))],
        compiler_params=pltpu.CompilerParams(vmem_limit_bytes=FINISH_VMEM * 2**20),
        name="finish",
    )(out, gi, vec, red, ff)


def body(
    entering_activations, sample_sizes, initial_layernorm_scale, initial_layernorm_offset, temporal_lookup_fraction,
    temporal_content_fraction, temporal_gating_fraction, fading_speed_logarithm, present_reward,
    temporal_gating_matrix, temporal_lookup_matrix, temporal_content_matrix, temporal_emission_matrix,
    latter_layernorm_scale, latter_layernorm_offset, feedforward_lookup_fraction, feedforward_gating_fraction,
    feedforward_gating_matrix, feedforward_lookup_matrix, feedforward_content_matrix, upstream_adjoint,
):
    vecs = (
        initial_layernorm_scale, initial_layernorm_offset, temporal_lookup_fraction, temporal_content_fraction,
        temporal_gating_fraction, fading_speed_logarithm, present_reward, latter_layernorm_scale,
        latter_layernorm_offset, feedforward_lookup_fraction, feedforward_gating_fraction,
    )
    mats = (
        temporal_gating_matrix, temporal_lookup_matrix, temporal_content_matrix, temporal_emission_matrix,
        feedforward_gating_matrix, feedforward_lookup_matrix, feedforward_content_matrix,
    )
    half = (lax.axis_index("tensor") // 2).astype(jnp.int32).reshape(1)
    fronts = front(half, sample_sizes, entering_activations, upstream_adjoint, vecs, mats)
    out, grad_inputs, recw, keyw, valw, outw, chrec, chkey, chval, *g = finish(*back(fronts, upstream_adjoint, vecs, mats))
    return (
        out, grad_inputs, g[0], g[1], g[2], g[3], g[4], g[5], g[6], recw, keyw, valw, outw,
        g[7], g[8], g[9], g[10], chrec, chkey, chval,
    )


def solution(mesh):
    split = P("dp", None)
    in_specs = (split, split) + (P(),) * 16 + (P(None, "tensor"), P("tensor", None), split)
    out_specs = (split, split) + (P(),) * 16 + (P(None, "tensor"), P("tensor", None))
    return jax.shard_map(body, mesh=mesh, in_specs=in_specs, out_specs=out_specs, check_vma=False)
```

```python
import functools

import jax
import jax.numpy as jnp
from jax import lax
from jax.experimental import pallas as pl
from jax.experimental.pallas import tpu as pltpu
from jax.sharding import PartitionSpec as P

F32 = jnp.float32
BF16 = jnp.bfloat16
EPSILON = 1e-05
SEG = 64
D = 768
T = 1024
HALF = 512
HALF_D = D // 2
BLK = 512
SUB = 32
NSEG = T // SEG
PER = HALF // BLK
SLOTS = PER


def nn(left, right):
    return jnp.dot(left, right, preferred_element_type=F32)


def nt(left, right):
    return lax.dot_general(left, right, (((1,), (1,)), ((), ())), preferred_element_type=F32)


def tn(left, right):
    return lax.dot_general(left, right, (((0,), (0,)), ((), ())), preferred_element_type=F32)


def normalize(v):
    c = v - jnp.mean(v, axis=-1, keepdims=True)
    r = lax.rsqrt(jnp.mean(c * c, axis=-1, keepdims=True) + EPSILON)
    return c * r, r


def roll_down(v, first):
    row = lax.broadcasted_iota(jnp.int32, v.shape, 0)
    return jnp.where(row == 0, first, pltpu.roll(v, 1, 0))


def two_parts(v):
    hi = v.astype(BF16)
    return hi, (v - hi.astype(F32)).astype(BF16)


def triangle(upper):
    row = lax.broadcasted_iota(jnp.int32, (SEG, 2 * SEG), 0)
    col = lax.broadcasted_iota(jnp.int32, (SEG, 2 * SEG), 1)
    col = jnp.where(col >= SEG, col - SEG, col)
    keep = (col > row) if upper else (col < row)
    return jnp.where(keep, 1.0, 0.0).astype(BF16)


def running(tri, first, second):
    both = jnp.concatenate([first, second], axis=1)
    hi, lo = two_parts(both)
    return nn(tri, jnp.concatenate([hi, lo], axis=0)), both


def decay_tables(dec, rise, fade):
    rate = jnp.exp(dec)
    offs = lax.broadcasted_iota(jnp.int32, (SEG, D), 0).astype(F32)
    rise[...] = jnp.exp((offs + 1.0) * rate)
    fade[...] = jnp.exp(-offs * rate)
    return jnp.exp(-float(SEG) * rate)


def spread(dst, first, v):
    for s in range(v.shape[0] // SEG):
        dst[2 * SEG * s + first : 2 * SEG * s + first + SEG, :] = v[SEG * s : SEG * (s + 1), :]


def front_kernel(
    half_ref, len_ref, x_ref, adj_ref, g1_h, b1_h, fk_h, fv_h, fr_h, dec_h, rew_h, g2_h, b2_h, ck_h, cr_h,
    wr_h, wk_h, wv_h, wo_h, wg_h, wfk_h, wfv_h,
    flags, pq, grads, n1_h, dh1_h, a_h, v_h, sr_h, w_h, rd_h, sn_h, sd_h, after_h, gate_h, n2_h, dh2_h,
    r1_h, r2_h, keyed_h, valued_h, recepted_h, mixed_h, chrec_h,
    wr, wk, wv, wo, wg, wfk, wfv, wide, narrow, low, gbuf,
    rise, fade, through, expu, nc, dc, p1, p2, kb, vb, rb, hb, cks, hid, gch, gpr, pv, win, outs, gsem,
):
    i = pl.program_id(0)
    slot = lax.rem(i, SLOTS)
    given = (g1_h, b1_h, fk_h, fv_h, fr_h, dec_h, rew_h, g2_h, b2_h, ck_h, cr_h)
    g1, b1, fk, fv, fr, dec, rew, g2, b2, ck, cr = (pv.at[k : k + 1, :] for k in range(len(given)))
    n1_o, dh1_o, a_o, v_o, sr_o, w_o, rd_o, sn_o, sd_o, after_o, gate_o, n2_o, dh2_o = (
        wide.at[slot, k] for k in range(13)
    )
    r1_o, r2_o = (narrow.at[slot, k] for k in range(2))
    keyed_o, valued_o, recepted_o, mixed_o, chrec_o = (low.at[slot, k] for k in range(5))
    loads = [
        pltpu.make_async_copy(src, dst, win.at[k])
        for k, (src, dst) in enumerate(
            ((wk_h, wk), (wv_h, wv), (wr_h, wr), (wo_h, wo), (wfk_h, wfk), (wg_h, wg), (wfv_h, wfv))
        )
    ]
    kept = pl.ds(pl.multiple_of(lax.rem(i, PER) * BLK, BLK), BLK)
    held = (
        (wide, 0, n1_h), (wide, 1, dh1_h), (narrow, 0, r1_h), (low, 0, keyed_h), (low, 1, valued_h), (low, 2, recepted_h),
        (wide, 2, a_h), (wide, 3, v_h), (wide, 4, sr_h), (wide, 5, w_h), (wide, 6, rd_h), (wide, 7, sn_h),
        (wide, 8, sd_h), (low, 3, mixed_h),
        (wide, 9, after_h), (wide, 11, n2_h), (wide, 12, dh2_h), (narrow, 1, r2_h), (low, 4, chrec_h),
        (wide, 10, gate_h),
    )

    def saves(at):
        return [
            pltpu.make_async_copy(src.at[at, n], dst.at[kept, :], outs.at[at, k])
            for k, (src, n, dst) in enumerate(held)
        ]

    def save(lo, hi):
        @pl.when(i // PER == half_ref[0])
        def _():
            for copy in saves(slot)[lo:hi]:
                copy.start()

    def loaded(lo, hi):
        @pl.when(i == 0)
        def _():
            for copy in loads[lo:hi]:
                copy.wait()

    @pl.when(i == 0)
    def _():
        for copy in loads:
            copy.start()

    def reuse(lo, hi):
        @pl.when((i >= PER) & (half_ref[0] == 0))
        def _():
            for copy in saves(slot)[lo:hi]:
                copy.wait()

    reuse(0, 6)
    @pl.when(i == 0)
    def _():
        for b in range(NSEG):
            flags[0, b] = 0.0
        begin = jnp.int32(0)
        for j in range(NSEG):
            size = len_ref[0, j]
            at = lax.shift_right_logical(begin, 6)

            @pl.when(size > 0)
            def _():
                flags[0, at] = 1.0

            begin = begin + size
        for b in range(NSEG):
            flags[1, b] = jnp.where(b * SEG < begin, 1.0, 0.0)
        for k, v in enumerate(given):
            pv[k : k + 1, :] = v[...].reshape(1, D)
        through[...] = decay_tables(dec[...], rise, fade)
        expu[...] = jnp.exp(rew[...])
        nc[...] = jnp.zeros_like(nc)
        dc[...] = jnp.zeros_like(dc)
        p1[...] = jnp.zeros_like(p1)
        p2[...] = jnp.zeros_like(p2)

    fresh = [flags[0, i * (BLK // SEG) + s] for s in range(BLK // SEG)]
    live = [flags[1, i * (BLK // SEG) + s] for s in range(BLK // SEG)]

    for s in range(BLK // SUB):
        at = pl.ds(s * SUB, SUB)
        n1, r1 = normalize(x_ref[at, :].astype(F32))
        h1 = n1 * g1[...] + b1[...]
        before = p1[...]
        if (s * SUB) % SEG == 0:
            before = before * (1.0 - fresh[s * SUB // SEG])
        sh = roll_down(h1, before)
        p1[...] = h1[SUB - 1 :, :]
        dh1 = h1 - sh
        keyed_o[at, :] = (sh + dh1 * fk[...]).astype(BF16)
        valued_o[at, :] = (sh + dh1 * fv[...]).astype(BF16)
        recepted_o[at, :] = (sh + dh1 * fr[...]).astype(BF16)
        n1_o[at, :] = n1
        dh1_o[at, :] = dh1
        r1_o[at, :] = jnp.broadcast_to(r1, (SUB, 128))

    save(0, 6)
    reuse(6, 14)
    loaded(0, 3)
    kb[...] = nn(keyed_o[...], wk[...])
    vb[...] = nn(valued_o[...], wv[...])
    rb[...] = nn(recepted_o[...], wr[...])

    tri = triangle(False)
    for s in range(BLK // SEG):
        at = pl.ds(s * SEG, SEG)
        keep = 1.0 - fresh[s]
        for c in range(D // 128):
            cols = pl.ds(c * 128, 128)
            a = jnp.exp(kb[at, cols])
            v = vb[at, cols]
            lift = rise[:, cols] * a
            cum, both = running(tri, lift * v, lift)
            ncar = nc[:, cols] * keep
            dcar = dc[:, cols] * keep
            sn = fade[:, cols] * (ncar + cum[:, :128])
            sd = fade[:, cols] * (dcar + cum[:, 128:])
            th = through[:, cols]
            nc[:, cols] = th * (ncar + (cum[SEG - 1 :, :128] + both[SEG - 1 :, :128]))
            dc[:, cols] = th * (dcar + (cum[SEG - 1 :, 128:] + both[SEG - 1 :, 128:]))
            e = expu[:, cols] * a
            rd = 1.0 / (sd + e)
            w = (sn + e * v) * rd
            sr = jax.nn.sigmoid(rb[at, cols])
            mixed_o[at, cols] = (sr * w).astype(BF16)

            a_o[at, cols] = a
            v_o[at, cols] = v
            sr_o[at, cols] = sr
            w_o[at, cols] = w
            rd_o[at, cols] = rd
            sn_o[at, cols] = sn
            sd_o[at, cols] = sd

    save(6, 14)
    reuse(14, 20)
    loaded(3, 4)
    hb[...] = nn(mixed_o[...], wo[...])

    rows0 = pl.multiple_of(i * BLK, BLK)
    for s in range(BLK // SUB):
        at = pl.ds(s * SUB, SUB)
        after = x_ref[at, :].astype(F32) + hb[at, :]
        n2, r2 = normalize(after)
        h2 = n2 * g2[...] + b2[...]
        before = p2[...]
        if (s * SUB) % SEG == 0:
            before = before * (1.0 - fresh[s * SUB // SEG])
        sh = roll_down(h2, before)
        p2[...] = h2[SUB - 1 :, :]
        dh2 = h2 - sh
        cks[pl.ds(rows0 + s * SUB, SUB), :] = (sh + dh2 * ck[...]).astype(BF16)
        chrec_o[at, :] = (sh + dh2 * cr[...]).astype(BF16)
        after_o[at, :] = after
        n2_o[at, :] = n2
        dh2_o[at, :] = dh2
        r2_o[at, :] = jnp.broadcast_to(r2, (SUB, 128))

    save(14, 19)
    loaded(4, 7)
    rows = pl.ds(rows0, BLK)
    hb[...] = nn(cks[rows, :], wfk[...])
    gate_o[...] = nn(chrec_o[...], wg[...])
    for s in range(BLK // SUB):
        at = pl.ds(s * SUB, SUB)
        hp = jnp.maximum(hb[at, :], 0.0)
        hid[pl.ds(rows0 + s * SUB, SUB), :] = (hp * hp).astype(BF16)
        gate = jax.nn.sigmoid(gate_o[at, :])
        gate_o[at, :] = gate
        go = adj_ref[at, :].astype(F32) * live[s * SUB // SEG]
        gch[pl.ds(rows0 + s * SUB, SUB), :] = (go * gate).astype(BF16)
    save(19, 20)
    spread(pq, 0, nn(hid[rows, :], wfv[...]))
    kb[...] = nt(gch[rows, :], wfv[...])
    for s in range(BLK // SUB):
        at = pl.ds(s * SUB, SUB)
        gpr[pl.ds(rows0 + s * SUB, SUB), :] = (2.0 * jnp.maximum(hb[at, :], 0.0) * kb[at, :]).astype(BF16)
    spread(pq, SEG, nt(gpr[rows, :], wfk[...]))

    @pl.when(i == T // BLK - 1)
    def _():
        out_copies = []
        for k, (left, right) in enumerate(((cks, gpr), (hid, gch))):
            for c in range(D // 256):
                at = pl.ds(D * k + 256 * c, 256)
                gbuf[at, :] = tn(left[:, pl.ds(256 * c, 256)], right[...])
                out_copies.append(pltpu.make_async_copy(gbuf.at[at, :], grads.at[at, :], gsem.at[3 * k + c]))
                out_copies[-1].start()
        for copy in out_copies:
            copy.wait()

    @pl.when((i == T // BLK - 1) & (half_ref[0] == 1))
    def _():
        for s in range(SLOTS):
            for copy in saves(s):
                copy.wait()


def front(half, sizes, x, adj, vecs, mats):
    steps = T // BLK
    blk = lambda w: pl.BlockSpec((BLK, w), lambda i, h: (i, 0))
    vec = pl.BlockSpec((D,), lambda i, h: (0,))
    anywhere = pl.BlockSpec(memory_space=pl.ANY)
    sds = jax.ShapeDtypeStruct
    vm = pltpu.VMEM
    return pl.pallas_call(
        front_kernel,
        grid_spec=pltpu.PrefetchScalarGridSpec(
            num_scalar_prefetch=1,
            grid=(steps,),
            in_specs=[pl.BlockSpec(memory_space=pltpu.SMEM), blk(D), blk(D)] + [vec] * 11 + [anywhere] * 7,
            out_specs=[pl.BlockSpec(memory_space=pltpu.SMEM), pl.BlockSpec((2 * BLK, D), lambda i, h: (i, 0))]
            + [anywhere] * 21,
            scratch_shapes=[vm((D, D), BF16)] * 7
            + [vm((SLOTS, 13, BLK, D), F32), vm((SLOTS, 2, BLK, 128), F32), vm((SLOTS, 5, BLK, D), BF16), vm((2 * D, D), F32)]
            + [vm((SEG, D), F32)] * 2 + [vm((1, D), F32)] * 6 + [vm((BLK, D), F32)] * 4
            + [vm((T, D), BF16)] * 4 + [vm((16, D), F32)]
            + [pltpu.SemaphoreType.DMA((7,)), pltpu.SemaphoreType.DMA((SLOTS, 20)), pltpu.SemaphoreType.DMA((6,))],
        ),
        out_shape=[sds((2, NSEG), F32), sds((2 * T, D), F32), sds((2 * D, D), F32)]
        + [sds((HALF, D), F32)] * 13 + [sds((HALF, 128), F32)] * 2 + [sds((HALF, D), BF16)] * 5,
        compiler_params=pltpu.CompilerParams(dimension_semantics=("arbitrary",), vmem_limit_bytes=62 * 2**20),
        cost_estimate=pl.CostEstimate(flops=11 * 2 * T * D * D, bytes_accessed=60 * 2**20, transcendentals=4 * T * D),
        name="front",
    )(half, sizes, x, adj, *vecs, *mats)


MESH = pl.DeviceIdType.MESH
COPIES = 256
FF_ROWS = 2 * D
R_ROWS = 2048
MATS = 5
BACK_VMEM = 39
FINISH_VMEM = 2
SETTLE = 24
ORDER = (
    "cbBaBMdbBBaBcdBMabdcabdcBabBdMMcMaMbMMdcMOMMbMMO",
    "OcMMpqMMMMMsMtpqrOMOMMMtpsrqMGptrsdaOOqrtsVpqdtV",
    "OrGsqGcptGGasrpbqtrsGVpGqtOsGrGV",
)
NVEC = 11


def rows(start, size):
    return pl.ds(pl.multiple_of(start, 8), size)


def each(count, step, body, reverse=False):
    def run(k, carry):
        body((count - 1 - k) * step if reverse else k * step)
        return carry

    lax.fori_loop(0, count, run, 0)


class Links:
    def __init__(self, sends, recvs):
        self.sends, self.recvs, self.used, self.open, self.step = sends, recvs, 0, [], 0

    def send(self, src, dst, device):
        k = self.used
        self.used += 1
        copy = pltpu.make_async_remote_copy(
            src_ref=src, dst_ref=dst, send_sem=self.sends.at[k], recv_sem=self.recvs.at[k],
            device_id=device, device_id_type=MESH,
        )
        copy.start()
        self.open.append((self.step, copy))
        return copy

    def sent(self, copy):
        if all(kept[1] is not copy for kept in self.open):
            return
        self.open = [kept for kept in self.open if kept[1] is not copy]
        copy.wait_send()

    def settle(self, steps):
        while self.open and self.open[0][0] < self.step - steps:
            self.open.pop(0)[1].wait_send()
        self.step += 1

    def finish(self):
        for _, copy in self.open:
            copy.wait_send()


def add_into(dst, dst_at, terms, size, step=16):
    if size % step:
        step = 8

    def body(r):
        total = dst[rows(dst_at + r, step), :]
        for ref, start in terms:
            total = total + ref[rows(start + r, step), :]
        dst[rows(dst_at + r, step), :] = total

    each(size // step, step, body)


def ring_reduce(links, data, base, size, place, up, down, land, land_at, source, loaded):
    s = size // 4
    qa = (s // 2 + 7) // 8 * 8
    qb = s - qa
    mine = base + place * s
    nxt = base + lax.rem(place + 1, 4) * s
    opp = base + lax.rem(place + 2, 4) * s
    prv = base + lax.rem(place + 3, 4) * s
    starts = [land_at]
    for size_k in (qa, qb, qb, qa, qa, qb):
        starts.append(starts[-1] + size_k)
    spot = [land.at[pl.ds(a, b - a), :] for a, b in zip(starts, starts[1:])]
    fwd_a = links.send(source.at[rows(opp, qa), :], spot[0], up)
    fwd_b = links.send(source.at[rows(opp + qa, qb), :], spot[1], down)
    dir_b = links.send(source.at[rows(nxt + qa, qb), :], spot[2], up)
    dir_a = links.send(source.at[rows(prv, qa), :], spot[3], down)
    yield
    if loaded is not None:
        loaded()
    fwd_a.wait_recv()
    add_into(land, starts[0], [(data, nxt)], qa)
    cmb_a = links.send(spot[0], spot[4], up)
    fwd_b.wait_recv()
    add_into(land, starts[1], [(data, prv + qa)], qb)
    for copy in (fwd_a, fwd_b, dir_b, dir_a):
        links.sent(copy)
    cmb_b = links.send(spot[1], spot[5], down)
    yield
    dir_a.wait_recv()
    dir_b.wait_recv()
    cmb_a.wait_recv()
    cmb_b.wait_recv()
    add_into(data, mine, [(land, starts[3]), (land, starts[4])], qa)
    add_into(data, mine + qa, [(land, starts[2]), (land, starts[5])], qb)


def ring_gather(links, data, base, size, place, up, down, share):
    s = size // 4
    qa = (s // 2 + 7) // 8 * 8
    qb = s - qa
    mine = base + place * s
    nxt = base + lax.rem(place + 1, 4) * s
    opp = base + lax.rem(place + 2, 4) * s
    prv = base + lax.rem(place + 3, 4) * s
    own = data.at[rows(mine, s), :]
    to_up = links.send(own, own, up)
    to_down = links.send(own, own, down)
    share(own)
    yield
    to_up.wait_recv()
    half_a = data.at[rows(prv, qa), :]
    on_a = links.send(half_a, half_a, up)
    to_down.wait_recv()
    half_b = data.at[rows(nxt + qa, qb), :]
    on_b = links.send(half_b, half_b, down)
    share(data.at[rows(prv, s), :])
    share(data.at[rows(nxt, s), :])
    yield
    on_a.wait_recv()
    on_b.wait_recv()
    share(data.at[rows(opp, s), :])


def near_reduce(links, data, base, size, place, others, land, land_at, stage_at):
    s = size // 4
    copies = []
    for k, device in enumerate(others):
        theirs = base + lax.rem(place + 1 + k, 4) * s
        stage = stage_at + k * s

        def body(r, theirs=theirs, stage=stage):
            land[rows(stage + r, 8), :] = data[rows(theirs + r, 8), :]

        each(s // 8, 8, body)
        copies.append(links.send(land.at[pl.ds(stage, s), :], land.at[pl.ds(land_at + k * s, s), :], device))
    yield
    for copy in copies:
        copy.wait_recv()
    add_into(data, base + place * s, [(land, land_at + k * s) for k in range(3)], s, 8)


def near_gather(links, data, base, size, place, others):
    s = size // 4
    own = data.at[rows(base + place * s, s), :]
    copies = [links.send(own, own, device) for device in others]
    yield
    for copy in copies:
        copy.wait_recv()


def sum_of_four(links, data, base, size, place, others, land, land_at):
    mine = rows(land_at + place * size, size)
    land[mine, :] = data[rows(base, size), :]
    copies = [links.send(land.at[mine, :], land.at[mine, :], device) for device in others]
    yield
    for copy in copies:
        copy.wait_recv()

    def body(r):
        a, b, c, d = (land[rows(land_at + k * size + r, 8), :] for k in range(4))
        data[rows(base + r, 8), :] = (a + b) + (c + d)

    each(size // 8, 8, body)


def all_reduce(links, data, base, size, axes, land, land_at, last, last_land, last_at, source, loaded, share):
    (place, up, _, down), (place_2, *others) = axes
    yield from ring_reduce(links, data, base, size, place, up, down, land, land_at, source, loaded)
    part = size // 4
    at = base + place * part
    yield from near_reduce(links, data, at, part, place_2, others, land, land_at + 3 * part, land_at + part)
    yield from last(links, data, at + place_2 * (part // 4), part // 4, last_land, last_at)
    yield from near_gather(links, data, at, part, place_2, others)
    yield from ring_gather(links, data, base, size, place, up, down, share)


def back_kernel(
    flags, pq, grads, n1_h, dh1_h, a_h, v_h, sr_h, w_h, rd_h, sn_h, sd_h, after_h, gate_h, n2_h, dh2_h,
    r1_h, r2_h, keyed_h, valued_h, recepted_h, mixed_h, chrec_h, adj_h,
    g1_h, fk_h, fv_h, fr_h, dec_h, rew_h, g2_h, ck_h, cr_h, wr_h, wk_h, wv_h, wo_h, wg_h,
    out_o, gi, vec_o, red, ff,
    front4, r1, r2, keyed, valued, recepted, mixed, chrec, adj, wr, wo, wg,
    fin, xb, gg, gb, gk, gv, gp, t0, t1, t2, other, ffland, yland, vland,
    urow, urow2, gsend, grecv, acc, rise, fade, through, expu, sums, gc, pv,
    sends, recvs, fill, ready_ring, ready_sib,
):
    dp = lax.axis_index("dp")
    tensor = lax.axis_index("tensor")
    x, z, yl = dp // 8, lax.rem(dp // 2, 4), lax.rem(dp, 2)
    h, c = tensor // 2, lax.rem(tensor, 2)
    y = 2 * h + yl

    def chip(cx, cz, cy):
        cx, cz, cy = lax.rem(cx + 4, 4), lax.rem(cz + 4, 4), lax.rem(cy + 4, 4)
        return {"dp": (cx * 4 + cz) * 2 + lax.rem(cy, 2), "tensor": (cy // 2) * 2 + c}

    xp, xo, xm = (chip(x + k, z, y) for k in (1, 2, 3))
    zp, zo, zm = (chip(x, z + k, y) for k in (1, 2, 3))
    yp, opp, ym = (chip(x, z, y + k) for k in (1, 2, 3))
    sib = {"dp": dp, "tensor": h * 2 + (1 - c)}
    pair = {"dp": dp + 1 - 2 * yl, "tensor": tensor}
    own_at, other_at = h * HALF, (1 - h) * HALF
    mine_at = c * R_ROWS

    given = (g1_h, fk_h, fv_h, fr_h, dec_h, rew_h, g2_h, ck_h, cr_h)
    g1, fk, fv, fr, dec, rew, g2, ck, cr = (pv.at[k : k + 1, :] for k in range(len(given)))
    barrier = pltpu.get_barrier_semaphore()
    partners = (xp, xo, xm, zp, zo, zm, yp, ym, opp, sib)
    for device in partners:
        pl.semaphore_signal(barrier, inc=1, device_id=device, device_id_type=MESH)

    fills = []

    def bring(src, dst):
        copy = pltpu.make_async_copy(src, dst, fill.at[len(fills)])
        copy.start()
        fills.append(copy)
        return copy

    def group(start):
        return rows(2 * start, 2 * SEG)

    PART, ARECV, CRECV, BRECV = (512 * k for k in range(4))
    part_in = [
        bring(pq.at[group(other_at + 128 * j + SEG * c), :], xb.at[pl.ds(PART + 128 * j, 128), :]) for j in range(4)
    ]
    ff_in = bring(grads, ff)
    fin_in = [
        bring(pq.at[group(own_at + 128 * j + SEG * c), :], fin.at[group(128 * j + SEG * c), :]) for j in range(4)
    ]
    pl.semaphore_wait(barrier, len(partners))

    links = Links(sends, recvs)
    ax, az, ay = (x, xp, xo, xm), (z, zp, zo, zm), (y, yp, opp, ym)

    def with_pair(links, data, base, size, land, land_at):
        whole = data.at[rows(base, size), :]
        copy = links.send(whole, land.at[pl.ds(land_at, size), :], pair)
        yield
        links.sent(copy)
        copy.wait_recv()
        add_into(data, base, [(land, land_at)], size, 8)

    def with_ring(axis):
        def last(links, data, base, size, land, land_at):
            yield from sum_of_four(links, data, base, size, axis[0], axis[1:], land, land_at)

        return last

    waited = []

    def ff_loaded():
        if not waited:
            ff_in.wait()
            waited.append(True)

    n = FF_ROWS // 4
    ffs = [
        all_reduce(
            links, ff, n * k, n, (ax, az) if k % 2 == 0 else (az, ax), ffland, n * k,
            with_pair, ffland, n * k + 15 * n // 16, grads, ff_loaded, lambda ref: None,
        )
        for k in range(4)
    ]

    a_in = [
        links.send(pq.at[group(other_at + 128 * j + SEG * (1 - c)), :], xb.at[pl.ds(ARECV + 128 * j, 128), :], sib)
        for j in range(4)
    ]
    c_in = [
        links.send(pq.at[group(own_at + 128 * j + SEG * (1 - c)), :], xb.at[pl.ds(CRECV + 128 * j, 128), :], sib)
        for j in range(4)
    ]
    half = pl.ds(0, HALF)
    AFTER, GATE, N2, DH2 = (HALF * k for k in range(4))
    SR, W, RD, A, V, SN, SD = (lax.rem(mine_at + HALF * k, 2 * R_ROWS) for k in range(1, 8))
    first_in = [
        bring(s.at[half, :], front4.at[pl.ds(HALF * k, HALF), :]) for k, s in enumerate((after_h, gate_h, n2_h, dh2_h))
    ]
    first_in += [bring(adj_h.at[rows(own_at, HALF), :], adj), bring(wg_h, wg), bring(r2_h.at[half, :], r2)]
    first_in += [bring(wo_h, wo)]
    second_in = [
        bring(s.at[half, :], red.at[rows(spot, HALF), :])
        for s, spot in ((a_h, A), (v_h, V), (sr_h, SR), (w_h, W), (rd_h, RD), (sn_h, SN), (sd_h, SD))
    ]
    lanes = pl.ds(pl.multiple_of(c * HALF_D, 128), HALF_D)
    third_in = [
        bring(s.at[half, lanes], d)
        for s, d in (
            (mixed_h, mixed), (chrec_h, chrec), (keyed_h, keyed), (valued_h, valued), (recepted_h, recepted),
        )
    ]
    third_in += [bring(r1_h.at[half, :], r1), bring(wr_h, wr)]
    b_in = []

    def other_half():
        for j in range(4):
            part_in[j].wait()
            a_in[j].wait_recv()
            for at in (128 * j, 128 * j + SEG):
                add_into(xb, PART + at, [(xb, ARECV + at)], SEG)
                b_in.append(links.send(xb.at[pl.ds(PART + at, SEG), :], xb.at[pl.ds(BRECV + at, SEG), :], opp))
                yield

    seg0 = h * (HALF // SEG)
    not_last = (1 - h).astype(F32)

    def fold(v):
        return jnp.sum(v.reshape(-1, 8, D), axis=0)

    def tally(k, v):
        acc[pl.ds(8 * k, 8), :] += fold(v)

    GAIN1, BIAS1, MIXK, MIXV, MIXR, LOGD, REW, GAIN2, BIAS2, CMIXK, CMIXR = range(NVEC)

    def take(j):
        fin_in[j].wait()
        c_in[j].wait_recv()
        b_in[2 * j].wait_recv()
        b_in[2 * j + 1].wait_recv()
        add_into(fin, 2 * (128 * j + SEG * c), [(xb, CRECV + 128 * j), (xb, BRECV + 128 * j)], 128)
        mine = fin.at[group(128 * j + SEG * c), :]
        links.sent(b_in[2 * j])
        links.sent(b_in[2 * j + 1])
        return links.send(mine, mine, sib)

    def gate_part(j):
        lo = 128 * j
        for seg in range(2):
            live = flags[1, seg0 + 2 * j + seg]

            def body(r, seg=seg, live=live):
                at = lo + SEG * seg + r
                gate = front4[rows(GATE + at, SUB), :]
                co = fin[rows(2 * (lo + SEG * seg) + r, SUB), :]
                res = live * (front4[rows(AFTER + at, SUB), :] + gate * co)
                front4[rows(AFTER + at, SUB), :] = res.astype(BF16).astype(F32)
                go = adj[rows(at, SUB), :].astype(F32) * live
                gg[rows(at, SUB), :] = (go * co * gate * (1.0 - gate)).astype(BF16)

            each(SEG // SUB, SUB, body)
        t0[...] = nt(gg[pl.ds(lo, 128), :], wg[...])
        for seg in range(2):

            def body2(r, seg=seg):
                at = 2 * (lo + SEG * seg) + r
                qk = fin[rows(at + SEG, SUB), :]
                qr = t0[rows(SEG * seg + r, SUB), :]
                dh2 = front4[rows(DH2 + lo + SEG * seg + r, SUB), :]
                tally(CMIXK, qk * dh2)
                tally(CMIXR, qr * dh2)
                base = qk * ck[...] + qr * cr[...]
                fin[rows(at, SUB), :] = base
                fin[rows(at + SEG, SUB), :] = (qk + qr) - base

            each(SEG // SUB, SUB, body2)

    def lifted(nxt, u):
        row = lax.broadcasted_iota(jnp.int32, u.shape, 0)
        return jnp.where(row == u.shape[0] - 1, nxt, pltpu.roll(u, u.shape[0] - 1, 0))

    def norm_back(e, n, r, gain):
        f = e * gain
        return r * (f - jnp.mean(f, axis=-1, keepdims=True) - n * jnp.mean(f * n, axis=-1, keepdims=True))

    def keep_next(seg):
        return 1.0 - flags[0, jnp.minimum(seg0 + seg + 1, NSEG - 1)]

    def walk_rows(j, edge_row, sub_body):
        for seg in (1, 0):
            s = 2 * j + seg
            live = flags[1, seg0 + s]
            for k in reversed(range(SEG // SUB)):
                lo = SEG * s + SUB * k
                at = 2 * SEG * s + SUB * k
                if lo + SUB == HALF:
                    nxt = edge_row[0:1, :] * (not_last * keep_next(s))
                elif k == SEG // SUB - 1:
                    nxt = fin[2 * SEG * (s + 1) + SEG : 2 * SEG * (s + 1) + SEG + 1, :] * keep_next(s)
                else:
                    nxt = fin[at + SEG + SUB : at + SEG + SUB + 1, :]
                sub_body(lo, at, live, nxt)

    def after_rows(lo, at, live, nxt):
        e = fin[pl.ds(at, SUB), :] + lifted(nxt, fin[pl.ds(at + SEG, SUB), :])
        n = front4[pl.ds(N2 + lo, SUB), :]
        tally(GAIN2, e * n)
        tally(BIAS2, e)
        go = adj[pl.ds(lo, SUB), :].astype(F32) * live
        ga = go + norm_back(e, n, r2[pl.ds(lo, SUB), 0:1], g2[...])
        front4[pl.ds(N2 + lo, SUB), :] = ga
        gb[pl.ds(lo, SUB), :] = ga.astype(BF16)

    def mixed_chunk(j):
        t0[...] = nt(gb[pl.ds(128 * j, 128), :], wo[...])
        for seg in (1, 0):
            total = 16 * (2 * j + seg)
            sums[pl.ds(total, 16), :] = jnp.zeros((16, D), F32)

            def body(r, seg=seg, total=total):
                at = 128 * j + SEG * seg + r
                gm = t0[rows(SEG * seg + r, SUB), :]
                sr = red[rows(SR + at, SUB), :]
                w = red[rows(W + at, SUB), :]
                gw = gm * sr
                q = gw * red[rows(RD + at, SUB), :]
                red[rows(RD + at, SUB), :] = q
                gp[rows(at, SUB), :] = (gw * w * (1.0 - sr)).astype(BF16)
                fq = fade[rows(r, SUB), :] * q
                sums[pl.ds(total, 8), :] += fold(fq)
                sums[pl.ds(total + 8, 8), :] += fold(fq * w)

            each(SEG // SUB, SUB, body)

    def chain():
        first = jnp.zeros((1, D), F32)
        second = jnp.zeros((1, D), F32)
        th = through[...]
        for s in reversed(range(8)):
            q = jnp.sum(sums[pl.ds(16 * s, 8), :], axis=0, keepdims=True)
            qw = jnp.sum(sums[pl.ds(16 * s + 8, 8), :], axis=0, keepdims=True)
            if s < 7:
                q = q + th * (first * keep_next(s))
                qw = qw + th * (second * keep_next(s))
            first, second = q, qw
        sums[0:1, :] = first
        sums[1:2, :] = second

    tri = triangle(True)

    def key_value(k, carry):
        s = 7 - k
        lo = SEG * s
        keep = 1.0 - flags[0, seg0 + s]
        for col in range(D // 128):
            cols = pl.ds(col * 128, 128)
            at = rows(lo, SEG)
            q = red[rows(RD + lo, SEG), cols]
            w = red[rows(W + lo, SEG), cols]
            a = red[rows(A + lo, SEG), cols]
            v = red[rows(V + lo, SEG), cols]
            fq = fade[:, cols] * q
            cum, both = running(tri, fq, fq * w)
            cn = through[:, cols] * gc[0:1, cols]
            cd = through[:, cols] * gc[1:2, cols]
            gn = rise[:, cols] * (cum[:, :128] + cn)
            gd = rise[:, cols] * (cum[:, 128:] + cd)
            gc[0:1, cols] = (both[0:1, :128] + cum[0:1, :128] + cn) * keep
            gc[1:2, cols] = (both[0:1, 128:] + cum[0:1, 128:] + cd) * keep
            eq = expu[:, cols] * a * q
            gvv = a * gn + eq
            gv[at, cols] = gvv.astype(BF16)
            gk[at, cols] = (v * gvv - (a * gd + eq * w)).astype(BF16)
            up = eq * (v - w)
            down = gn * red[rows(SN + lo, SEG), cols] - gd * red[rows(SD + lo, SEG), cols]
            acc[pl.ds(8 * REW, 8), cols] += jnp.sum(up.reshape(-1, 8, 128), axis=0)
            acc[pl.ds(8 * LOGD, 8), cols] += jnp.sum(down.reshape(-1, 8, 128), axis=0)
        return carry

    def weights(k, left, right):
        for col in range(D // 256):
            cols = pl.ds(256 * col, 256)
            red[rows(mine_at + HALF_D * k, HALF_D), cols] = tn(left[...], right[:, cols])

    shared = []

    def share(ref):
        if not shared:
            pl.semaphore_wait(ready_sib, 1)
        shared.append(links.send(ref, ref, sib))

    orders = ((ax, az, ay), (az, ax, ay), (ax, az, ay), (az, ax, ay), (ay, ax, az))

    def reduce_weights(k):
        if k == 0:
            pl.semaphore_wait(ready_ring, 6)
        first, second, third = orders[k]
        yield from all_reduce(
            links, red, mine_at + HALF_D * k, HALF_D, (first, second), xb, HALF_D * k,
            with_ring(third), yland, HALF_D // 4 * k, red, None, share,
        )

    def front_chunk(j):
        at0 = pl.ds(128 * j, 128)
        t0[...] = nt(gk[at0, :], wk[...])
        t1[...] = nt(gv[at0, :], wv[...])
        t2[...] = nt(gp[at0, :], wr[...])
        for seg in range(2):

            def body(r, seg=seg):
                lo = 128 * j + SEG * seg
                pk, pv_, pr = (t[rows(SEG * seg + r, SUB), :] for t in (t0, t1, t2))
                dh1 = front4[rows(DH2 + lo + r, SUB), :]
                tally(MIXK, pk * dh1)
                tally(MIXV, pv_ * dh1)
                tally(MIXR, pr * dh1)
                base = pk * fk[...] + pv_ * fv[...] + pr * fr[...]
                fin[rows(2 * lo + r, SUB), :] = base
                fin[rows(2 * lo + SEG + r, SUB), :] = (pk + pv_ + pr) - base

            each(SEG // SUB, SUB, body)

    def input_rows(lo, at, live, nxt):
        e = fin[pl.ds(at, SUB), :] + lifted(nxt, fin[pl.ds(at + SEG, SUB), :])
        n = front4[pl.ds(GATE + lo, SUB), :]
        tally(GAIN1, e * n)
        tally(BIAS1, e)
        gi[rows(own_at + lo, SUB), :] = front4[pl.ds(N2 + lo, SUB), :] + norm_back(e, n, r1[pl.ds(lo, SUB), 0:1], g1[...])

    def vector_sums():
        scale = -jnp.exp(dec[...]) * jnp.exp(-jnp.exp(dec[...]))
        vec_o[...] = jnp.zeros_like(vec_o)
        for k in range(NVEC):
            total = jnp.sum(acc[pl.ds(8 * k, 8), :], axis=0, keepdims=True)
            vec_o[k : k + 1, :] = total * scale if k == LOGD else total

    def cast_rows(r):
        out_o[rows(own_at + r, SUB), :] = front4[rows(AFTER + r, SUB), :].astype(BF16)
        out_o[rows(other_at + r, SUB), :] = other[rows(r, SUB), :].astype(BF16)

    wk, wv = wg, wo

    def compute():
        for k, v in enumerate(given):
            pv[k : k + 1, :] = v[...].reshape(1, D)
        through[...] = decay_tables(dec[...], rise, fade)
        expu[...] = jnp.exp(rew[...])
        acc[...] = jnp.zeros_like(acc)
        for copy in first_in:
            copy.wait()
        yield
        for j in range(4):
            e_in = take(j)
            if j == 3:
                for device in (xp, xm, zp, zm, yp, ym):
                    pl.semaphore_signal(ready_ring, inc=1, device_id=device, device_id_type=MESH)
            yield
            e_in.wait_recv()
            links.sent(e_in)
            gate_part(j)
            if j == 0:
                gsend[...] = fin[SEG : SEG + 8, :]
                u_in = links.send(gsend, urow, opp)
            yield
        wk_in = bring(wk_h, wk)
        u_in.wait_recv()
        for copy in second_in:
            copy.wait()
        for j in reversed(range(4)):
            walk_rows(j, urow, after_rows)
            mixed_chunk(j)
            if j > 0:
                yield
        chain()
        g_in = links.send(sums.at[pl.ds(0, 8), :], grecv, opp)
        late = [wk_in, bring(wv_h, wv), bring(n1_h.at[half, :], front4.at[pl.ds(GATE, HALF), :])]
        late.append(bring(dh1_h.at[half, :], front4.at[pl.ds(DH2, HALF), :]))
        yield
        for copy in third_in:
            copy.wait()
        weights(0, mixed, gb)
        yield
        weights(1, chrec, gg)
        yield
        g_in.wait_recv()
        edge = not_last * keep_next(7)
        gc[0:1, :] = grecv[0:1, :] * edge
        gc[1:2, :] = grecv[1:2, :] * edge
        lax.fori_loop(0, 4, key_value, 0)
        yield
        lax.fori_loop(4, 8, key_value, 0)
        pl.semaphore_signal(ready_sib, inc=1, device_id=sib, device_id_type=MESH)
        yield
        weights(2, recepted, gp)
        yield
        weights(3, keyed, gk)
        yield
        weights(4, valued, gv)
        yield
        for copy in late:
            copy.wait()
        for j in range(4):
            front_chunk(j)
            if j == 0:
                u2_in = links.send(fin.at[pl.ds(SEG, 8), :], urow2, opp)
            yield
        u2_in.wait_recv()
        for j in reversed(range(4)):
            walk_rows(j, urow2, input_rows)
            if j == 2:
                yield
        vector_sums()

    def vectors():
        for k, (place, others) in enumerate(((x, (xp, xo, xm)), (z, (zp, zo, zm)), (y, (yp, opp, ym)))):
            yield from sum_of_four(links, vec_o, 0, 16, place, others, vland, 64 * k)

    def swap(src, src_at, dst, dst_at, back_at):
        there = []
        for k in range(4):
            there.append(
                links.send(src.at[rows(src_at + SEG * k, SEG), :], dst.at[rows(dst_at + SEG * k, SEG), :], opp)
            )
            yield
        onward = []
        for k in range(4):
            there[k].wait_recv()
            theirs = dst.at[rows(back_at + SEG * k, SEG), :]
            onward.append(links.send(theirs, theirs, sib))
            yield
        for copy in onward:
            copy.wait_recv()

    def result():
        yield from swap(front4, AFTER + 256 * c, other, 256 * c, 256 * c)
        each(HALF // SUB, SUB, cast_rows)

    def input_grads():
        yield from swap(gi, own_at + 256 * c, gi, own_at + 256 * c, other_at + 256 * c)

    jobs = dict(zip("abcd", ffs))
    jobs.update(zip("pqrst", (reduce_weights(k) for k in range(MATS))))
    jobs.update(M=compute(), B=other_half(), V=vectors(), O=result(), G=input_grads())
    for name in "".join(ORDER):
        next(jobs[name], None)
        links.settle(SETTLE)
    for copy in shared:
        copy.wait_recv()
    links.finish()


def back(front_outs, adj, vecs, mats):
    g1, b1, fk, fv, fr, dec, rew, g2, b2, ck, cr = vecs
    flags, rest = front_outs[0], front_outs[1:]
    vm = pltpu.VMEM
    anywhere = pl.BlockSpec(memory_space=pl.ANY)
    vmem = pl.BlockSpec(memory_space=pltpu.VMEM)
    half = lambda dt: vm((HALF, D), dt)
    return pl.pallas_call(
        back_kernel,
        in_specs=[pl.BlockSpec(memory_space=pltpu.SMEM)] + [anywhere] * len(rest) + [anywhere]
        + [vmem] * 9 + [anywhere] * 5,
        out_specs=[vmem] * 5,
        out_shape=[vm((T, D), BF16), vm((T, D), F32), vm((16, D), F32), vm((2 * R_ROWS, D), F32), vm((FF_ROWS, D), F32)],
        scratch_shapes=[vm((4 * HALF, D), F32), vm((HALF, 128), F32), vm((HALF, 128), F32)]
        + [vm((HALF, HALF_D), BF16)] * 5 + [half(BF16)] + [vm((D, D), BF16)] * 3
        + [vm((2 * HALF, D), F32), vm((R_ROWS, D), F32)]
        + [half(BF16)] * 5 + [vm((128, D), F32)] * 3 + [half(F32)]
        + [vm((FF_ROWS, D), F32), vm((R_ROWS // 4, D), F32), vm((192, D), F32)]
        + [vm((8, D), F32)] * 4 + [vm((8 * NVEC, D), F32)] + [vm((SEG, D), F32)] * 2
        + [vm((1, D), F32)] * 2 + [vm((128, D), F32), vm((8, D), F32), vm((16, D), F32)]
        + [pltpu.SemaphoreType.DMA((COPIES,)), pltpu.SemaphoreType.DMA((COPIES,)),
           pltpu.SemaphoreType.DMA((48,)), pltpu.SemaphoreType.REGULAR, pltpu.SemaphoreType.REGULAR],
        compiler_params=pltpu.CompilerParams(collective_id=1, has_side_effects=True, vmem_limit_bytes=BACK_VMEM * 2**20),
        cost_estimate=pl.CostEstimate(flops=14 * T * D * D, bytes_accessed=60 * 2**20, transcendentals=0),
        name="back",
    )(flags, *rest, adj, g1, fk, fv, fr, dec, rew, g2, ck, cr, *mats[:5])


def finish_kernel(out, gi, vec, red, ff, *refs):
    out_o, gi_o, mats, ck_o, cv_o, vecs, sems = refs[0], refs[1], refs[2:7], refs[7], refs[8], refs[9:20], refs[20]
    pairs = [(gi, gi_o), (ff.at[pl.ds(0, D), :], ck_o), (ff.at[pl.ds(D, D), :], cv_o), (out, out_o)]
    for k in range(MATS):
        for core in range(2):
            src = red.at[pl.ds(core * R_ROWS + HALF_D * k, HALF_D), :]
            pairs.append((src, mats[(3, 4, 0, 1, 2)[k]].at[pl.ds(HALF_D * core, HALF_D), :]))
    copies = [pltpu.make_async_copy(src, dst, sems.at[k]) for k, (src, dst) in enumerate(pairs)]
    for copy in copies:
        copy.start()
    for k in range(NVEC):
        vecs[k][...] = vec[k : k + 1, :].reshape(D)
    for copy in copies:
        copy.wait()


def finish(out, gi, vec, red, ff):
    sds = jax.ShapeDtypeStruct
    anywhere = pl.BlockSpec(memory_space=pl.ANY)
    vmem = pl.BlockSpec(memory_space=pltpu.VMEM)
    return pl.pallas_call(
        finish_kernel,
        in_specs=[vmem] * 5,
        out_specs=[anywhere] * 9 + [vmem] * NVEC,
        out_shape=[sds((T, D), BF16), sds((T, D), F32)] + [sds((D, D), F32)] * 7 + [sds((D,), F32)] * NVEC,
        scratch_shapes=[pltpu.SemaphoreType.DMA((16,))],
        compiler_params=pltpu.CompilerParams(vmem_limit_bytes=FINISH_VMEM * 2**20),
        name="finish",
    )(out, gi, vec, red, ff)


def body(
    entering_activations, sample_sizes, initial_layernorm_scale, initial_layernorm_offset, temporal_lookup_fraction,
    temporal_content_fraction, temporal_gating_fraction, fading_speed_logarithm, present_reward,
    temporal_gating_matrix, temporal_lookup_matrix, temporal_content_matrix, temporal_emission_matrix,
    latter_layernorm_scale, latter_layernorm_offset, feedforward_lookup_fraction, feedforward_gating_fraction,
    feedforward_gating_matrix, feedforward_lookup_matrix, feedforward_content_matrix, upstream_adjoint,
):
    vecs = (
        initial_layernorm_scale, initial_layernorm_offset, temporal_lookup_fraction, temporal_content_fraction,
        temporal_gating_fraction, fading_speed_logarithm, present_reward, latter_layernorm_scale,
        latter_layernorm_offset, feedforward_lookup_fraction, feedforward_gating_fraction,
    )
    mats = (
        temporal_gating_matrix, temporal_lookup_matrix, temporal_content_matrix, temporal_emission_matrix,
        feedforward_gating_matrix, feedforward_lookup_matrix, feedforward_content_matrix,
    )
    half = (lax.axis_index("tensor") // 2).astype(jnp.int32).reshape(1)
    fronts = front(half, sample_sizes, entering_activations, upstream_adjoint, vecs, mats)
    out, grad_inputs, recw, keyw, valw, outw, chrec, chkey, chval, *g = finish(*back(fronts, upstream_adjoint, vecs, mats))
    return (
        out, grad_inputs, g[0], g[1], g[2], g[3], g[4], g[5], g[6], recw, keyw, valw, outw,
        g[7], g[8], g[9], g[10], chrec, chkey, chval,
    )


def solution(mesh):
    split = P("dp", None)
    in_specs = (split, split) + (P(),) * 16 + (P(None, "tensor"), P("tensor", None), split)
    out_specs = (split, split) + (P(),) * 16 + (P(None, "tensor"), P("tensor", None))
    return jax.shard_map(body, mesh=mesh, in_specs=in_specs, out_specs=out_specs, check_vma=False)
```

```python
import functools

import jax
import jax.numpy as jnp
from jax import lax
from jax.experimental import pallas as pl
from jax.experimental.pallas import tpu as pltpu
from jax.sharding import PartitionSpec as P

F32 = jnp.float32
BF16 = jnp.bfloat16
EPSILON = 1e-05
SEG = 64
D = 768
T = 1024
HALF = 512
HALF_D = D // 2
BLK = 512
SUB = 32
NSEG = T // SEG
PER = HALF // BLK
SLOTS = PER


def nn(left, right):
    return jnp.dot(left, right, preferred_element_type=F32)


def nt(left, right):
    return lax.dot_general(left, right, (((1,), (1,)), ((), ())), preferred_element_type=F32)


def tn(left, right):
    return lax.dot_general(left, right, (((0,), (0,)), ((), ())), preferred_element_type=F32)


def normalize(v):
    c = v - jnp.mean(v, axis=-1, keepdims=True)
    r = lax.rsqrt(jnp.mean(c * c, axis=-1, keepdims=True) + EPSILON)
    return c * r, r


def roll_down(v, first):
    row = lax.broadcasted_iota(jnp.int32, v.shape, 0)
    return jnp.where(row == 0, first, pltpu.roll(v, 1, 0))


def two_parts(v):
    hi = v.astype(BF16)
    return hi, (v - hi.astype(F32)).astype(BF16)


def triangle(upper):
    row = lax.broadcasted_iota(jnp.int32, (SEG, 2 * SEG), 0)
    col = lax.broadcasted_iota(jnp.int32, (SEG, 2 * SEG), 1)
    col = jnp.where(col >= SEG, col - SEG, col)
    keep = (col > row) if upper else (col < row)
    return jnp.where(keep, 1.0, 0.0).astype(BF16)


def running(tri, first, second):
    both = jnp.concatenate([first, second], axis=1)
    hi, lo = two_parts(both)
    return nn(tri, jnp.concatenate([hi, lo], axis=0)), both


def decay_tables(dec, rise, fade):
    rate = jnp.exp(dec)
    offs = lax.broadcasted_iota(jnp.int32, (SEG, D), 0).astype(F32)
    rise[...] = jnp.exp((offs + 1.0) * rate)
    fade[...] = jnp.exp(-offs * rate)
    return jnp.exp(-float(SEG) * rate)


def spread(dst, first, cols, v):
    for s in range(v.shape[0] // SEG):
        dst[first + 2 * SEG * s : first + 2 * SEG * s + SEG, cols] = v[SEG * s : SEG * (s + 1), :]


def weave(products, others):
    done = 0
    for k, product in enumerate(products):
        product()
        upto = len(others) * (k + 1) // len(products)
        for other in others[done:upto]:
            other()
        done = upto
    for other in others[done:]:
        other()


def front_kernel(
    half_ref, len_ref, x_ref, adj_ref, g1_h, b1_h, fk_h, fv_h, fr_h, dec_h, rew_h, g2_h, b2_h, ck_h, cr_h,
    wr_h, wk_h, wv_h, wo_h, wg_h, wfk_h, wfv_h,
    flags, pq, grads, n1_h, dh1_h, a_h, v_h, sr_h, w_h, rd_h, sn_h, sd_h, after_h, gate_h, n2_h, dh2_h,
    r1_h, r2_h, keyed_h, valued_h, recepted_h, mixed_h, chrec_h,
    wr, wk, wv, wo, wg, wfk, wfv, wide, narrow, low, gbuf,
    rise, fade, through, expu, nc, dc, p1, p2, kb, vb, rb, hb, cks_all, hid_all, gch_all, gpr_all, pv, win, outs, gsem,
):
    i = pl.program_id(0)
    slot = lax.rem(i, SLOTS) if SLOTS > 1 else 0
    cks, hid, gch, gpr = (ref.at[i] for ref in (cks_all, hid_all, gch_all, gpr_all))
    given = (g1_h, b1_h, fk_h, fv_h, fr_h, dec_h, rew_h, g2_h, b2_h, ck_h, cr_h)
    g1, b1, fk, fv, fr, dec, rew, g2, b2, ck, cr = (pv.at[k : k + 1, :] for k in range(len(given)))
    n1_o, dh1_o, a_o, v_o, sr_o, w_o, rd_o, sn_o, sd_o, after_o, gate_o, n2_o, dh2_o = (
        wide.at[slot, k] for k in range(13)
    )
    r1_o, r2_o = (narrow.at[slot, k] for k in range(2))
    keyed_o, valued_o, recepted_o, mixed_o, chrec_o = (low.at[slot, k] for k in range(5))
    loads = [
        pltpu.make_async_copy(src, dst, win.at[k])
        for k, (src, dst) in enumerate(
            ((wk_h, wk), (wv_h, wv), (wr_h, wr), (wo_h, wo), (wfk_h, wfk), (wg_h, wg), (wfv_h, wfv))
        )
    ]
    kept = pl.ds(pl.multiple_of(lax.rem(i, PER) * BLK, BLK), BLK)
    held = (
        (wide, 0, n1_h), (wide, 1, dh1_h), (narrow, 0, r1_h), (low, 0, keyed_h), (low, 1, valued_h), (low, 2, recepted_h),
        (wide, 2, a_h), (wide, 3, v_h), (wide, 4, sr_h), (wide, 5, w_h), (wide, 6, rd_h), (wide, 7, sn_h),
        (wide, 8, sd_h), (low, 3, mixed_h),
        (wide, 9, after_h), (wide, 11, n2_h), (wide, 12, dh2_h), (narrow, 1, r2_h), (low, 4, chrec_h),
        (wide, 10, gate_h),
    )

    def saves(at):
        return [
            pltpu.make_async_copy(src.at[at, n], dst.at[kept, :], outs.at[at, k])
            for k, (src, n, dst) in enumerate(held)
        ]

    def save(lo, hi):
        @pl.when(i // PER == half_ref[0])
        def _():
            for copy in saves(slot)[lo:hi]:
                copy.start()

    def loaded(lo, hi):
        @pl.when(i == 0)
        def _():
            for copy in loads[lo:hi]:
                copy.wait()

    @pl.when(i == 0)
    def _():
        for copy in loads:
            copy.start()

    def reuse(lo, hi):
        @pl.when((i >= PER) & (half_ref[0] == 0))
        def _():
            for copy in saves(slot)[lo:hi]:
                copy.wait()

    reuse(0, 6)
    @pl.when(i == 0)
    def _():
        for b in range(NSEG):
            flags[0, b] = 0.0
        begin = jnp.int32(0)
        for j in range(NSEG):
            size = len_ref[0, j]
            at = lax.shift_right_logical(begin, 6)

            @pl.when(size > 0)
            def _():
                flags[0, at] = 1.0

            begin = begin + size
        for b in range(NSEG):
            flags[1, b] = jnp.where(b * SEG < begin, 1.0, 0.0)
        for k, v in enumerate(given):
            pv[k : k + 1, :] = v[...].reshape(1, D)
        through[...] = decay_tables(dec[...], rise, fade)
        expu[...] = jnp.exp(rew[...])
        nc[...] = jnp.zeros_like(nc)
        dc[...] = jnp.zeros_like(dc)
        p1[...] = jnp.zeros_like(p1)
        p2[...] = jnp.zeros_like(p2)

    fresh = [flags[0, i * (BLK // SEG) + s] for s in range(BLK // SEG)]
    live = [flags[1, i * (BLK // SEG) + s] for s in range(BLK // SEG)]

    tri = triangle(False)
    part = BLK // 2
    subs = part // SUB
    segs = part // SEG
    col_tiles = [pl.ds(0, D)]

    def first_norm(s):
        at = pl.ds(s * SUB, SUB)
        n1, r1 = normalize(x_ref[at, :].astype(F32))
        h1 = n1 * g1[...] + b1[...]
        before = p1[...]
        if (s * SUB) % SEG == 0:
            before = before * (1.0 - fresh[s * SUB // SEG])
        sh = roll_down(h1, before)
        p1[...] = h1[SUB - 1 :, :]
        dh1 = h1 - sh
        keyed_o[at, :] = (sh + dh1 * fk[...]).astype(BF16)
        valued_o[at, :] = (sh + dh1 * fv[...]).astype(BF16)
        recepted_o[at, :] = (sh + dh1 * fr[...]).astype(BF16)
        n1_o[at, :] = n1
        dh1_o[at, :] = dh1
        r1_o[at, :] = jnp.broadcast_to(r1, (SUB, 128))

    def mix_time(s, c):
        at = pl.ds(s * SEG, SEG)
        keep = 1.0 - fresh[s]
        cols = pl.ds(c * 128, 128)
        a = jnp.exp(kb[at, cols])
        v = vb[at, cols]
        lift = rise[:, cols] * a
        cum, both = running(tri, lift * v, lift)
        ncar = nc[:, cols] * keep
        dcar = dc[:, cols] * keep
        sn = fade[:, cols] * (ncar + cum[:, :128])
        sd = fade[:, cols] * (dcar + cum[:, 128:])
        th = through[:, cols]
        nc[:, cols] = th * (ncar + (cum[SEG - 1 :, :128] + both[SEG - 1 :, :128]))
        dc[:, cols] = th * (dcar + (cum[SEG - 1 :, 128:] + both[SEG - 1 :, 128:]))
        e = expu[:, cols] * a
        rd = 1.0 / (sd + e)
        w = (sn + e * v) * rd
        sr = jax.nn.sigmoid(rb[at, cols])
        mixed_o[at, cols] = (sr * w).astype(BF16)
        a_o[at, cols] = a
        v_o[at, cols] = v
        sr_o[at, cols] = sr
        w_o[at, cols] = w
        rd_o[at, cols] = rd
        sn_o[at, cols] = sn
        sd_o[at, cols] = sd

    def second_norm(s):
        at = pl.ds(s * SUB, SUB)
        after = x_ref[at, :].astype(F32) + hb[at, :]
        n2, r2 = normalize(after)
        h2 = n2 * g2[...] + b2[...]
        before = p2[...]
        if (s * SUB) % SEG == 0:
            before = before * (1.0 - fresh[s * SUB // SEG])
        sh = roll_down(h2, before)
        p2[...] = h2[SUB - 1 :, :]
        dh2 = h2 - sh
        cks[at, :] = (sh + dh2 * ck[...]).astype(BF16)
        chrec_o[at, :] = (sh + dh2 * cr[...]).astype(BF16)
        after_o[at, :] = after
        n2_o[at, :] = n2
        dh2_o[at, :] = dh2
        r2_o[at, :] = jnp.broadcast_to(r2, (SUB, 128))

    def gates(s):
        at = pl.ds(s * SUB, SUB)
        hp = jnp.maximum(kb[at, :], 0.0)
        hid[at, :] = (hp * hp).astype(BF16)
        gate = jax.nn.sigmoid(rb[at, :])
        gate_o[at, :] = gate
        go = adj_ref[at, :].astype(F32) * live[s * SUB // SEG]
        gch[at, :] = (go * gate).astype(BF16)

    def hidden_grads(s):
        at = pl.ds(s * SUB, SUB)
        gpr[at, :] = (2.0 * jnp.maximum(kb[at, :], 0.0) * vb[at, :]).astype(BF16)

    def all_of(fn, p, count):
        return [functools.partial(fn, p * count + k) for k in range(count)]

    def times(p, dst, left, right):
        at = pl.ds(p * part, part)

        def piece(cols):
            dst[at, cols] = nn(left[at, :], right[:, cols])

        return [functools.partial(piece, cols) for cols in col_tiles]

    def times_turned(p, dst, left, right):
        at = pl.ds(p * part, part)

        def piece(cols):
            dst[at, cols] = nt(left[at, :], right[cols, :])

        return [functools.partial(piece, cols) for cols in col_tiles]

    def to_pq(p, first, product, left, right):
        at = pl.ds(p * part, part)

        def piece(cols):
            v = nn(left[at, :], right[:, cols]) if product is nn else nt(left[at, :], right[cols, :])
            spread(pq, 2 * p * part + first, cols, v)

        return [functools.partial(piece, cols) for cols in col_tiles]

    def projections(p):
        return times(p, kb, keyed_o, wk) + times(p, vb, valued_o, wv) + times(p, rb, recepted_o, wr)

    def mixing(p):
        return [functools.partial(mix_time, p * segs + s, c) for s in range(segs) for c in range(D // 128)]

    def hidden(p):
        return times(p, kb, cks, wfk) + times(p, rb, chrec_o, wg)

    def outward(p):
        return to_pq(p, 0, nn, hid, wfv) + times_turned(p, vb, gch, wfv)

    weave([], all_of(first_norm, 0, subs))
    loaded(0, 3)
    weave(projections(0), all_of(first_norm, 1, subs))
    save(0, 6)
    reuse(6, 14)
    loaded(3, 4)
    weave(projections(1), mixing(0))
    weave(times(0, hb, mixed_o, wo), mixing(1))
    save(6, 14)
    reuse(14, 20)
    loaded(4, 7)
    weave(times(1, hb, mixed_o, wo), all_of(second_norm, 0, subs))
    weave(hidden(0), all_of(second_norm, 1, subs))
    save(14, 19)
    weave(hidden(1), all_of(gates, 0, subs))
    weave(outward(0), all_of(gates, 1, subs))
    save(19, 20)
    weave(outward(1), all_of(hidden_grads, 0, subs))
    weave(to_pq(0, SEG, nt, gpr, wfk), all_of(hidden_grads, 1, subs))
    weave(to_pq(1, SEG, nt, gpr, wfk), [])

    @pl.when(i == T // BLK - 1)
    def _():
        out_copies = []
        for k, (left, right) in enumerate(((cks_all, gpr_all), (hid_all, gch_all))):
            for c in range(D // 256):
                at = pl.ds(D * k + 256 * c, 256)
                gbuf[at, :] = tn(left[:, :, pl.ds(256 * c, 256)].reshape(T, 256), right[...].reshape(T, D))
                out_copies.append(pltpu.make_async_copy(gbuf.at[at, :], grads.at[at, :], gsem.at[3 * k + c]))
                out_copies[-1].start()
        for copy in out_copies:
            copy.wait()

    @pl.when((i == T // BLK - 1) & (half_ref[0] == 1))
    def _():
        for s in range(SLOTS):
            for copy in saves(s):
                copy.wait()


def front(half, sizes, x, adj, vecs, mats):
    steps = T // BLK
    blk = lambda w: pl.BlockSpec((BLK, w), lambda i, h: (i, 0))
    vec = pl.BlockSpec((D,), lambda i, h: (0,))
    anywhere = pl.BlockSpec(memory_space=pl.ANY)
    sds = jax.ShapeDtypeStruct
    vm = pltpu.VMEM
    return pl.pallas_call(
        front_kernel,
        grid_spec=pltpu.PrefetchScalarGridSpec(
            num_scalar_prefetch=1,
            grid=(steps,),
            in_specs=[pl.BlockSpec(memory_space=pltpu.SMEM), blk(D), blk(D)] + [vec] * 11 + [anywhere] * 7,
            out_specs=[pl.BlockSpec(memory_space=pltpu.SMEM), pl.BlockSpec((2 * BLK, D), lambda i, h: (i, 0))]
            + [anywhere] * 21,
            scratch_shapes=[vm((D, D), BF16)] * 7
            + [vm((SLOTS, 13, BLK, D), F32), vm((SLOTS, 2, BLK, 128), F32), vm((SLOTS, 5, BLK, D), BF16), vm((2 * D, D), F32)]
            + [vm((SEG, D), F32)] * 2 + [vm((1, D), F32)] * 6 + [vm((BLK, D), F32)] * 4
            + [vm((T // BLK, BLK, D), BF16)] * 4 + [vm((16, D), F32)]
            + [pltpu.SemaphoreType.DMA((7,)), pltpu.SemaphoreType.DMA((SLOTS, 20)), pltpu.SemaphoreType.DMA((6,))],
        ),
        out_shape=[sds((2, NSEG), F32), sds((2 * T, D), F32), sds((2 * D, D), F32)]
        + [sds((HALF, D), F32)] * 13 + [sds((HALF, 128), F32)] * 2 + [sds((HALF, D), BF16)] * 5,
        compiler_params=pltpu.CompilerParams(dimension_semantics=("arbitrary",), vmem_limit_bytes=62 * 2**20),
        cost_estimate=pl.CostEstimate(flops=11 * 2 * T * D * D, bytes_accessed=60 * 2**20, transcendentals=4 * T * D),
        name="front",
    )(half, sizes, x, adj, *vecs, *mats)


MESH = pl.DeviceIdType.MESH
COPIES = 256
FF_ROWS = 2 * D
R_ROWS = 2048
MATS = 5
BACK_VMEM = 39
FINISH_VMEM = 2
SETTLE = 24
NEAR = (0, 1, 2, 3, 4)
ORDER = (
    "bcBBBMbBcBadbcMaMcdbMBBcbaMdMMBcbMaMMbdcMMMMpMOq",
    "MMOMMrsMtpsrOdcqtMsOaMMprqMtaOdsMqMpstrqdtGVbGpr",
    "psGrtOOqVpsGOtqdraGGVGsptGrOqGVa",
)
NVEC = 11


def rows(start, size):
    return pl.ds(pl.multiple_of(start, 8), size)


def each(count, step, body, reverse=False):
    def run(k, carry):
        body((count - 1 - k) * step if reverse else k * step)
        return carry

    lax.fori_loop(0, count, run, 0)


class Links:
    def __init__(self, sends, recvs):
        self.sends, self.recvs, self.used, self.open, self.step = sends, recvs, 0, [], 0

    def send(self, src, dst, device):
        k = self.used
        self.used += 1
        copy = pltpu.make_async_remote_copy(
            src_ref=src, dst_ref=dst, send_sem=self.sends.at[k], recv_sem=self.recvs.at[k],
            device_id=device, device_id_type=MESH,
        )
        copy.start()
        self.open.append((self.step, copy))
        return copy

    def sent(self, copy):
        if all(kept[1] is not copy for kept in self.open):
            return
        self.open = [kept for kept in self.open if kept[1] is not copy]
        copy.wait_send()

    def settle(self, steps):
        while self.open and self.open[0][0] < self.step - steps:
            self.open.pop(0)[1].wait_send()
        self.step += 1

    def finish(self):
        for _, copy in self.open:
            copy.wait_send()


def add_into(dst, dst_at, terms, size, step=16):
    if size % step:
        step = 8

    def body(r):
        total = dst[rows(dst_at + r, step), :]
        for ref, start in terms:
            total = total + ref[rows(start + r, step), :]
        dst[rows(dst_at + r, step), :] = total

    each(size // step, step, body)


def ring_reduce(links, data, base, size, place, up, down, land, land_at, source, loaded):
    s = size // 4
    qa = (s // 2 + 7) // 8 * 8
    qb = s - qa
    mine = base + place * s
    nxt = base + lax.rem(place + 1, 4) * s
    opp = base + lax.rem(place + 2, 4) * s
    prv = base + lax.rem(place + 3, 4) * s
    starts = [land_at]
    for size_k in (qa, qb, qb, qa, qa, qb):
        starts.append(starts[-1] + size_k)
    spot = [land.at[pl.ds(a, b - a), :] for a, b in zip(starts, starts[1:])]
    fwd_a = links.send(source.at[rows(opp, qa), :], spot[0], up)
    fwd_b = links.send(source.at[rows(opp + qa, qb), :], spot[1], down)
    dir_b = links.send(source.at[rows(nxt + qa, qb), :], spot[2], up)
    dir_a = links.send(source.at[rows(prv, qa), :], spot[3], down)
    yield
    if loaded is not None:
        loaded()
    fwd_a.wait_recv()
    add_into(land, starts[0], [(data, nxt)], qa)
    cmb_a = links.send(spot[0], spot[4], up)
    fwd_b.wait_recv()
    add_into(land, starts[1], [(data, prv + qa)], qb)
    for copy in (fwd_a, fwd_b, dir_b, dir_a):
        links.sent(copy)
    cmb_b = links.send(spot[1], spot[5], down)
    yield
    dir_a.wait_recv()
    dir_b.wait_recv()
    cmb_a.wait_recv()
    cmb_b.wait_recv()
    add_into(data, mine, [(land, starts[3]), (land, starts[4])], qa)
    add_into(data, mine + qa, [(land, starts[2]), (land, starts[5])], qb)


def ring_gather(links, data, base, size, place, up, down, share):
    s = size // 4
    qa = (s // 2 + 7) // 8 * 8
    qb = s - qa
    mine = base + place * s
    nxt = base + lax.rem(place + 1, 4) * s
    opp = base + lax.rem(place + 2, 4) * s
    prv = base + lax.rem(place + 3, 4) * s
    own = data.at[rows(mine, s), :]
    to_up = links.send(own, own, up)
    to_down = links.send(own, own, down)
    share(own)
    yield
    to_up.wait_recv()
    half_a = data.at[rows(prv, qa), :]
    on_a = links.send(half_a, half_a, up)
    to_down.wait_recv()
    half_b = data.at[rows(nxt + qa, qb), :]
    on_b = links.send(half_b, half_b, down)
    share(data.at[rows(prv, s), :])
    share(data.at[rows(nxt, s), :])
    yield
    on_a.wait_recv()
    on_b.wait_recv()
    share(data.at[rows(opp, s), :])


def near_reduce(links, data, base, size, place, others, land, land_at, stage_at):
    s = size // 4
    copies = []
    for k, device in enumerate(others):
        theirs = base + lax.rem(place + 1 + k, 4) * s
        stage = stage_at + k * s

        def body(r, theirs=theirs, stage=stage):
            land[rows(stage + r, 8), :] = data[rows(theirs + r, 8), :]

        each(s // 8, 8, body)
        copies.append(links.send(land.at[pl.ds(stage, s), :], land.at[pl.ds(land_at + k * s, s), :], device))
    yield
    for copy in copies:
        copy.wait_recv()
    add_into(data, base + place * s, [(land, land_at + k * s) for k in range(3)], s, 8)


def near_gather(links, data, base, size, place, others):
    s = size // 4
    own = data.at[rows(base + place * s, s), :]
    copies = [links.send(own, own, device) for device in others]
    yield
    for copy in copies:
        copy.wait_recv()


def sum_of_four(links, data, base, size, place, others, land, land_at):
    mine = rows(land_at + place * size, size)
    land[mine, :] = data[rows(base, size), :]
    copies = [links.send(land.at[mine, :], land.at[mine, :], device) for device in others]
    yield
    for copy in copies:
        copy.wait_recv()

    def body(r):
        a, b, c, d = (land[rows(land_at + k * size + r, 8), :] for k in range(4))
        data[rows(base + r, 8), :] = (a + b) + (c + d)

    each(size // 8, 8, body)


def all_reduce(links, data, base, size, axes, land, land_at, last, last_land, last_at, source, loaded, share, near):
    (place, up, _, down), (place_2, up_2, opp_2, down_2) = axes
    others = (up_2, opp_2, down_2)
    yield from ring_reduce(links, data, base, size, place, up, down, land, land_at, source, loaded)
    part = size // 4
    at = base + place * part
    if near:
        yield from near_reduce(links, data, at, part, place_2, others, land, land_at + 3 * part, land_at + part)
    else:
        yield from ring_reduce(links, data, at, part, place_2, up_2, down_2, land, land_at + 3 * part, data, None)
    yield from last(links, data, at + place_2 * (part // 4), part // 4, last_land, last_at)
    if near:
        yield from near_gather(links, data, at, part, place_2, others)
    else:
        yield from ring_gather(links, data, at, part, place_2, up_2, down_2, lambda ref: None)
    yield from ring_gather(links, data, base, size, place, up, down, share)


def back_kernel(
    flags, pq, grads, n1_h, dh1_h, a_h, v_h, sr_h, w_h, rd_h, sn_h, sd_h, after_h, gate_h, n2_h, dh2_h,
    r1_h, r2_h, keyed_h, valued_h, recepted_h, mixed_h, chrec_h, adj_h,
    g1_h, fk_h, fv_h, fr_h, dec_h, rew_h, g2_h, ck_h, cr_h, wr_h, wk_h, wv_h, wo_h, wg_h,
    out_o, gi, vec_o, red, ff,
    front4, r1, r2, keyed, valued, recepted, mixed, chrec, adj, wr, wo, wg,
    fin, xb, gg, gb, gk, gv, gp, t0, t1, t2, other, ffland, yland, vland,
    urow, urow2, gsend, grecv, acc, rise, fade, through, expu, sums, gc, pv,
    sends, recvs, fill, ready_ring, ready_sib,
):
    dp = lax.axis_index("dp")
    tensor = lax.axis_index("tensor")
    x, z, yl = dp // 8, lax.rem(dp // 2, 4), lax.rem(dp, 2)
    h, c = tensor // 2, lax.rem(tensor, 2)
    y = 2 * h + yl

    def chip(cx, cz, cy):
        cx, cz, cy = lax.rem(cx + 4, 4), lax.rem(cz + 4, 4), lax.rem(cy + 4, 4)
        return {"dp": (cx * 4 + cz) * 2 + lax.rem(cy, 2), "tensor": (cy // 2) * 2 + c}

    xp, xo, xm = (chip(x + k, z, y) for k in (1, 2, 3))
    zp, zo, zm = (chip(x, z + k, y) for k in (1, 2, 3))
    yp, opp, ym = (chip(x, z, y + k) for k in (1, 2, 3))
    sib = {"dp": dp, "tensor": h * 2 + (1 - c)}
    pair = {"dp": dp + 1 - 2 * yl, "tensor": tensor}
    own_at, other_at = h * HALF, (1 - h) * HALF
    mine_at = c * R_ROWS

    given = (g1_h, fk_h, fv_h, fr_h, dec_h, rew_h, g2_h, ck_h, cr_h)
    g1, fk, fv, fr, dec, rew, g2, ck, cr = (pv.at[k : k + 1, :] for k in range(len(given)))
    barrier = pltpu.get_barrier_semaphore()
    partners = (xp, xo, xm, zp, zo, zm, yp, ym, opp, sib)
    for device in partners:
        pl.semaphore_signal(barrier, inc=1, device_id=device, device_id_type=MESH)

    fills = []

    def bring(src, dst):
        copy = pltpu.make_async_copy(src, dst, fill.at[len(fills)])
        copy.start()
        fills.append(copy)
        return copy

    def group(start):
        return rows(2 * start, 2 * SEG)

    PART, ARECV, CRECV, BRECV = (512 * k for k in range(4))
    part_in = [
        bring(pq.at[group(other_at + 128 * j + SEG * c), :], xb.at[pl.ds(PART + 128 * j, 128), :]) for j in range(4)
    ]
    ff_in = bring(grads, ff)
    fin_in = [
        bring(pq.at[group(own_at + 128 * j + SEG * c), :], fin.at[group(128 * j + SEG * c), :]) for j in range(4)
    ]
    pl.semaphore_wait(barrier, len(partners))

    links = Links(sends, recvs)
    ax, az, ay = (x, xp, xo, xm), (z, zp, zo, zm), (y, yp, opp, ym)

    def with_pair(links, data, base, size, land, land_at):
        whole = data.at[rows(base, size), :]
        copy = links.send(whole, land.at[pl.ds(land_at, size), :], pair)
        yield
        links.sent(copy)
        copy.wait_recv()
        add_into(data, base, [(land, land_at)], size, 8)

    def with_ring(axis):
        def last(links, data, base, size, land, land_at):
            yield from sum_of_four(links, data, base, size, axis[0], axis[1:], land, land_at)

        return last

    waited = []

    def ff_loaded():
        if not waited:
            ff_in.wait()
            waited.append(True)

    n = FF_ROWS // 4
    ffs = [
        all_reduce(
            links, ff, n * k, n, (ax, az) if k % 2 == 0 else (az, ax), ffland, n * k,
            with_pair, ffland, n * k + 15 * n // 16, grads, ff_loaded, lambda ref: None, True,
        )
        for k in range(4)
    ]

    a_in = [
        links.send(pq.at[group(other_at + 128 * j + SEG * (1 - c)), :], xb.at[pl.ds(ARECV + 128 * j, 128), :], sib)
        for j in range(4)
    ]
    c_in = [
        links.send(pq.at[group(own_at + 128 * j + SEG * (1 - c)), :], xb.at[pl.ds(CRECV + 128 * j, 128), :], sib)
        for j in range(4)
    ]
    half = pl.ds(0, HALF)
    AFTER, GATE, N2, DH2 = (HALF * k for k in range(4))
    SR, W, RD, A, V, SN, SD = (lax.rem(mine_at + HALF * k, 2 * R_ROWS) for k in range(1, 8))
    first_in = [
        bring(s.at[half, :], front4.at[pl.ds(HALF * k, HALF), :]) for k, s in enumerate((after_h, gate_h, n2_h, dh2_h))
    ]
    first_in += [bring(adj_h.at[rows(own_at, HALF), :], adj), bring(wg_h, wg), bring(r2_h.at[half, :], r2)]
    first_in += [bring(wo_h, wo)]
    second_in = [
        bring(s.at[half, :], red.at[rows(spot, HALF), :])
        for s, spot in ((a_h, A), (v_h, V), (sr_h, SR), (w_h, W), (rd_h, RD), (sn_h, SN), (sd_h, SD))
    ]
    lanes = pl.ds(pl.multiple_of(c * HALF_D, 128), HALF_D)
    third_in = [
        bring(s.at[half, lanes], d)
        for s, d in (
            (mixed_h, mixed), (chrec_h, chrec), (keyed_h, keyed), (valued_h, valued), (recepted_h, recepted),
        )
    ]
    third_in += [bring(r1_h.at[half, :], r1), bring(wr_h, wr)]
    b_in = {}

    def other_half():
        for j in (0, 3, 2, 1):
            part_in[j].wait()
            a_in[j].wait_recv()
            for at in (128 * j, 128 * j + SEG):
                add_into(xb, PART + at, [(xb, ARECV + at)], SEG)
                b_in[at] = links.send(xb.at[pl.ds(PART + at, SEG), :], xb.at[pl.ds(BRECV + at, SEG), :], opp)
                yield

    seg0 = h * (HALF // SEG)
    not_last = (1 - h).astype(F32)

    def fold(v):
        return jnp.sum(v.reshape(-1, 8, D), axis=0)

    def tally(k, v):
        acc[pl.ds(8 * k, 8), :] += fold(v)

    GAIN1, BIAS1, MIXK, MIXV, MIXR, LOGD, REW, GAIN2, BIAS2, CMIXK, CMIXR = range(NVEC)

    def take(j):
        fin_in[j].wait()
        c_in[j].wait_recv()
        b_in[128 * j].wait_recv()
        b_in[128 * j + SEG].wait_recv()
        add_into(fin, 2 * (128 * j + SEG * c), [(xb, CRECV + 128 * j), (xb, BRECV + 128 * j)], 128)
        mine = fin.at[group(128 * j + SEG * c), :]
        links.sent(b_in[128 * j])
        links.sent(b_in[128 * j + SEG])
        return links.send(mine, mine, sib)

    def gate_part(j):
        lo = 128 * j
        for seg in range(2):
            live = flags[1, seg0 + 2 * j + seg]

            def body(r, seg=seg, live=live):
                at = lo + SEG * seg + r
                gate = front4[rows(GATE + at, SUB), :]
                co = fin[rows(2 * (lo + SEG * seg) + r, SUB), :]
                res = live * (front4[rows(AFTER + at, SUB), :] + gate * co)
                front4[rows(AFTER + at, SUB), :] = res.astype(BF16).astype(F32)
                go = adj[rows(at, SUB), :].astype(F32) * live
                gg[rows(at, SUB), :] = (go * co * gate * (1.0 - gate)).astype(BF16)

            each(SEG // SUB, SUB, body)
        t0[...] = nt(gg[pl.ds(lo, 128), :], wg[...])
        for seg in range(2):

            def body2(r, seg=seg):
                at = 2 * (lo + SEG * seg) + r
                qk = fin[rows(at + SEG, SUB), :]
                qr = t0[rows(SEG * seg + r, SUB), :]
                dh2 = front4[rows(DH2 + lo + SEG * seg + r, SUB), :]
                tally(CMIXK, qk * dh2)
                tally(CMIXR, qr * dh2)
                base = qk * ck[...] + qr * cr[...]
                fin[rows(at, SUB), :] = base
                fin[rows(at + SEG, SUB), :] = (qk + qr) - base

            each(SEG // SUB, SUB, body2)

    def lifted(nxt, u):
        row = lax.broadcasted_iota(jnp.int32, u.shape, 0)
        return jnp.where(row == u.shape[0] - 1, nxt, pltpu.roll(u, u.shape[0] - 1, 0))

    def norm_back(e, n, r, gain):
        f = e * gain
        return r * (f - jnp.mean(f, axis=-1, keepdims=True) - n * jnp.mean(f * n, axis=-1, keepdims=True))

    def keep_next(seg):
        return 1.0 - flags[0, jnp.minimum(seg0 + seg + 1, NSEG - 1)]

    def walk_rows(j, edge_row, sub_body):
        for seg in (1, 0):
            s = 2 * j + seg
            live = flags[1, seg0 + s]
            for k in reversed(range(SEG // SUB)):
                lo = SEG * s + SUB * k
                at = 2 * SEG * s + SUB * k
                if lo + SUB == HALF:
                    nxt = edge_row[0:1, :] * (not_last * keep_next(s))
                elif k == SEG // SUB - 1:
                    nxt = fin[2 * SEG * (s + 1) + SEG : 2 * SEG * (s + 1) + SEG + 1, :] * keep_next(s)
                else:
                    nxt = fin[at + SEG + SUB : at + SEG + SUB + 1, :]
                sub_body(lo, at, live, nxt)

    def after_rows(lo, at, live, nxt):
        e = fin[pl.ds(at, SUB), :] + lifted(nxt, fin[pl.ds(at + SEG, SUB), :])
        n = front4[pl.ds(N2 + lo, SUB), :]
        tally(GAIN2, e * n)
        tally(BIAS2, e)
        go = adj[pl.ds(lo, SUB), :].astype(F32) * live
        ga = go + norm_back(e, n, r2[pl.ds(lo, SUB), 0:1], g2[...])
        front4[pl.ds(N2 + lo, SUB), :] = ga
        gb[pl.ds(lo, SUB), :] = ga.astype(BF16)

    def mixed_chunk(j):
        t0[...] = nt(gb[pl.ds(128 * j, 128), :], wo[...])
        for seg in (1, 0):
            total = 16 * (2 * j + seg)
            sums[pl.ds(total, 16), :] = jnp.zeros((16, D), F32)

            def body(r, seg=seg, total=total):
                at = 128 * j + SEG * seg + r
                gm = t0[rows(SEG * seg + r, SUB), :]
                sr = red[rows(SR + at, SUB), :]
                w = red[rows(W + at, SUB), :]
                gw = gm * sr
                q = gw * red[rows(RD + at, SUB), :]
                red[rows(RD + at, SUB), :] = q
                gp[rows(at, SUB), :] = (gw * w * (1.0 - sr)).astype(BF16)
                fq = fade[rows(r, SUB), :] * q
                sums[pl.ds(total, 8), :] += fold(fq)
                sums[pl.ds(total + 8, 8), :] += fold(fq * w)

            each(SEG // SUB, SUB, body)

    def chain():
        first = jnp.zeros((1, D), F32)
        second = jnp.zeros((1, D), F32)
        th = through[...]
        for s in reversed(range(8)):
            q = jnp.sum(sums[pl.ds(16 * s, 8), :], axis=0, keepdims=True)
            qw = jnp.sum(sums[pl.ds(16 * s + 8, 8), :], axis=0, keepdims=True)
            if s < 7:
                q = q + th * (first * keep_next(s))
                qw = qw + th * (second * keep_next(s))
            first, second = q, qw
        sums[0:1, :] = first
        sums[1:2, :] = second

    tri = triangle(True)

    def key_value(k, carry):
        s = 7 - k
        lo = SEG * s
        keep = 1.0 - flags[0, seg0 + s]
        for col in range(D // 128):
            cols = pl.ds(col * 128, 128)
            at = rows(lo, SEG)
            q = red[rows(RD + lo, SEG), cols]
            w = red[rows(W + lo, SEG), cols]
            a = red[rows(A + lo, SEG), cols]
            v = red[rows(V + lo, SEG), cols]
            fq = fade[:, cols] * q
            cum, both = running(tri, fq, fq * w)
            cn = through[:, cols] * gc[0:1, cols]
            cd = through[:, cols] * gc[1:2, cols]
            gn = rise[:, cols] * (cum[:, :128] + cn)
            gd = rise[:, cols] * (cum[:, 128:] + cd)
            gc[0:1, cols] = (both[0:1, :128] + cum[0:1, :128] + cn) * keep
            gc[1:2, cols] = (both[0:1, 128:] + cum[0:1, 128:] + cd) * keep
            eq = expu[:, cols] * a * q
            gvv = a * gn + eq
            gv[at, cols] = gvv.astype(BF16)
            gk[at, cols] = (v * gvv - (a * gd + eq * w)).astype(BF16)
            up = eq * (v - w)
            down = gn * red[rows(SN + lo, SEG), cols] - gd * red[rows(SD + lo, SEG), cols]
            acc[pl.ds(8 * REW, 8), cols] += jnp.sum(up.reshape(-1, 8, 128), axis=0)
            acc[pl.ds(8 * LOGD, 8), cols] += jnp.sum(down.reshape(-1, 8, 128), axis=0)
        return carry

    def weights(k, left, right):
        for col in range(D // 256):
            cols = pl.ds(256 * col, 256)
            red[rows(mine_at + HALF_D * k, HALF_D), cols] = tn(left[...], right[:, cols])

    shared = []

    def share(ref):
        if not shared:
            pl.semaphore_wait(ready_sib, 1)
        shared.append(links.send(ref, ref, sib))

    orders = ((ax, az, ay), (az, ax, ay), (ax, az, ay), (az, ax, ay), (ay, ax, az))

    def reduce_weights(k):
        if k == 0:
            pl.semaphore_wait(ready_ring, 6)
        first, second, third = orders[k]
        yield from all_reduce(
            links, red, mine_at + HALF_D * k, HALF_D, (first, second), xb, HALF_D * k,
            with_ring(third), yland, HALF_D // 4 * k, red, None, share, k in NEAR,
        )

    def front_chunk(j):
        at0 = pl.ds(128 * j, 128)
        t0[...] = nt(gk[at0, :], wk[...])
        t1[...] = nt(gv[at0, :], wv[...])
        t2[...] = nt(gp[at0, :], wr[...])
        for seg in range(2):

            def body(r, seg=seg):
                lo = 128 * j + SEG * seg
                pk, pv_, pr = (t[rows(SEG * seg + r, SUB), :] for t in (t0, t1, t2))
                dh1 = front4[rows(DH2 + lo + r, SUB), :]
                tally(MIXK, pk * dh1)
                tally(MIXV, pv_ * dh1)
                tally(MIXR, pr * dh1)
                base = pk * fk[...] + pv_ * fv[...] + pr * fr[...]
                fin[rows(2 * lo + r, SUB), :] = base
                fin[rows(2 * lo + SEG + r, SUB), :] = (pk + pv_ + pr) - base

            each(SEG // SUB, SUB, body)

    def input_rows(lo, at, live, nxt):
        e = fin[pl.ds(at, SUB), :] + lifted(nxt, fin[pl.ds(at + SEG, SUB), :])
        n = front4[pl.ds(GATE + lo, SUB), :]
        tally(GAIN1, e * n)
        tally(BIAS1, e)
        gi[rows(own_at + lo, SUB), :] = front4[pl.ds(N2 + lo, SUB), :] + norm_back(e, n, r1[pl.ds(lo, SUB), 0:1], g1[...])

    def vector_sums():
        scale = -jnp.exp(dec[...]) * jnp.exp(-jnp.exp(dec[...]))
        vec_o[...] = jnp.zeros_like(vec_o)
        for k in range(NVEC):
            total = jnp.sum(acc[pl.ds(8 * k, 8), :], axis=0, keepdims=True)
            vec_o[k : k + 1, :] = total * scale if k == LOGD else total

    def cast_rows(r):
        out_o[rows(own_at + r, SUB), :] = front4[rows(AFTER + r, SUB), :].astype(BF16)
        out_o[rows(other_at + r, SUB), :] = other[rows(r, SUB), :].astype(BF16)

    wk, wv = wg, wo

    def compute():
        for k, v in enumerate(given):
            pv[k : k + 1, :] = v[...].reshape(1, D)
        through[...] = decay_tables(dec[...], rise, fade)
        expu[...] = jnp.exp(rew[...])
        acc[...] = jnp.zeros_like(acc)
        for copy in first_in:
            copy.wait()
        yield
        for j in (0, 3, 2, 1):
            e_in = take(j)
            if j == 1:
                for device in (xp, xm, zp, zm, yp, ym):
                    pl.semaphore_signal(ready_ring, inc=1, device_id=device, device_id_type=MESH)
            yield
            e_in.wait_recv()
            links.sent(e_in)
            gate_part(j)
            if j == 0:
                gsend[...] = fin[SEG : SEG + 8, :]
                u_in = links.send(gsend, urow, opp)
            yield
            if j == 0:
                continue
            if j == 3:
                u_in.wait_recv()
                for copy in second_in:
                    copy.wait()
            if j == 1:
                wk_in = bring(wk_h, wk)
            walk_rows(j, urow, after_rows)
            mixed_chunk(j)
            yield
        walk_rows(0, urow, after_rows)
        mixed_chunk(0)
        chain()
        g_in = links.send(sums.at[pl.ds(0, 8), :], grecv, opp)
        late = [wk_in, bring(wv_h, wv), bring(n1_h.at[half, :], front4.at[pl.ds(GATE, HALF), :])]
        late.append(bring(dh1_h.at[half, :], front4.at[pl.ds(DH2, HALF), :]))
        yield
        for copy in third_in:
            copy.wait()
        weights(0, mixed, gb)
        yield
        weights(1, chrec, gg)
        yield
        g_in.wait_recv()
        edge = not_last * keep_next(7)
        gc[0:1, :] = grecv[0:1, :] * edge
        gc[1:2, :] = grecv[1:2, :] * edge
        lax.fori_loop(0, 4, key_value, 0)
        yield
        lax.fori_loop(4, 8, key_value, 0)
        pl.semaphore_signal(ready_sib, inc=1, device_id=sib, device_id_type=MESH)
        yield
        weights(2, recepted, gp)
        yield
        weights(3, keyed, gk)
        yield
        weights(4, valued, gv)
        yield
        for copy in late:
            copy.wait()
        for j in range(4):
            front_chunk(j)
            if j == 0:
                u2_in = links.send(fin.at[pl.ds(SEG, 8), :], urow2, opp)
            yield
        u2_in.wait_recv()
        for j in reversed(range(4)):
            walk_rows(j, urow2, input_rows)
            if j == 2:
                yield
        vector_sums()

    def vectors():
        for k, (place, others) in enumerate(((x, (xp, xo, xm)), (z, (zp, zo, zm)), (y, (yp, opp, ym)))):
            yield from sum_of_four(links, vec_o, 0, 16, place, others, vland, 64 * k)

    def swap(src, src_at, dst, dst_at, back_at):
        there = []
        for k in range(4):
            there.append(
                links.send(src.at[rows(src_at + SEG * k, SEG), :], dst.at[rows(dst_at + SEG * k, SEG), :], opp)
            )
            yield
        onward = []
        for k in range(4):
            there[k].wait_recv()
            theirs = dst.at[rows(back_at + SEG * k, SEG), :]
            onward.append(links.send(theirs, theirs, sib))
            yield
        for copy in onward:
            copy.wait_recv()

    def result():
        yield from swap(front4, AFTER + 256 * c, other, 256 * c, 256 * c)
        each(HALF // SUB, SUB, cast_rows)

    def input_grads():
        yield from swap(gi, own_at + 256 * c, gi, own_at + 256 * c, other_at + 256 * c)

    jobs = dict(zip("abcd", ffs))
    jobs.update(zip("pqrst", (reduce_weights(k) for k in range(MATS))))
    jobs.update(M=compute(), B=other_half(), V=vectors(), O=result(), G=input_grads())
    for name in "".join(ORDER):
        next(jobs[name], None)
        links.settle(SETTLE)
    for copy in shared:
        copy.wait_recv()
    links.finish()


def back(front_outs, adj, vecs, mats):
    g1, b1, fk, fv, fr, dec, rew, g2, b2, ck, cr = vecs
    flags, rest = front_outs[0], front_outs[1:]
    vm = pltpu.VMEM
    anywhere = pl.BlockSpec(memory_space=pl.ANY)
    vmem = pl.BlockSpec(memory_space=pltpu.VMEM)
    half = lambda dt: vm((HALF, D), dt)
    return pl.pallas_call(
        back_kernel,
        in_specs=[pl.BlockSpec(memory_space=pltpu.SMEM)] + [anywhere] * len(rest) + [anywhere]
        + [vmem] * 9 + [anywhere] * 5,
        out_specs=[vmem] * 5,
        out_shape=[vm((T, D), BF16), vm((T, D), F32), vm((16, D), F32), vm((2 * R_ROWS, D), F32), vm((FF_ROWS, D), F32)],
        scratch_shapes=[vm((4 * HALF, D), F32), vm((HALF, 128), F32), vm((HALF, 128), F32)]
        + [vm((HALF, HALF_D), BF16)] * 5 + [half(BF16)] + [vm((D, D), BF16)] * 3
        + [vm((2 * HALF, D), F32), vm((R_ROWS, D), F32)]
        + [half(BF16)] * 5 + [vm((128, D), F32)] * 3 + [half(F32)]
        + [vm((FF_ROWS, D), F32), vm((R_ROWS // 4, D), F32), vm((192, D), F32)]
        + [vm((8, D), F32)] * 4 + [vm((8 * NVEC, D), F32)] + [vm((SEG, D), F32)] * 2
        + [vm((1, D), F32)] * 2 + [vm((128, D), F32), vm((8, D), F32), vm((16, D), F32)]
        + [pltpu.SemaphoreType.DMA((COPIES,)), pltpu.SemaphoreType.DMA((COPIES,)),
           pltpu.SemaphoreType.DMA((48,)), pltpu.SemaphoreType.REGULAR, pltpu.SemaphoreType.REGULAR],
        compiler_params=pltpu.CompilerParams(collective_id=1, has_side_effects=True, vmem_limit_bytes=BACK_VMEM * 2**20),
        cost_estimate=pl.CostEstimate(flops=14 * T * D * D, bytes_accessed=60 * 2**20, transcendentals=0),
        name="back",
    )(flags, *rest, adj, g1, fk, fv, fr, dec, rew, g2, ck, cr, *mats[:5])


def finish_kernel(out, gi, vec, red, ff, *refs):
    out_o, gi_o, mats, ck_o, cv_o, vecs, sems = refs[0], refs[1], refs[2:7], refs[7], refs[8], refs[9:20], refs[20]
    pairs = [(gi, gi_o), (ff.at[pl.ds(0, D), :], ck_o), (ff.at[pl.ds(D, D), :], cv_o), (out, out_o)]
    for k in range(MATS):
        for core in range(2):
            src = red.at[pl.ds(core * R_ROWS + HALF_D * k, HALF_D), :]
            pairs.append((src, mats[(3, 4, 0, 1, 2)[k]].at[pl.ds(HALF_D * core, HALF_D), :]))
    copies = [pltpu.make_async_copy(src, dst, sems.at[k]) for k, (src, dst) in enumerate(pairs)]
    for copy in copies:
        copy.start()
    for k in range(NVEC):
        vecs[k][...] = vec[k : k + 1, :].reshape(D)
    for copy in copies:
        copy.wait()


def finish(out, gi, vec, red, ff):
    sds = jax.ShapeDtypeStruct
    anywhere = pl.BlockSpec(memory_space=pl.ANY)
    vmem = pl.BlockSpec(memory_space=pltpu.VMEM)
    return pl.pallas_call(
        finish_kernel,
        in_specs=[vmem] * 5,
        out_specs=[anywhere] * 9 + [vmem] * NVEC,
        out_shape=[sds((T, D), BF16), sds((T, D), F32)] + [sds((D, D), F32)] * 7 + [sds((D,), F32)] * NVEC,
        scratch_shapes=[pltpu.SemaphoreType.DMA((16,))],
        compiler_params=pltpu.CompilerParams(vmem_limit_bytes=FINISH_VMEM * 2**20),
        name="finish",
    )(out, gi, vec, red, ff)


def body(
    entering_activations, sample_sizes, initial_layernorm_scale, initial_layernorm_offset, temporal_lookup_fraction,
    temporal_content_fraction, temporal_gating_fraction, fading_speed_logarithm, present_reward,
    temporal_gating_matrix, temporal_lookup_matrix, temporal_content_matrix, temporal_emission_matrix,
    latter_layernorm_scale, latter_layernorm_offset, feedforward_lookup_fraction, feedforward_gating_fraction,
    feedforward_gating_matrix, feedforward_lookup_matrix, feedforward_content_matrix, upstream_adjoint,
):
    vecs = (
        initial_layernorm_scale, initial_layernorm_offset, temporal_lookup_fraction, temporal_content_fraction,
        temporal_gating_fraction, fading_speed_logarithm, present_reward, latter_layernorm_scale,
        latter_layernorm_offset, feedforward_lookup_fraction, feedforward_gating_fraction,
    )
    mats = (
        temporal_gating_matrix, temporal_lookup_matrix, temporal_content_matrix, temporal_emission_matrix,
        feedforward_gating_matrix, feedforward_lookup_matrix, feedforward_content_matrix,
    )
    half = (lax.axis_index("tensor") // 2).astype(jnp.int32).reshape(1)
    fronts = front(half, sample_sizes, entering_activations, upstream_adjoint, vecs, mats)
    out, grad_inputs, recw, keyw, valw, outw, chrec, chkey, chval, *g = finish(*back(fronts, upstream_adjoint, vecs, mats))
    return (
        out, grad_inputs, g[0], g[1], g[2], g[3], g[4], g[5], g[6], recw, keyw, valw, outw,
        g[7], g[8], g[9], g[10], chrec, chkey, chval,
    )


def solution(mesh):
    split = P("dp", None)
    in_specs = (split, split) + (P(),) * 16 + (P(None, "tensor"), P("tensor", None), split)
    out_specs = (split, split) + (P(),) * 16 + (P(None, "tensor"), P("tensor", None))
    return jax.shard_map(body, mesh=mesh, in_specs=in_specs, out_specs=out_specs, check_vma=False)
```

```python
import functools

import jax
import jax.numpy as jnp
from jax import lax
from jax.experimental import pallas as pl
from jax.experimental.pallas import tpu as pltpu
from jax.sharding import PartitionSpec as P

F32 = jnp.float32
BF16 = jnp.bfloat16
EPSILON = 1e-05
SEG = 64
D = 768
T = 1024
HALF = 512
HALF_D = D // 2
BLK = 512
SUB = 32
NSEG = T // SEG
PER = HALF // BLK
SLOTS = PER


def nn(left, right):
    return jnp.dot(left, right, preferred_element_type=F32)


def nt(left, right):
    return lax.dot_general(left, right, (((1,), (1,)), ((), ())), preferred_element_type=F32)


def tn(left, right):
    return lax.dot_general(left, right, (((0,), (0,)), ((), ())), preferred_element_type=F32)


def normalize(v):
    c = v - jnp.mean(v, axis=-1, keepdims=True)
    r = lax.rsqrt(jnp.mean(c * c, axis=-1, keepdims=True) + EPSILON)
    return c * r, r


def roll_down(v, first):
    row = lax.broadcasted_iota(jnp.int32, v.shape, 0)
    return jnp.where(row == 0, first, pltpu.roll(v, 1, 0))


def two_parts(v):
    hi = v.astype(BF16)
    return hi, (v - hi.astype(F32)).astype(BF16)


def triangle(upper):
    row = lax.broadcasted_iota(jnp.int32, (SEG, 2 * SEG), 0)
    col = lax.broadcasted_iota(jnp.int32, (SEG, 2 * SEG), 1)
    col = jnp.where(col >= SEG, col - SEG, col)
    keep = (col > row) if upper else (col < row)
    return jnp.where(keep, 1.0, 0.0).astype(BF16)


def running(tri, first, second):
    both = jnp.concatenate([first, second], axis=1)
    hi, lo = two_parts(both)
    return nn(tri, jnp.concatenate([hi, lo], axis=0)), both


def decay_tables(dec, rise, fade):
    rate = jnp.exp(dec)
    offs = lax.broadcasted_iota(jnp.int32, (SEG, D), 0).astype(F32)
    rise[...] = jnp.exp((offs + 1.0) * rate)
    fade[...] = jnp.exp(-offs * rate)
    return jnp.exp(-float(SEG) * rate)


def spread(dst, first, cols, v):
    for s in range(v.shape[0] // SEG):
        dst[first + 2 * SEG * s : first + 2 * SEG * s + SEG, cols] = v[SEG * s : SEG * (s + 1), :]


def weave(products, others):
    done = 0
    for k, product in enumerate(products):
        product()
        upto = len(others) * (k + 1) // len(products)
        for other in others[done:upto]:
            other()
        done = upto
    for other in others[done:]:
        other()


def front_kernel(
    half_ref, len_ref, x_ref, adj_ref, g1_h, b1_h, fk_h, fv_h, fr_h, dec_h, rew_h, g2_h, b2_h, ck_h, cr_h,
    wr_h, wk_h, wv_h, wo_h, wg_h, wfk_h, wfv_h,
    flags, pq, grads, n1_h, dh1_h, a_h, v_h, sr_h, w_h, rd_h, sn_h, sd_h, after_h, gate_h, n2_h, dh2_h,
    r1_h, r2_h, keyed_h, valued_h, recepted_h, mixed_h, chrec_h,
    wr, wk, wv, wo, wg, wfk, wfv, wide, narrow, low, gbuf,
    rise, fade, through, expu, nc, dc, p1, p2, kb, vb, rb, hb, cks_all, hid_all, gch_all, gpr_all, pv, win, outs, gsem,
):
    i = pl.program_id(0)
    slot = lax.rem(i, SLOTS) if SLOTS > 1 else 0
    cks, hid, gch, gpr = (ref.at[i] for ref in (cks_all, hid_all, gch_all, gpr_all))
    given = (g1_h, b1_h, fk_h, fv_h, fr_h, dec_h, rew_h, g2_h, b2_h, ck_h, cr_h)
    g1, b1, fk, fv, fr, dec, rew, g2, b2, ck, cr = (pv.at[k : k + 1, :] for k in range(len(given)))
    n1_o, dh1_o, a_o, v_o, sr_o, w_o, rd_o, sn_o, sd_o, after_o, gate_o, n2_o, dh2_o = (
        wide.at[slot, k] for k in range(13)
    )
    r1_o, r2_o = (narrow.at[slot, k] for k in range(2))
    keyed_o, valued_o, recepted_o, mixed_o, chrec_o = (low.at[slot, k] for k in range(5))
    loads = [
        pltpu.make_async_copy(src, dst, win.at[k])
        for k, (src, dst) in enumerate(
            ((wk_h, wk), (wv_h, wv), (wr_h, wr), (wo_h, wo), (wfk_h, wfk), (wg_h, wg), (wfv_h, wfv))
        )
    ]
    kept = pl.ds(pl.multiple_of(lax.rem(i, PER) * BLK, BLK), BLK)
    held = (
        (wide, 0, n1_h), (wide, 1, dh1_h), (narrow, 0, r1_h), (low, 0, keyed_h), (low, 1, valued_h), (low, 2, recepted_h),
        (wide, 2, a_h), (wide, 3, v_h), (wide, 4, sr_h), (wide, 5, w_h), (wide, 6, rd_h), (wide, 7, sn_h),
        (wide, 8, sd_h), (low, 3, mixed_h),
        (wide, 9, after_h), (wide, 11, n2_h), (wide, 12, dh2_h), (narrow, 1, r2_h), (low, 4, chrec_h),
        (wide, 10, gate_h),
    )

    def saves(at):
        return [
            pltpu.make_async_copy(src.at[at, n], dst.at[kept, :], outs.at[at, k])
            for k, (src, n, dst) in enumerate(held)
        ]

    def save(lo, hi):
        @pl.when(i // PER == half_ref[0])
        def _():
            for copy in saves(slot)[lo:hi]:
                copy.start()

    def loaded(lo, hi):
        @pl.when(i == 0)
        def _():
            for copy in loads[lo:hi]:
                copy.wait()

    @pl.when(i == 0)
    def _():
        for copy in loads:
            copy.start()

    def reuse(lo, hi):
        @pl.when((i >= PER) & (half_ref[0] == 0))
        def _():
            for copy in saves(slot)[lo:hi]:
                copy.wait()

    reuse(0, 6)
    @pl.when(i == 0)
    def _():
        for b in range(NSEG):
            flags[0, b] = 0.0
        begin = jnp.int32(0)
        for j in range(NSEG):
            size = len_ref[0, j]
            at = lax.shift_right_logical(begin, 6)

            @pl.when(size > 0)
            def _():
                flags[0, at] = 1.0

            begin = begin + size
        for b in range(NSEG):
            flags[1, b] = jnp.where(b * SEG < begin, 1.0, 0.0)
        for k, v in enumerate(given):
            pv[k : k + 1, :] = v[...].reshape(1, D)
        through[...] = decay_tables(dec[...], rise, fade)
        expu[...] = jnp.exp(rew[...])
        nc[...] = jnp.zeros_like(nc)
        dc[...] = jnp.zeros_like(dc)
        p1[...] = jnp.zeros_like(p1)
        p2[...] = jnp.zeros_like(p2)

    fresh = [flags[0, i * (BLK // SEG) + s] for s in range(BLK // SEG)]
    live = [flags[1, i * (BLK // SEG) + s] for s in range(BLK // SEG)]

    tri = triangle(False)
    part = BLK // 2
    subs = part // SUB
    segs = part // SEG
    col_tiles = [pl.ds(0, D)]

    def first_norm(s):
        at = pl.ds(s * SUB, SUB)
        n1, r1 = normalize(x_ref[at, :].astype(F32))
        h1 = n1 * g1[...] + b1[...]
        before = p1[...]
        if (s * SUB) % SEG == 0:
            before = before * (1.0 - fresh[s * SUB // SEG])
        sh = roll_down(h1, before)
        p1[...] = h1[SUB - 1 :, :]
        dh1 = h1 - sh
        keyed_o[at, :] = (sh + dh1 * fk[...]).astype(BF16)
        valued_o[at, :] = (sh + dh1 * fv[...]).astype(BF16)
        recepted_o[at, :] = (sh + dh1 * fr[...]).astype(BF16)
        n1_o[at, :] = n1
        dh1_o[at, :] = dh1
        r1_o[at, :] = jnp.broadcast_to(r1, (SUB, 128))

    def mix_time(s, c):
        at = pl.ds(s * SEG, SEG)
        keep = 1.0 - fresh[s]
        cols = pl.ds(c * 128, 128)
        a = jnp.exp(kb[at, cols])
        v = vb[at, cols]
        lift = rise[:, cols] * a
        cum, both = running(tri, lift * v, lift)
        ncar = nc[:, cols] * keep
        dcar = dc[:, cols] * keep
        sn = fade[:, cols] * (ncar + cum[:, :128])
        sd = fade[:, cols] * (dcar + cum[:, 128:])
        th = through[:, cols]
        nc[:, cols] = th * (ncar + (cum[SEG - 1 :, :128] + both[SEG - 1 :, :128]))
        dc[:, cols] = th * (dcar + (cum[SEG - 1 :, 128:] + both[SEG - 1 :, 128:]))
        e = expu[:, cols] * a
        rd = 1.0 / (sd + e)
        w = (sn + e * v) * rd
        sr = jax.nn.sigmoid(rb[at, cols])
        mixed_o[at, cols] = (sr * w).astype(BF16)
        a_o[at, cols] = a
        v_o[at, cols] = v
        sr_o[at, cols] = sr
        w_o[at, cols] = w
        rd_o[at, cols] = rd
        sn_o[at, cols] = sn
        sd_o[at, cols] = sd

    def second_norm(s):
        at = pl.ds(s * SUB, SUB)
        after = x_ref[at, :].astype(F32) + hb[at, :]
        n2, r2 = normalize(after)
        h2 = n2 * g2[...] + b2[...]
        before = p2[...]
        if (s * SUB) % SEG == 0:
            before = before * (1.0 - fresh[s * SUB // SEG])
        sh = roll_down(h2, before)
        p2[...] = h2[SUB - 1 :, :]
        dh2 = h2 - sh
        cks[at, :] = (sh + dh2 * ck[...]).astype(BF16)
        chrec_o[at, :] = (sh + dh2 * cr[...]).astype(BF16)
        after_o[at, :] = after
        n2_o[at, :] = n2
        dh2_o[at, :] = dh2
        r2_o[at, :] = jnp.broadcast_to(r2, (SUB, 128))

    def gates(s):
        at = pl.ds(s * SUB, SUB)
        hp = jnp.maximum(kb[at, :], 0.0)
        hid[at, :] = (hp * hp).astype(BF16)
        gate = jax.nn.sigmoid(rb[at, :])
        gate_o[at, :] = gate
        go = adj_ref[at, :].astype(F32) * live[s * SUB // SEG]
        gch[at, :] = (go * gate).astype(BF16)

    def hidden_grads(s):
        at = pl.ds(s * SUB, SUB)
        gpr[at, :] = (2.0 * jnp.maximum(kb[at, :], 0.0) * vb[at, :]).astype(BF16)

    def all_of(fn, p, count):
        return [functools.partial(fn, p * count + k) for k in range(count)]

    def times(p, dst, left, right):
        at = pl.ds(p * part, part)

        def piece(cols):
            dst[at, cols] = nn(left[at, :], right[:, cols])

        return [functools.partial(piece, cols) for cols in col_tiles]

    def times_turned(p, dst, left, right):
        at = pl.ds(p * part, part)

        def piece(cols):
            dst[at, cols] = nt(left[at, :], right[cols, :])

        return [functools.partial(piece, cols) for cols in col_tiles]

    def to_pq(p, first, product, left, right):
        at = pl.ds(p * part, part)

        def piece(cols):
            v = nn(left[at, :], right[:, cols]) if product is nn else nt(left[at, :], right[cols, :])
            spread(pq, 2 * p * part + first, cols, v)

        return [functools.partial(piece, cols) for cols in col_tiles]

    def projections(p):
        return times(p, kb, keyed_o, wk) + times(p, vb, valued_o, wv) + times(p, rb, recepted_o, wr)

    def mixing(p):
        return [functools.partial(mix_time, p * segs + s, c) for s in range(segs) for c in range(D // 128)]

    def hidden(p):
        return times(p, kb, cks, wfk) + times(p, rb, chrec_o, wg)

    def outward(p):
        return to_pq(p, 0, nn, hid, wfv) + times_turned(p, vb, gch, wfv)

    weave([], all_of(first_norm, 0, subs))
    loaded(0, 3)
    weave(projections(0), all_of(first_norm, 1, subs))
    save(0, 6)
    reuse(6, 14)
    loaded(3, 4)
    weave(projections(1), mixing(0))
    weave(times(0, hb, mixed_o, wo), mixing(1))
    save(6, 14)
    reuse(14, 20)
    loaded(4, 7)
    weave(times(1, hb, mixed_o, wo), all_of(second_norm, 0, subs))
    weave(hidden(0), all_of(second_norm, 1, subs))
    save(14, 19)
    weave(hidden(1), all_of(gates, 0, subs))
    weave(outward(0), all_of(gates, 1, subs))
    save(19, 20)
    weave(outward(1), all_of(hidden_grads, 0, subs))
    weave(to_pq(0, SEG, nt, gpr, wfk), all_of(hidden_grads, 1, subs))
    weave(to_pq(1, SEG, nt, gpr, wfk), [])

    @pl.when(i == T // BLK - 1)
    def _():
        out_copies = []
        for k, (left, right) in enumerate(((cks_all, gpr_all), (hid_all, gch_all))):
            for c in range(D // 256):
                at = pl.ds(D * k + 256 * c, 256)
                gbuf[at, :] = tn(left[:, :, pl.ds(256 * c, 256)].reshape(T, 256), right[...].reshape(T, D))
                out_copies.append(pltpu.make_async_copy(gbuf.at[at, :], grads.at[at, :], gsem.at[3 * k + c]))
                out_copies[-1].start()
        for copy in out_copies:
            copy.wait()

    @pl.when((i == T // BLK - 1) & (half_ref[0] == 1))
    def _():
        for s in range(SLOTS):
            for copy in saves(s):
                copy.wait()


def front(half, sizes, x, adj, vecs, mats):
    steps = T // BLK
    blk = lambda w: pl.BlockSpec((BLK, w), lambda i, h: (i, 0))
    vec = pl.BlockSpec((D,), lambda i, h: (0,))
    anywhere = pl.BlockSpec(memory_space=pl.ANY)
    sds = jax.ShapeDtypeStruct
    vm = pltpu.VMEM
    return pl.pallas_call(
        front_kernel,
        grid_spec=pltpu.PrefetchScalarGridSpec(
            num_scalar_prefetch=1,
            grid=(steps,),
            in_specs=[pl.BlockSpec(memory_space=pltpu.SMEM), blk(D), blk(D)] + [vec] * 11 + [anywhere] * 7,
            out_specs=[pl.BlockSpec(memory_space=pltpu.SMEM), pl.BlockSpec((2 * BLK, D), lambda i, h: (i, 0))]
            + [anywhere] * 21,
            scratch_shapes=[vm((D, D), BF16)] * 7
            + [vm((SLOTS, 13, BLK, D), F32), vm((SLOTS, 2, BLK, 128), F32), vm((SLOTS, 5, BLK, D), BF16), vm((2 * D, D), F32)]
            + [vm((SEG, D), F32)] * 2 + [vm((1, D), F32)] * 6 + [vm((BLK, D), F32)] * 4
            + [vm((T // BLK, BLK, D), BF16)] * 4 + [vm((16, D), F32)]
            + [pltpu.SemaphoreType.DMA((7,)), pltpu.SemaphoreType.DMA((SLOTS, 20)), pltpu.SemaphoreType.DMA((6,))],
        ),
        out_shape=[sds((2, NSEG), F32), sds((2 * T, D), F32), sds((2 * D, D), F32)]
        + [sds((HALF, D), F32)] * 13 + [sds((HALF, 128), F32)] * 2 + [sds((HALF, D), BF16)] * 5,
        compiler_params=pltpu.CompilerParams(dimension_semantics=("arbitrary",), vmem_limit_bytes=62 * 2**20),
        cost_estimate=pl.CostEstimate(flops=11 * 2 * T * D * D, bytes_accessed=60 * 2**20, transcendentals=4 * T * D),
        name="front",
    )(half, sizes, x, adj, *vecs, *mats)


MESH = pl.DeviceIdType.MESH
COPIES = 256
FF_ROWS = 2 * D
R_ROWS = 2048
MATS = 5
BACK_VMEM = 39
FINISH_VMEM = 2
SETTLE = 14
NEAR = (0, 1, 2, 3, 4)
ORDER = (
    "daBBacBdaBBdMMbaMMcdBbMdBBacbMdMaMbMcMbcaMMMOMpM",
    "qMOMMMrMtsMpMqsObMOrMtqpscrqbsOdMtapqOrsMcOtGOpG",
    "rtVsGrptOqVGrsGGdqGctVbpGtGrspqV",
)
NVEC = 11


def rows(start, size):
    return pl.ds(pl.multiple_of(start, 8), size)


def each(count, step, body, reverse=False):
    def run(k, carry):
        body((count - 1 - k) * step if reverse else k * step)
        return carry

    lax.fori_loop(0, count, run, 0)


class Links:
    def __init__(self, sends, recvs):
        self.sends, self.recvs, self.used, self.open, self.step = sends, recvs, 0, [], 0

    def send(self, src, dst, device):
        k = self.used
        self.used += 1
        copy = pltpu.make_async_remote_copy(
            src_ref=src, dst_ref=dst, send_sem=self.sends.at[k], recv_sem=self.recvs.at[k],
            device_id=device, device_id_type=MESH,
        )
        copy.start()
        self.open.append((self.step, copy))
        return copy

    def sent(self, copy):
        if all(kept[1] is not copy for kept in self.open):
            return
        self.open = [kept for kept in self.open if kept[1] is not copy]
        copy.wait_send()

    def settle(self, steps):
        while self.open and self.open[0][0] < self.step - steps:
            self.open.pop(0)[1].wait_send()
        self.step += 1

    def finish(self):
        for _, copy in self.open:
            copy.wait_send()


def add_into(dst, dst_at, terms, size, step=16):
    if size % step:
        step = 8

    def body(r):
        total = dst[rows(dst_at + r, step), :]
        for ref, start in terms:
            total = total + ref[rows(start + r, step), :]
        dst[rows(dst_at + r, step), :] = total

    each(size // step, step, body)


def ring_reduce(links, data, base, size, place, up, down, land, land_at, source, loaded):
    s = size // 4
    qa = (s // 2 + 7) // 8 * 8
    qb = s - qa
    mine = base + place * s
    nxt = base + lax.rem(place + 1, 4) * s
    opp = base + lax.rem(place + 2, 4) * s
    prv = base + lax.rem(place + 3, 4) * s
    starts = [land_at]
    for size_k in (qa, qb, qb, qa, qa, qb):
        starts.append(starts[-1] + size_k)
    spot = [land.at[pl.ds(a, b - a), :] for a, b in zip(starts, starts[1:])]
    fwd_a = links.send(source.at[rows(opp, qa), :], spot[0], up)
    fwd_b = links.send(source.at[rows(opp + qa, qb), :], spot[1], down)
    dir_b = links.send(source.at[rows(nxt + qa, qb), :], spot[2], up)
    dir_a = links.send(source.at[rows(prv, qa), :], spot[3], down)
    yield
    if loaded is not None:
        loaded()
    fwd_a.wait_recv()
    add_into(land, starts[0], [(data, nxt)], qa)
    cmb_a = links.send(spot[0], spot[4], up)
    fwd_b.wait_recv()
    add_into(land, starts[1], [(data, prv + qa)], qb)
    for copy in (fwd_a, fwd_b, dir_b, dir_a):
        links.sent(copy)
    cmb_b = links.send(spot[1], spot[5], down)
    yield
    dir_a.wait_recv()
    dir_b.wait_recv()
    cmb_a.wait_recv()
    cmb_b.wait_recv()
    add_into(data, mine, [(land, starts[3]), (land, starts[4])], qa)
    add_into(data, mine + qa, [(land, starts[2]), (land, starts[5])], qb)


def ring_gather(links, data, base, size, place, up, down, share):
    s = size // 4
    qa = (s // 2 + 7) // 8 * 8
    qb = s - qa
    mine = base + place * s
    nxt = base + lax.rem(place + 1, 4) * s
    opp = base + lax.rem(place + 2, 4) * s
    prv = base + lax.rem(place + 3, 4) * s
    own = data.at[rows(mine, s), :]
    to_up = links.send(own, own, up)
    to_down = links.send(own, own, down)
    share(own)
    yield
    to_up.wait_recv()
    half_a = data.at[rows(prv, qa), :]
    on_a = links.send(half_a, half_a, up)
    to_down.wait_recv()
    half_b = data.at[rows(nxt + qa, qb), :]
    on_b = links.send(half_b, half_b, down)
    share(data.at[rows(prv, s), :])
    share(data.at[rows(nxt, s), :])
    yield
    on_a.wait_recv()
    on_b.wait_recv()
    share(data.at[rows(opp, s), :])


def near_reduce(links, data, base, size, place, others, land, land_at, stage_at):
    s = size // 4
    copies = []
    for k, device in enumerate(others):
        theirs = base + lax.rem(place + 1 + k, 4) * s
        stage = stage_at + k * s

        def body(r, theirs=theirs, stage=stage):
            land[rows(stage + r, 8), :] = data[rows(theirs + r, 8), :]

        each(s // 8, 8, body)
        copies.append(links.send(land.at[pl.ds(stage, s), :], land.at[pl.ds(land_at + k * s, s), :], device))
    yield
    for copy in copies:
        copy.wait_recv()
    add_into(data, base + place * s, [(land, land_at + k * s) for k in range(3)], s, 8)


def near_gather(links, data, base, size, place, others):
    s = size // 4
    own = data.at[rows(base + place * s, s), :]
    copies = [links.send(own, own, device) for device in others]
    yield
    for copy in copies:
        copy.wait_recv()


def sum_of_four(links, data, base, size, place, others, land, land_at):
    mine = rows(land_at + place * size, size)
    land[mine, :] = data[rows(base, size), :]
    copies = [links.send(land.at[mine, :], land.at[mine, :], device) for device in others]
    yield
    for copy in copies:
        copy.wait_recv()

    def body(r):
        a, b, c, d = (land[rows(land_at + k * size + r, 8), :] for k in range(4))
        data[rows(base + r, 8), :] = (a + b) + (c + d)

    each(size // 8, 8, body)


def all_reduce(links, data, base, size, axes, land, land_at, last, last_land, last_at, source, loaded, share, near):
    (place, up, _, down), (place_2, up_2, opp_2, down_2) = axes
    others = (up_2, opp_2, down_2)
    yield from ring_reduce(links, data, base, size, place, up, down, land, land_at, source, loaded)
    part = size // 4
    at = base + place * part
    if near:
        yield from near_reduce(links, data, at, part, place_2, others, land, land_at + 3 * part, land_at + part)
    else:
        yield from ring_reduce(links, data, at, part, place_2, up_2, down_2, land, land_at + 3 * part, data, None)
    yield from last(links, data, at + place_2 * (part // 4), part // 4, last_land, last_at)
    if near:
        yield from near_gather(links, data, at, part, place_2, others)
    else:
        yield from ring_gather(links, data, at, part, place_2, up_2, down_2, lambda ref: None)
    yield from ring_gather(links, data, base, size, place, up, down, share)


def back_kernel(
    flags, pq, grads, n1_h, dh1_h, a_h, v_h, sr_h, w_h, rd_h, sn_h, sd_h, after_h, gate_h, n2_h, dh2_h,
    r1_h, r2_h, keyed_h, valued_h, recepted_h, mixed_h, chrec_h, adj_h,
    g1_h, fk_h, fv_h, fr_h, dec_h, rew_h, g2_h, ck_h, cr_h, wr_h, wk_h, wv_h, wo_h, wg_h,
    out_o, gi, vec_o, red, ff,
    front4, r1, r2, keyed, valued, recepted, mixed, chrec, adj, wr, wo, wg,
    fin, xb, gg, gb, gk, gv, gp, t0, t1, t2, other, ffland, yland, vland,
    urow, urow2, gsend, grecv, acc, rise, fade, through, expu, sums, gc, pv,
    sends, recvs, fill, ready_ring, ready_sib,
):
    dp = lax.axis_index("dp")
    tensor = lax.axis_index("tensor")
    x, z, yl = dp // 8, lax.rem(dp // 2, 4), lax.rem(dp, 2)
    h, c = tensor // 2, lax.rem(tensor, 2)
    y = 2 * h + yl

    def chip(cx, cz, cy):
        cx, cz, cy = lax.rem(cx + 4, 4), lax.rem(cz + 4, 4), lax.rem(cy + 4, 4)
        return {"dp": (cx * 4 + cz) * 2 + lax.rem(cy, 2), "tensor": (cy // 2) * 2 + c}

    xp, xo, xm = (chip(x + k, z, y) for k in (1, 2, 3))
    zp, zo, zm = (chip(x, z + k, y) for k in (1, 2, 3))
    yp, opp, ym = (chip(x, z, y + k) for k in (1, 2, 3))
    sib = {"dp": dp, "tensor": h * 2 + (1 - c)}
    pair = {"dp": dp + 1 - 2 * yl, "tensor": tensor}
    own_at, other_at = h * HALF, (1 - h) * HALF
    mine_at = c * R_ROWS

    given = (g1_h, fk_h, fv_h, fr_h, dec_h, rew_h, g2_h, ck_h, cr_h)
    g1, fk, fv, fr, dec, rew, g2, ck, cr = (pv.at[k : k + 1, :] for k in range(len(given)))
    barrier = pltpu.get_barrier_semaphore()
    partners = (xp, xo, xm, zp, zo, zm, yp, ym, opp, sib)
    for device in partners:
        pl.semaphore_signal(barrier, inc=1, device_id=device, device_id_type=MESH)

    fills = []

    def bring(src, dst):
        copy = pltpu.make_async_copy(src, dst, fill.at[len(fills)])
        copy.start()
        fills.append(copy)
        return copy

    def group(start):
        return rows(2 * start, 2 * SEG)

    PART, ARECV, CRECV, BRECV = (512 * k for k in range(4))
    part_in = [
        bring(pq.at[group(other_at + 128 * j + SEG * c), :], xb.at[pl.ds(PART + 128 * j, 128), :]) for j in range(4)
    ]
    ff_in = bring(grads, ff)
    pl.semaphore_wait(barrier, len(partners))

    links = Links(sends, recvs)
    ax, az, ay = (x, xp, xo, xm), (z, zp, zo, zm), (y, yp, opp, ym)

    def with_pair(links, data, base, size, land, land_at):
        whole = data.at[rows(base, size), :]
        copy = links.send(whole, land.at[pl.ds(land_at, size), :], pair)
        yield
        links.sent(copy)
        copy.wait_recv()
        add_into(data, base, [(land, land_at)], size, 8)

    def with_ring(axis):
        def last(links, data, base, size, land, land_at):
            yield from sum_of_four(links, data, base, size, axis[0], axis[1:], land, land_at)

        return last

    waited = []

    def ff_loaded():
        if not waited:
            ff_in.wait()
            waited.append(True)

    n = FF_ROWS // 4
    ffs = [
        all_reduce(
            links, ff, n * k, n, (ax, az) if k % 2 == 0 else (az, ax), ffland, n * k,
            with_pair, ffland, n * k + 15 * n // 16, grads, ff_loaded, lambda ref: None, True,
        )
        for k in range(4)
    ]

    a_in = [
        links.send(pq.at[group(other_at + 128 * j + SEG * (1 - c)), :], xb.at[pl.ds(ARECV + 128 * j, 128), :], sib)
        for j in range(4)
    ]
    AFTER, GATE, N2, DH2 = (HALF * k for k in range(4))
    SR, W, RD, A, V, SN, SD = (lax.rem(mine_at + HALF * k, 2 * R_ROWS) for k in range(1, 8))
    lanes = pl.ds(pl.multiple_of(c * HALF_D, 128), HALF_D)
    half = pl.ds(0, HALF)
    b_in = {}
    c_in = []
    fin_in = []

    def other_half():
        for j in (0, 3, 2, 1):
            part_in[j].wait()
            a_in[j].wait_recv()
            for at in (128 * j, 128 * j + SEG):
                add_into(xb, PART + at, [(xb, ARECV + at)], SEG)
                b_in[at] = links.send(xb.at[pl.ds(PART + at, SEG), :], xb.at[pl.ds(BRECV + at, SEG), :], opp)
                yield

    seg0 = h * (HALF // SEG)
    not_last = (1 - h).astype(F32)

    def fold(v):
        return jnp.sum(v.reshape(-1, 8, D), axis=0)

    def tally(k, v):
        acc[pl.ds(8 * k, 8), :] += fold(v)

    GAIN1, BIAS1, MIXK, MIXV, MIXR, LOGD, REW, GAIN2, BIAS2, CMIXK, CMIXR = range(NVEC)

    def take(j):
        fin_in[j].wait()
        c_in[j].wait_recv()
        b_in[128 * j].wait_recv()
        b_in[128 * j + SEG].wait_recv()
        add_into(fin, 2 * (128 * j + SEG * c), [(xb, CRECV + 128 * j), (xb, BRECV + 128 * j)], 128)
        mine = fin.at[group(128 * j + SEG * c), :]
        links.sent(b_in[128 * j])
        links.sent(b_in[128 * j + SEG])
        return links.send(mine, mine, sib)

    def gate_part(j):
        lo = 128 * j
        for seg in range(2):
            live = flags[1, seg0 + 2 * j + seg]

            def body(r, seg=seg, live=live):
                at = lo + SEG * seg + r
                gate = front4[rows(GATE + at, SUB), :]
                co = fin[rows(2 * (lo + SEG * seg) + r, SUB), :]
                res = live * (front4[rows(AFTER + at, SUB), :] + gate * co)
                front4[rows(AFTER + at, SUB), :] = res.astype(BF16).astype(F32)
                go = adj[rows(at, SUB), :].astype(F32) * live
                gg[rows(at, SUB), :] = (go * co * gate * (1.0 - gate)).astype(BF16)

            each(SEG // SUB, SUB, body)
        t0[...] = nt(gg[pl.ds(lo, 128), :], wg[...])
        for seg in range(2):

            def body2(r, seg=seg):
                at = 2 * (lo + SEG * seg) + r
                qk = fin[rows(at + SEG, SUB), :]
                qr = t0[rows(SEG * seg + r, SUB), :]
                dh2 = front4[rows(DH2 + lo + SEG * seg + r, SUB), :]
                tally(CMIXK, qk * dh2)
                tally(CMIXR, qr * dh2)
                base = qk * ck[...] + qr * cr[...]
                fin[rows(at, SUB), :] = base
                fin[rows(at + SEG, SUB), :] = (qk + qr) - base

            each(SEG // SUB, SUB, body2)

    def lifted(nxt, u):
        row = lax.broadcasted_iota(jnp.int32, u.shape, 0)
        return jnp.where(row == u.shape[0] - 1, nxt, pltpu.roll(u, u.shape[0] - 1, 0))

    def norm_back(e, n, r, gain):
        f = e * gain
        return r * (f - jnp.mean(f, axis=-1, keepdims=True) - n * jnp.mean(f * n, axis=-1, keepdims=True))

    def keep_next(seg):
        return 1.0 - flags[0, jnp.minimum(seg0 + seg + 1, NSEG - 1)]

    def walk_rows(j, edge_row, sub_body):
        for seg in (1, 0):
            s = 2 * j + seg
            live = flags[1, seg0 + s]
            for k in reversed(range(SEG // SUB)):
                lo = SEG * s + SUB * k
                at = 2 * SEG * s + SUB * k
                if lo + SUB == HALF:
                    nxt = edge_row[0:1, :] * (not_last * keep_next(s))
                elif k == SEG // SUB - 1:
                    nxt = fin[2 * SEG * (s + 1) + SEG : 2 * SEG * (s + 1) + SEG + 1, :] * keep_next(s)
                else:
                    nxt = fin[at + SEG + SUB : at + SEG + SUB + 1, :]
                sub_body(lo, at, live, nxt)

    def after_rows(lo, at, live, nxt):
        e = fin[pl.ds(at, SUB), :] + lifted(nxt, fin[pl.ds(at + SEG, SUB), :])
        n = front4[pl.ds(N2 + lo, SUB), :]
        tally(GAIN2, e * n)
        tally(BIAS2, e)
        go = adj[pl.ds(lo, SUB), :].astype(F32) * live
        ga = go + norm_back(e, n, r2[pl.ds(lo, SUB), 0:1], g2[...])
        front4[pl.ds(N2 + lo, SUB), :] = ga
        gb[pl.ds(lo, SUB), :] = ga.astype(BF16)

    def mixed_chunk(j):
        t0[...] = nt(gb[pl.ds(128 * j, 128), :], wo[...])
        for seg in (1, 0):
            total = 16 * (2 * j + seg)
            sums[pl.ds(total, 16), :] = jnp.zeros((16, D), F32)

            def body(r, seg=seg, total=total):
                at = 128 * j + SEG * seg + r
                gm = t0[rows(SEG * seg + r, SUB), :]
                sr = red[rows(SR + at, SUB), :]
                w = red[rows(W + at, SUB), :]
                gw = gm * sr
                q = gw * red[rows(RD + at, SUB), :]
                red[rows(RD + at, SUB), :] = q
                gp[rows(at, SUB), :] = (gw * w * (1.0 - sr)).astype(BF16)
                fq = fade[rows(r, SUB), :] * q
                sums[pl.ds(total, 8), :] += fold(fq)
                sums[pl.ds(total + 8, 8), :] += fold(fq * w)

            each(SEG // SUB, SUB, body)

    def chain():
        first = jnp.zeros((1, D), F32)
        second = jnp.zeros((1, D), F32)
        th = through[...]
        for s in reversed(range(8)):
            q = jnp.sum(sums[pl.ds(16 * s, 8), :], axis=0, keepdims=True)
            qw = jnp.sum(sums[pl.ds(16 * s + 8, 8), :], axis=0, keepdims=True)
            if s < 7:
                q = q + th * (first * keep_next(s))
                qw = qw + th * (second * keep_next(s))
            first, second = q, qw
        sums[0:1, :] = first
        sums[1:2, :] = second

    tri = triangle(True)

    def key_value(k, carry):
        s = 7 - k
        lo = SEG * s
        keep = 1.0 - flags[0, seg0 + s]
        for col in range(D // 128):
            cols = pl.ds(col * 128, 128)
            at = rows(lo, SEG)
            q = red[rows(RD + lo, SEG), cols]
            w = red[rows(W + lo, SEG), cols]
            a = red[rows(A + lo, SEG), cols]
            v = red[rows(V + lo, SEG), cols]
            fq = fade[:, cols] * q
            cum, both = running(tri, fq, fq * w)
            cn = through[:, cols] * gc[0:1, cols]
            cd = through[:, cols] * gc[1:2, cols]
            gn = rise[:, cols] * (cum[:, :128] + cn)
            gd = rise[:, cols] * (cum[:, 128:] + cd)
            gc[0:1, cols] = (both[0:1, :128] + cum[0:1, :128] + cn) * keep
            gc[1:2, cols] = (both[0:1, 128:] + cum[0:1, 128:] + cd) * keep
            eq = expu[:, cols] * a * q
            gvv = a * gn + eq
            gv[at, cols] = gvv.astype(BF16)
            gk[at, cols] = (v * gvv - (a * gd + eq * w)).astype(BF16)
            up = eq * (v - w)
            down = gn * red[rows(SN + lo, SEG), cols] - gd * red[rows(SD + lo, SEG), cols]
            acc[pl.ds(8 * REW, 8), cols] += jnp.sum(up.reshape(-1, 8, 128), axis=0)
            acc[pl.ds(8 * LOGD, 8), cols] += jnp.sum(down.reshape(-1, 8, 128), axis=0)
        return carry

    def weights(k, left, right):
        for col in range(D // 256):
            cols = pl.ds(256 * col, 256)
            red[rows(mine_at + HALF_D * k, HALF_D), cols] = tn(left[...], right[:, cols])

    shared = []

    def share(ref):
        if not shared:
            pl.semaphore_wait(ready_sib, 1)
        shared.append((links.step, links.send(ref, ref, sib)))

    orders = ((ax, az, ay), (az, ax, ay), (ax, az, ay), (az, ax, ay), (ay, ax, az))

    def reduce_weights(k):
        if k == 0:
            pl.semaphore_wait(ready_ring, 6)
        first, second, third = orders[k]
        yield from all_reduce(
            links, red, mine_at + HALF_D * k, HALF_D, (first, second), xb, HALF_D * k,
            with_ring(third), yland, HALF_D // 4 * k, red, None, share, k in NEAR,
        )

    def front_chunk(j):
        at0 = pl.ds(128 * j, 128)
        t0[...] = nt(gk[at0, :], wk[...])
        t1[...] = nt(gv[at0, :], wv[...])
        t2[...] = nt(gp[at0, :], wr[...])
        for seg in range(2):

            def body(r, seg=seg):
                lo = 128 * j + SEG * seg
                pk, pv_, pr = (t[rows(SEG * seg + r, SUB), :] for t in (t0, t1, t2))
                dh1 = front4[rows(DH2 + lo + r, SUB), :]
                tally(MIXK, pk * dh1)
                tally(MIXV, pv_ * dh1)
                tally(MIXR, pr * dh1)
                base = pk * fk[...] + pv_ * fv[...] + pr * fr[...]
                fin[rows(2 * lo + r, SUB), :] = base
                fin[rows(2 * lo + SEG + r, SUB), :] = (pk + pv_ + pr) - base

            each(SEG // SUB, SUB, body)

    def input_rows(lo, at, live, nxt):
        e = fin[pl.ds(at, SUB), :] + lifted(nxt, fin[pl.ds(at + SEG, SUB), :])
        n = front4[pl.ds(GATE + lo, SUB), :]
        tally(GAIN1, e * n)
        tally(BIAS1, e)
        gi[rows(own_at + lo, SUB), :] = front4[pl.ds(N2 + lo, SUB), :] + norm_back(e, n, r1[pl.ds(lo, SUB), 0:1], g1[...])

    def vector_sums():
        scale = -jnp.exp(dec[...]) * jnp.exp(-jnp.exp(dec[...]))
        vec_o[...] = jnp.zeros_like(vec_o)
        for k in range(NVEC):
            total = jnp.sum(acc[pl.ds(8 * k, 8), :], axis=0, keepdims=True)
            vec_o[k : k + 1, :] = total * scale if k == LOGD else total

    def cast_rows(r):
        out_o[rows(own_at + r, SUB), :] = front4[rows(AFTER + r, SUB), :].astype(BF16)
        out_o[rows(other_at + r, SUB), :] = other[rows(r, SUB), :].astype(BF16)

    wk, wv = wg, wo

    def compute():
        fin_in.extend(
            bring(pq.at[group(own_at + 128 * j + SEG * c), :], fin.at[group(128 * j + SEG * c), :]) for j in range(4)
        )
        c_in.extend(
            links.send(pq.at[group(own_at + 128 * j + SEG * (1 - c)), :], xb.at[pl.ds(CRECV + 128 * j, 128), :], sib)
            for j in range(4)
        )
        first_in = [
            bring(s.at[half, :], front4.at[pl.ds(HALF * k, HALF), :]) for k, s in enumerate((after_h, gate_h, n2_h, dh2_h))
        ]
        first_in += [bring(adj_h.at[rows(own_at, HALF), :], adj), bring(wg_h, wg), bring(r2_h.at[half, :], r2)]
        first_in += [bring(wo_h, wo)]
        second_in = [
            bring(s.at[half, :], red.at[rows(spot, HALF), :])
            for s, spot in ((a_h, A), (v_h, V), (sr_h, SR), (w_h, W), (rd_h, RD), (sn_h, SN), (sd_h, SD))
        ]
        third_in = [
            bring(s.at[half, lanes], d)
            for s, d in (
                (mixed_h, mixed), (chrec_h, chrec), (keyed_h, keyed), (valued_h, valued), (recepted_h, recepted),
            )
        ]
        third_in += [bring(r1_h.at[half, :], r1), bring(wr_h, wr)]
        for k, v in enumerate(given):
            pv[k : k + 1, :] = v[...].reshape(1, D)
        through[...] = decay_tables(dec[...], rise, fade)
        expu[...] = jnp.exp(rew[...])
        acc[...] = jnp.zeros_like(acc)
        yield
        for j in (0, 3, 2, 1):
            e_in = take(j)
            if j == 1:
                for device in (xp, xm, zp, zm, yp, ym):
                    pl.semaphore_signal(ready_ring, inc=1, device_id=device, device_id_type=MESH)
            yield
            e_in.wait_recv()
            links.sent(e_in)
            if j == 0:
                for copy in first_in:
                    copy.wait()
            gate_part(j)
            if j == 0:
                gsend[...] = fin[SEG : SEG + 8, :]
                u_in = links.send(gsend, urow, opp)
            yield
            if j == 0:
                continue
            if j == 3:
                u_in.wait_recv()
                for copy in second_in:
                    copy.wait()
            if j == 1:
                wk_in = bring(wk_h, wk)
            walk_rows(j, urow, after_rows)
            mixed_chunk(j)
            yield
        walk_rows(0, urow, after_rows)
        mixed_chunk(0)
        chain()
        g_in = links.send(sums.at[pl.ds(0, 8), :], grecv, opp)
        late = [wk_in, bring(wv_h, wv), bring(n1_h.at[half, :], front4.at[pl.ds(GATE, HALF), :])]
        late.append(bring(dh1_h.at[half, :], front4.at[pl.ds(DH2, HALF), :]))
        yield
        for copy in third_in:
            copy.wait()
        weights(0, mixed, gb)
        yield
        weights(1, chrec, gg)
        yield
        g_in.wait_recv()
        edge = not_last * keep_next(7)
        gc[0:1, :] = grecv[0:1, :] * edge
        gc[1:2, :] = grecv[1:2, :] * edge
        lax.fori_loop(0, 4, key_value, 0)
        yield
        lax.fori_loop(4, 8, key_value, 0)
        pl.semaphore_signal(ready_sib, inc=1, device_id=sib, device_id_type=MESH)
        yield
        weights(2, recepted, gp)
        yield
        weights(3, keyed, gk)
        yield
        weights(4, valued, gv)
        yield
        for copy in late:
            copy.wait()
        for j in range(4):
            front_chunk(j)
            if j == 0:
                u2_in = links.send(fin.at[pl.ds(SEG, 8), :], urow2, opp)
            yield
        u2_in.wait_recv()
        for j in reversed(range(4)):
            walk_rows(j, urow2, input_rows)
            if j == 2:
                yield
        vector_sums()

    def vectors():
        for k, (place, others) in enumerate(((x, (xp, xo, xm)), (z, (zp, zo, zm)), (y, (yp, opp, ym)))):
            yield from sum_of_four(links, vec_o, 0, 16, place, others, vland, 64 * k)

    def swap(src, src_at, dst, dst_at, back_at):
        there = []
        for k in range(4):
            there.append(
                links.send(src.at[rows(src_at + SEG * k, SEG), :], dst.at[rows(dst_at + SEG * k, SEG), :], opp)
            )
            yield
        onward = []
        for k in range(4):
            there[k].wait_recv()
            theirs = dst.at[rows(back_at + SEG * k, SEG), :]
            onward.append(links.send(theirs, theirs, sib))
            yield
        for copy in onward:
            copy.wait_recv()

    def result():
        yield from swap(front4, AFTER + 256 * c, other, 256 * c, 256 * c)
        each(HALF // SUB, SUB, cast_rows)

    def input_grads():
        yield from swap(gi, own_at + 256 * c, gi, own_at + 256 * c, other_at + 256 * c)

    jobs = dict(zip("abcd", ffs))
    jobs.update(zip("pqrst", (reduce_weights(k) for k in range(MATS))))
    jobs.update(M=compute(), B=other_half(), V=vectors(), O=result(), G=input_grads())
    arrived = 0
    for name in "".join(ORDER):
        next(jobs[name], None)
        links.settle(SETTLE)
        while shared[arrived:] and shared[arrived][0] < links.step - SETTLE:
            shared[arrived][1].wait_recv()
            arrived += 1
    for _, copy in shared[arrived:]:
        copy.wait_recv()
    links.finish()


def back(front_outs, adj, vecs, mats):
    g1, b1, fk, fv, fr, dec, rew, g2, b2, ck, cr = vecs
    flags, rest = front_outs[0], front_outs[1:]
    vm = pltpu.VMEM
    anywhere = pl.BlockSpec(memory_space=pl.ANY)
    vmem = pl.BlockSpec(memory_space=pltpu.VMEM)
    half = lambda dt: vm((HALF, D), dt)
    return pl.pallas_call(
        back_kernel,
        in_specs=[pl.BlockSpec(memory_space=pltpu.SMEM)] + [anywhere] * len(rest) + [anywhere]
        + [vmem] * 9 + [anywhere] * 5,
        out_specs=[vmem] * 5,
        out_shape=[vm((T, D), BF16), vm((T, D), F32), vm((16, D), F32), vm((2 * R_ROWS, D), F32), vm((FF_ROWS, D), F32)],
        scratch_shapes=[vm((4 * HALF, D), F32), vm((HALF, 128), F32), vm((HALF, 128), F32)]
        + [vm((HALF, HALF_D), BF16)] * 5 + [half(BF16)] + [vm((D, D), BF16)] * 3
        + [vm((2 * HALF, D), F32), vm((R_ROWS, D), F32)]
        + [half(BF16)] * 5 + [vm((128, D), F32)] * 3 + [half(F32)]
        + [vm((FF_ROWS, D), F32), vm((R_ROWS // 4, D), F32), vm((192, D), F32)]
        + [vm((8, D), F32)] * 4 + [vm((8 * NVEC, D), F32)] + [vm((SEG, D), F32)] * 2
        + [vm((1, D), F32)] * 2 + [vm((128, D), F32), vm((8, D), F32), vm((16, D), F32)]
        + [pltpu.SemaphoreType.DMA((COPIES,)), pltpu.SemaphoreType.DMA((COPIES,)),
           pltpu.SemaphoreType.DMA((48,)), pltpu.SemaphoreType.REGULAR, pltpu.SemaphoreType.REGULAR],
        compiler_params=pltpu.CompilerParams(collective_id=1, has_side_effects=True, vmem_limit_bytes=BACK_VMEM * 2**20),
        cost_estimate=pl.CostEstimate(flops=14 * T * D * D, bytes_accessed=60 * 2**20, transcendentals=0),
        name="back",
    )(flags, *rest, adj, g1, fk, fv, fr, dec, rew, g2, ck, cr, *mats[:5])


def finish_kernel(out, gi, vec, red, ff, *refs):
    out_o, gi_o, mats, ck_o, cv_o, vecs, sems = refs[0], refs[1], refs[2:7], refs[7], refs[8], refs[9:20], refs[20]
    pairs = [(gi, gi_o), (ff.at[pl.ds(0, D), :], ck_o), (ff.at[pl.ds(D, D), :], cv_o), (out, out_o)]
    for k in range(MATS):
        for core in range(2):
            src = red.at[pl.ds(core * R_ROWS + HALF_D * k, HALF_D), :]
            pairs.append((src, mats[(3, 4, 0, 1, 2)[k]].at[pl.ds(HALF_D * core, HALF_D), :]))
    copies = [pltpu.make_async_copy(src, dst, sems.at[k]) for k, (src, dst) in enumerate(pairs)]
    for copy in copies:
        copy.start()
    for k in range(NVEC):
        vecs[k][...] = vec[k : k + 1, :].reshape(D)
    for copy in copies:
        copy.wait()


def finish(out, gi, vec, red, ff):
    sds = jax.ShapeDtypeStruct
    anywhere = pl.BlockSpec(memory_space=pl.ANY)
    vmem = pl.BlockSpec(memory_space=pltpu.VMEM)
    return pl.pallas_call(
        finish_kernel,
        in_specs=[vmem] * 5,
        out_specs=[anywhere] * 9 + [vmem] * NVEC,
        out_shape=[sds((T, D), BF16), sds((T, D), F32)] + [sds((D, D), F32)] * 7 + [sds((D,), F32)] * NVEC,
        scratch_shapes=[pltpu.SemaphoreType.DMA((16,))],
        compiler_params=pltpu.CompilerParams(vmem_limit_bytes=FINISH_VMEM * 2**20),
        name="finish",
    )(out, gi, vec, red, ff)


def body(
    entering_activations, sample_sizes, initial_layernorm_scale, initial_layernorm_offset, temporal_lookup_fraction,
    temporal_content_fraction, temporal_gating_fraction, fading_speed_logarithm, present_reward,
    temporal_gating_matrix, temporal_lookup_matrix, temporal_content_matrix, temporal_emission_matrix,
    latter_layernorm_scale, latter_layernorm_offset, feedforward_lookup_fraction, feedforward_gating_fraction,
    feedforward_gating_matrix, feedforward_lookup_matrix, feedforward_content_matrix, upstream_adjoint,
):
    vecs = (
        initial_layernorm_scale, initial_layernorm_offset, temporal_lookup_fraction, temporal_content_fraction,
        temporal_gating_fraction, fading_speed_logarithm, present_reward, latter_layernorm_scale,
        latter_layernorm_offset, feedforward_lookup_fraction, feedforward_gating_fraction,
    )
    mats = (
        temporal_gating_matrix, temporal_lookup_matrix, temporal_content_matrix, temporal_emission_matrix,
        feedforward_gating_matrix, feedforward_lookup_matrix, feedforward_content_matrix,
    )
    half = (lax.axis_index("tensor") // 2).astype(jnp.int32).reshape(1)
    fronts = front(half, sample_sizes, entering_activations, upstream_adjoint, vecs, mats)
    out, grad_inputs, recw, keyw, valw, outw, chrec, chkey, chval, *g = finish(*back(fronts, upstream_adjoint, vecs, mats))
    return (
        out, grad_inputs, g[0], g[1], g[2], g[3], g[4], g[5], g[6], recw, keyw, valw, outw,
        g[7], g[8], g[9], g[10], chrec, chkey, chval,
    )


def solution(mesh):
    split = P("dp", None)
    in_specs = (split, split) + (P(),) * 16 + (P(None, "tensor"), P("tensor", None), split)
    out_specs = (split, split) + (P(),) * 16 + (P(None, "tensor"), P("tensor", None))
    return jax.shard_map(body, mesh=mesh, in_specs=in_specs, out_specs=out_specs, check_vma=False)
```

```python
import functools

import jax
import jax.numpy as jnp
from jax import lax
from jax.experimental import pallas as pl
from jax.experimental.pallas import tpu as pltpu
from jax.sharding import PartitionSpec as P

F32 = jnp.float32
BF16 = jnp.bfloat16
EPSILON = 1e-05
SEG = 64
D = 768
T = 1024
HALF = 512
HALF_D = D // 2
BLK = 512
SUB = 32
NSEG = T // SEG
PER = HALF // BLK
SLOTS = PER


def nn(left, right):
    return jnp.dot(left, right, preferred_element_type=F32)


def nt(left, right):
    return lax.dot_general(left, right, (((1,), (1,)), ((), ())), preferred_element_type=F32)


def tn(left, right):
    return lax.dot_general(left, right, (((0,), (0,)), ((), ())), preferred_element_type=F32)


def normalize(v):
    c = v - jnp.mean(v, axis=-1, keepdims=True)
    r = lax.rsqrt(jnp.mean(c * c, axis=-1, keepdims=True) + EPSILON)
    return c * r, r


def roll_down(v, first):
    row = lax.broadcasted_iota(jnp.int32, v.shape, 0)
    return jnp.where(row == 0, first, pltpu.roll(v, 1, 0))


def two_parts(v):
    hi = v.astype(BF16)
    return hi, (v - hi.astype(F32)).astype(BF16)


def triangle(upper):
    row = lax.broadcasted_iota(jnp.int32, (SEG, 2 * SEG), 0)
    col = lax.broadcasted_iota(jnp.int32, (SEG, 2 * SEG), 1)
    col = jnp.where(col >= SEG, col - SEG, col)
    keep = (col > row) if upper else (col < row)
    return jnp.where(keep, 1.0, 0.0).astype(BF16)


def running(tri, first, second):
    both = jnp.concatenate([first, second], axis=1)
    hi, lo = two_parts(both)
    return nn(tri, jnp.concatenate([hi, lo], axis=0)), both


def decay_tables(dec, rise, fade):
    rate = jnp.exp(dec)
    offs = lax.broadcasted_iota(jnp.int32, (SEG, D), 0).astype(F32)
    rise[...] = jnp.exp((offs + 1.0) * rate)
    fade[...] = jnp.exp(-offs * rate)
    return jnp.exp(-float(SEG) * rate)


def spread(dst, first, cols, v):
    for s in range(v.shape[0] // SEG):
        dst[first + 2 * SEG * s : first + 2 * SEG * s + SEG, cols] = v[SEG * s : SEG * (s + 1), :]


def weave(products, others):
    done = 0
    for k, product in enumerate(products):
        product()
        upto = len(others) * (k + 1) // len(products)
        for other in others[done:upto]:
            other()
        done = upto
    for other in others[done:]:
        other()


def front_kernel(
    half_ref, len_ref, x_ref, adj_ref, g1_h, b1_h, fk_h, fv_h, fr_h, dec_h, rew_h, g2_h, b2_h, ck_h, cr_h,
    wr_h, wk_h, wv_h, wo_h, wg_h, wfk_h, wfv_h,
    flags, pq, grads, n1_h, dh1_h, a_h, v_h, sr_h, w_h, rd_h, sn_h, sd_h, after_h, gate_h, n2_h, dh2_h,
    r1_h, r2_h, keyed_h, valued_h, recepted_h, mixed_h, chrec_h,
    wr, wk, wv, wo, wg, wfk, wfv, wide, narrow, low, gbuf,
    rise, fade, through, expu, nc, dc, p1, p2, kb, vb, rb, hb, cks_all, hid_all, gch_all, gpr_all, pv, win, outs, gsem,
):
    i = pl.program_id(0)
    slot = lax.rem(i, SLOTS) if SLOTS > 1 else 0
    cks, hid, gch, gpr = (ref.at[i] for ref in (cks_all, hid_all, gch_all, gpr_all))
    given = (g1_h, b1_h, fk_h, fv_h, fr_h, dec_h, rew_h, g2_h, b2_h, ck_h, cr_h)
    g1, b1, fk, fv, fr, dec, rew, g2, b2, ck, cr = (pv.at[k : k + 1, :] for k in range(len(given)))
    n1_o, dh1_o, a_o, v_o, sr_o, w_o, rd_o, sn_o, sd_o, after_o, gate_o, n2_o, dh2_o = (
        wide.at[slot, k] for k in range(13)
    )
    r1_o, r2_o = (narrow.at[slot, k] for k in range(2))
    keyed_o, valued_o, recepted_o, mixed_o, chrec_o = (low.at[slot, k] for k in range(5))
    loads = [
        pltpu.make_async_copy(src, dst, win.at[k])
        for k, (src, dst) in enumerate(
            ((wk_h, wk), (wv_h, wv), (wr_h, wr), (wo_h, wo), (wfk_h, wfk), (wg_h, wg), (wfv_h, wfv))
        )
    ]
    kept = pl.ds(pl.multiple_of(lax.rem(i, PER) * BLK, BLK), BLK)
    held = (
        (wide, 0, n1_h), (wide, 1, dh1_h), (narrow, 0, r1_h), (low, 0, keyed_h), (low, 1, valued_h), (low, 2, recepted_h),
        (wide, 2, a_h), (wide, 3, v_h), (wide, 4, sr_h), (wide, 5, w_h), (wide, 6, rd_h), (wide, 7, sn_h),
        (wide, 8, sd_h), (low, 3, mixed_h),
        (wide, 9, after_h), (wide, 11, n2_h), (wide, 12, dh2_h), (narrow, 1, r2_h), (low, 4, chrec_h),
        (wide, 10, gate_h),
    )

    def saves(at):
        return [
            pltpu.make_async_copy(src.at[at, n], dst.at[kept, :], outs.at[at, k])
            for k, (src, n, dst) in enumerate(held)
        ]

    def save(lo, hi):
        @pl.when(i // PER == half_ref[0])
        def _():
            for copy in saves(slot)[lo:hi]:
                copy.start()

    def loaded(lo, hi):
        @pl.when(i == 0)
        def _():
            for copy in loads[lo:hi]:
                copy.wait()

    @pl.when(i == 0)
    def _():
        for copy in loads:
            copy.start()

    def reuse(lo, hi):
        @pl.when((i >= PER) & (half_ref[0] == 0))
        def _():
            for copy in saves(slot)[lo:hi]:
                copy.wait()

    reuse(0, 6)
    @pl.when(i == 0)
    def _():
        for b in range(NSEG):
            flags[0, b] = 0.0
        begin = jnp.int32(0)
        for j in range(NSEG):
            size = len_ref[0, j]
            at = lax.shift_right_logical(begin, 6)

            @pl.when(size > 0)
            def _():
                flags[0, at] = 1.0

            begin = begin + size
        for b in range(NSEG):
            flags[1, b] = jnp.where(b * SEG < begin, 1.0, 0.0)
        for k, v in enumerate(given):
            pv[k : k + 1, :] = v[...].reshape(1, D)
        through[...] = decay_tables(dec[...], rise, fade)
        expu[...] = jnp.exp(rew[...])
        nc[...] = jnp.zeros_like(nc)
        dc[...] = jnp.zeros_like(dc)
        p1[...] = jnp.zeros_like(p1)
        p2[...] = jnp.zeros_like(p2)

    fresh = [flags[0, i * (BLK // SEG) + s] for s in range(BLK // SEG)]
    live = [flags[1, i * (BLK // SEG) + s] for s in range(BLK // SEG)]

    tri = triangle(False)
    part = BLK // 2
    subs = part // SUB
    segs = part // SEG
    col_tiles = [pl.ds(0, D)]

    def first_norm(s):
        at = pl.ds(s * SUB, SUB)
        n1, r1 = normalize(x_ref[at, :].astype(F32))
        h1 = n1 * g1[...] + b1[...]
        before = p1[...]
        if (s * SUB) % SEG == 0:
            before = before * (1.0 - fresh[s * SUB // SEG])
        sh = roll_down(h1, before)
        p1[...] = h1[SUB - 1 :, :]
        dh1 = h1 - sh
        keyed_o[at, :] = (sh + dh1 * fk[...]).astype(BF16)
        valued_o[at, :] = (sh + dh1 * fv[...]).astype(BF16)
        recepted_o[at, :] = (sh + dh1 * fr[...]).astype(BF16)
        n1_o[at, :] = n1
        dh1_o[at, :] = dh1
        r1_o[at, :] = jnp.broadcast_to(r1, (SUB, 128))

    def mix_time(s, c):
        at = pl.ds(s * SEG, SEG)
        keep = 1.0 - fresh[s]
        cols = pl.ds(c * 128, 128)
        a = jnp.exp(kb[at, cols])
        v = vb[at, cols]
        lift = rise[:, cols] * a
        cum, both = running(tri, lift * v, lift)
        ncar = nc[:, cols] * keep
        dcar = dc[:, cols] * keep
        sn = fade[:, cols] * (ncar + cum[:, :128])
        sd = fade[:, cols] * (dcar + cum[:, 128:])
        th = through[:, cols]
        nc[:, cols] = th * (ncar + (cum[SEG - 1 :, :128] + both[SEG - 1 :, :128]))
        dc[:, cols] = th * (dcar + (cum[SEG - 1 :, 128:] + both[SEG - 1 :, 128:]))
        e = expu[:, cols] * a
        rd = 1.0 / (sd + e)
        w = (sn + e * v) * rd
        sr = jax.nn.sigmoid(rb[at, cols])
        mixed_o[at, cols] = (sr * w).astype(BF16)
        a_o[at, cols] = a
        v_o[at, cols] = v
        sr_o[at, cols] = sr
        w_o[at, cols] = w
        rd_o[at, cols] = rd
        sn_o[at, cols] = sn
        sd_o[at, cols] = sd

    def second_norm(s):
        at = pl.ds(s * SUB, SUB)
        after = x_ref[at, :].astype(F32) + hb[at, :]
        n2, r2 = normalize(after)
        h2 = n2 * g2[...] + b2[...]
        before = p2[...]
        if (s * SUB) % SEG == 0:
            before = before * (1.0 - fresh[s * SUB // SEG])
        sh = roll_down(h2, before)
        p2[...] = h2[SUB - 1 :, :]
        dh2 = h2 - sh
        cks[at, :] = (sh + dh2 * ck[...]).astype(BF16)
        chrec_o[at, :] = (sh + dh2 * cr[...]).astype(BF16)
        after_o[at, :] = after
        n2_o[at, :] = n2
        dh2_o[at, :] = dh2
        r2_o[at, :] = jnp.broadcast_to(r2, (SUB, 128))

    def gates(s):
        at = pl.ds(s * SUB, SUB)
        hp = jnp.maximum(kb[at, :], 0.0)
        hid[at, :] = (hp * hp).astype(BF16)
        gate = jax.nn.sigmoid(rb[at, :])
        gate_o[at, :] = gate
        go = adj_ref[at, :].astype(F32) * live[s * SUB // SEG]
        gch[at, :] = (go * gate).astype(BF16)

    def hidden_grads(s):
        at = pl.ds(s * SUB, SUB)
        gpr[at, :] = (2.0 * jnp.maximum(kb[at, :], 0.0) * vb[at, :]).astype(BF16)

    def all_of(fn, p, count):
        return [functools.partial(fn, p * count + k) for k in range(count)]

    def times(p, dst, left, right):
        at = pl.ds(p * part, part)

        def piece(cols):
            dst[at, cols] = nn(left[at, :], right[:, cols])

        return [functools.partial(piece, cols) for cols in col_tiles]

    def times_turned(p, dst, left, right):
        at = pl.ds(p * part, part)

        def piece(cols):
            dst[at, cols] = nt(left[at, :], right[cols, :])

        return [functools.partial(piece, cols) for cols in col_tiles]

    def to_pq(p, first, product, left, right):
        at = pl.ds(p * part, part)

        def piece(cols):
            v = nn(left[at, :], right[:, cols]) if product is nn else nt(left[at, :], right[cols, :])
            spread(pq, 2 * p * part + first, cols, v)

        return [functools.partial(piece, cols) for cols in col_tiles]

    def projections(p):
        return times(p, kb, keyed_o, wk) + times(p, vb, valued_o, wv) + times(p, rb, recepted_o, wr)

    def mixing(p):
        return [functools.partial(mix_time, p * segs + s, c) for s in range(segs) for c in range(D // 128)]

    def hidden(p):
        return times(p, kb, cks, wfk) + times(p, rb, chrec_o, wg)

    def outward(p):
        return to_pq(p, 0, nn, hid, wfv) + times_turned(p, vb, gch, wfv)

    weave([], all_of(first_norm, 0, subs))
    loaded(0, 3)
    weave(projections(0), all_of(first_norm, 1, subs))
    save(0, 6)
    reuse(6, 14)
    loaded(3, 4)
    weave(projections(1), mixing(0))
    weave(times(0, hb, mixed_o, wo), mixing(1))
    save(6, 14)
    reuse(14, 20)
    loaded(4, 7)
    weave(times(1, hb, mixed_o, wo), all_of(second_norm, 0, subs))
    weave(hidden(0), all_of(second_norm, 1, subs))
    save(14, 19)
    weave(hidden(1), all_of(gates, 0, subs))
    weave(outward(0), all_of(gates, 1, subs))
    save(19, 20)
    weave(outward(1), all_of(hidden_grads, 0, subs))
    weave(to_pq(0, SEG, nt, gpr, wfk), all_of(hidden_grads, 1, subs))
    weave(to_pq(1, SEG, nt, gpr, wfk), [])

    @pl.when(i == T // BLK - 1)
    def _():
        out_copies = []
        for k, (left, right) in enumerate(((cks_all, gpr_all), (hid_all, gch_all))):
            for c in range(D // 256):
                at = pl.ds(D * k + 256 * c, 256)
                gbuf[at, :] = tn(left[:, :, pl.ds(256 * c, 256)].reshape(T, 256), right[...].reshape(T, D))
                out_copies.append(pltpu.make_async_copy(gbuf.at[at, :], grads.at[at, :], gsem.at[3 * k + c]))
                out_copies[-1].start()
        for copy in out_copies:
            copy.wait()

    @pl.when((i == T // BLK - 1) & (half_ref[0] == 1))
    def _():
        for s in range(SLOTS):
            for copy in saves(s):
                copy.wait()


def front(half, sizes, x, adj, vecs, mats):
    steps = T // BLK
    blk = lambda w: pl.BlockSpec((BLK, w), lambda i, h: (i, 0))
    vec = pl.BlockSpec((D,), lambda i, h: (0,))
    anywhere = pl.BlockSpec(memory_space=pl.ANY)
    sds = jax.ShapeDtypeStruct
    vm = pltpu.VMEM
    return pl.pallas_call(
        front_kernel,
        grid_spec=pltpu.PrefetchScalarGridSpec(
            num_scalar_prefetch=1,
            grid=(steps,),
            in_specs=[pl.BlockSpec(memory_space=pltpu.SMEM), blk(D), blk(D)] + [vec] * 11 + [anywhere] * 7,
            out_specs=[pl.BlockSpec(memory_space=pltpu.SMEM), pl.BlockSpec((2 * BLK, D), lambda i, h: (i, 0))]
            + [anywhere] * 21,
            scratch_shapes=[vm((D, D), BF16)] * 7
            + [vm((SLOTS, 13, BLK, D), F32), vm((SLOTS, 2, BLK, 128), F32), vm((SLOTS, 5, BLK, D), BF16), vm((2 * D, D), F32)]
            + [vm((SEG, D), F32)] * 2 + [vm((1, D), F32)] * 6 + [vm((BLK, D), F32)] * 4
            + [vm((T // BLK, BLK, D), BF16)] * 4 + [vm((16, D), F32)]
            + [pltpu.SemaphoreType.DMA((7,)), pltpu.SemaphoreType.DMA((SLOTS, 20)), pltpu.SemaphoreType.DMA((6,))],
        ),
        out_shape=[sds((2, NSEG), F32), sds((2 * T, D), F32), sds((2 * D, D), F32)]
        + [sds((HALF, D), F32)] * 13 + [sds((HALF, 128), F32)] * 2 + [sds((HALF, D), BF16)] * 5,
        compiler_params=pltpu.CompilerParams(dimension_semantics=("arbitrary",), vmem_limit_bytes=62 * 2**20),
        cost_estimate=pl.CostEstimate(flops=11 * 2 * T * D * D, bytes_accessed=60 * 2**20, transcendentals=4 * T * D),
        name="front",
    )(half, sizes, x, adj, *vecs, *mats)


MESH = pl.DeviceIdType.MESH
COPIES = 256
FF_ROWS = 2 * D
R_ROWS = 2048
MATS = 5
BACK_VMEM = 39
FINISH_VMEM = 2
SETTLE = 14
NEAR = (0, 1, 2, 3, 4)
ORDER = (
    "adBBBadBbcMMdBabcMMadBMbadMBcBMabMcdMMcbaMMMMOMp",
    "qMMMMrsMtMpqMMtsrOqbpstrqOcMMbsptaMrOdqGstprOsVt",
    "bGcqGrpVstqrdVpGtcGrsqpV",
)
NVEC = 11


def rows(start, size):
    return pl.ds(pl.multiple_of(start, 8), size)


def each(count, step, body, reverse=False):
    def run(k, carry):
        body((count - 1 - k) * step if reverse else k * step)
        return carry

    lax.fori_loop(0, count, run, 0)


class Links:
    def __init__(self, sends, recvs):
        self.sends, self.recvs, self.used, self.open, self.step = sends, recvs, 0, [], 0

    def send(self, src, dst, device):
        k = self.used
        self.used += 1
        copy = pltpu.make_async_remote_copy(
            src_ref=src, dst_ref=dst, send_sem=self.sends.at[k], recv_sem=self.recvs.at[k],
            device_id=device, device_id_type=MESH,
        )
        copy.start()
        self.open.append((self.step, copy))
        return copy

    def sent(self, copy):
        if all(kept[1] is not copy for kept in self.open):
            return
        self.open = [kept for kept in self.open if kept[1] is not copy]
        copy.wait_send()

    def settle(self, steps):
        while self.open and self.open[0][0] < self.step - steps:
            self.open.pop(0)[1].wait_send()
        self.step += 1

    def finish(self):
        for _, copy in self.open:
            copy.wait_send()


def add_into(dst, dst_at, terms, size, step=16):
    if size % step:
        step = 8

    def body(r):
        total = dst[rows(dst_at + r, step), :]
        for ref, start in terms:
            total = total + ref[rows(start + r, step), :]
        dst[rows(dst_at + r, step), :] = total

    each(size // step, step, body)


def ring_reduce(links, data, base, size, place, up, down, land, land_at, source, loaded):
    s = size // 4
    qa = (s // 2 + 7) // 8 * 8
    qb = s - qa
    mine = base + place * s
    nxt = base + lax.rem(place + 1, 4) * s
    opp = base + lax.rem(place + 2, 4) * s
    prv = base + lax.rem(place + 3, 4) * s
    starts = [land_at]
    for size_k in (qa, qb, qb, qa, qa, qb):
        starts.append(starts[-1] + size_k)
    spot = [land.at[pl.ds(a, b - a), :] for a, b in zip(starts, starts[1:])]
    fwd_a = links.send(source.at[rows(opp, qa), :], spot[0], up)
    fwd_b = links.send(source.at[rows(opp + qa, qb), :], spot[1], down)
    dir_b = links.send(source.at[rows(nxt + qa, qb), :], spot[2], up)
    dir_a = links.send(source.at[rows(prv, qa), :], spot[3], down)
    yield
    if loaded is not None:
        loaded()
    fwd_a.wait_recv()
    add_into(land, starts[0], [(data, nxt)], qa)
    cmb_a = links.send(spot[0], spot[4], up)
    fwd_b.wait_recv()
    add_into(land, starts[1], [(data, prv + qa)], qb)
    for copy in (fwd_a, fwd_b, dir_b, dir_a):
        links.sent(copy)
    cmb_b = links.send(spot[1], spot[5], down)
    yield
    dir_a.wait_recv()
    dir_b.wait_recv()
    cmb_a.wait_recv()
    cmb_b.wait_recv()
    add_into(data, mine, [(land, starts[3]), (land, starts[4])], qa)
    add_into(data, mine + qa, [(land, starts[2]), (land, starts[5])], qb)


def ring_gather(links, data, base, size, place, up, down, share):
    s = size // 4
    qa = (s // 2 + 7) // 8 * 8
    qb = s - qa
    mine = base + place * s
    nxt = base + lax.rem(place + 1, 4) * s
    opp = base + lax.rem(place + 2, 4) * s
    prv = base + lax.rem(place + 3, 4) * s
    own = data.at[rows(mine, s), :]
    to_up = links.send(own, own, up)
    to_down = links.send(own, own, down)
    share(own)
    yield
    to_up.wait_recv()
    half_a = data.at[rows(prv, qa), :]
    on_a = links.send(half_a, half_a, up)
    to_down.wait_recv()
    half_b = data.at[rows(nxt + qa, qb), :]
    on_b = links.send(half_b, half_b, down)
    share(data.at[rows(prv, s), :])
    share(data.at[rows(nxt, s), :])
    yield
    on_a.wait_recv()
    on_b.wait_recv()
    share(data.at[rows(opp, s), :])


def near_reduce(links, data, base, size, place, others, land, land_at, stage_at):
    s = size // 4
    copies = []
    for k, device in enumerate(others):
        theirs = base + lax.rem(place + 1 + k, 4) * s
        stage = stage_at + k * s

        def body(r, theirs=theirs, stage=stage):
            land[rows(stage + r, 8), :] = data[rows(theirs + r, 8), :]

        each(s // 8, 8, body)
        copies.append(links.send(land.at[pl.ds(stage, s), :], land.at[pl.ds(land_at + k * s, s), :], device))
    yield
    for copy in copies:
        copy.wait_recv()
    add_into(data, base + place * s, [(land, land_at + k * s) for k in range(3)], s, 8)


def near_gather(links, data, base, size, place, others):
    s = size // 4
    own = data.at[rows(base + place * s, s), :]
    copies = [links.send(own, own, device) for device in others]
    yield
    for copy in copies:
        copy.wait_recv()


def sum_of_four(links, data, base, size, place, others, land, land_at):
    mine = rows(land_at + place * size, size)
    land[mine, :] = data[rows(base, size), :]
    copies = [links.send(land.at[mine, :], land.at[mine, :], device) for device in others]
    yield
    for copy in copies:
        copy.wait_recv()

    def body(r):
        a, b, c, d = (land[rows(land_at + k * size + r, 8), :] for k in range(4))
        data[rows(base + r, 8), :] = (a + b) + (c + d)

    each(size // 8, 8, body)


def all_reduce(links, data, base, size, axes, land, land_at, last, last_land, last_at, source, loaded, share, near):
    (place, up, _, down), (place_2, up_2, opp_2, down_2) = axes
    others = (up_2, opp_2, down_2)
    yield from ring_reduce(links, data, base, size, place, up, down, land, land_at, source, loaded)
    part = size // 4
    at = base + place * part
    if near:
        yield from near_reduce(links, data, at, part, place_2, others, land, land_at + 3 * part, land_at + part)
    else:
        yield from ring_reduce(links, data, at, part, place_2, up_2, down_2, land, land_at + 3 * part, data, None)
    yield from last(links, data, at + place_2 * (part // 4), part // 4, last_land, last_at)
    if near:
        yield from near_gather(links, data, at, part, place_2, others)
    else:
        yield from ring_gather(links, data, at, part, place_2, up_2, down_2, lambda ref: None)
    yield from ring_gather(links, data, base, size, place, up, down, share)


def back_kernel(
    flags, pq, grads, n1_h, dh1_h, a_h, v_h, sr_h, w_h, rd_h, sn_h, sd_h, after_h, gate_h, n2_h, dh2_h,
    r1_h, r2_h, keyed_h, valued_h, recepted_h, mixed_h, chrec_h, adj_h,
    g1_h, fk_h, fv_h, fr_h, dec_h, rew_h, g2_h, ck_h, cr_h, wr_h, wk_h, wv_h, wo_h, wg_h,
    out_o, gi, vec_o, red, ff,
    front4, r1, r2, keyed, valued, recepted, mixed, chrec, adj, wr, wo, wg,
    fin, xb, gg, gb, gk, gv, gp, t0, t1, t2, other, ffland, yland, vland,
    urow, urow2, gsend, grecv, acc, rise, fade, through, expu, sums, gc, pv,
    sends, recvs, fill, ready_ring, ready_sib,
):
    dp = lax.axis_index("dp")
    tensor = lax.axis_index("tensor")
    x, z, yl = dp // 8, lax.rem(dp // 2, 4), lax.rem(dp, 2)
    h, c = tensor // 2, lax.rem(tensor, 2)
    y = 2 * h + yl

    def chip(cx, cz, cy):
        cx, cz, cy = lax.rem(cx + 4, 4), lax.rem(cz + 4, 4), lax.rem(cy + 4, 4)
        return {"dp": (cx * 4 + cz) * 2 + lax.rem(cy, 2), "tensor": (cy // 2) * 2 + c}

    xp, xo, xm = (chip(x + k, z, y) for k in (1, 2, 3))
    zp, zo, zm = (chip(x, z + k, y) for k in (1, 2, 3))
    yp, opp, ym = (chip(x, z, y + k) for k in (1, 2, 3))
    sib = {"dp": dp, "tensor": h * 2 + (1 - c)}
    pair = {"dp": dp + 1 - 2 * yl, "tensor": tensor}
    own_at, other_at = h * HALF, (1 - h) * HALF
    mine_at = c * R_ROWS

    given = (g1_h, fk_h, fv_h, fr_h, dec_h, rew_h, g2_h, ck_h, cr_h)
    g1, fk, fv, fr, dec, rew, g2, ck, cr = (pv.at[k : k + 1, :] for k in range(len(given)))
    barrier = pltpu.get_barrier_semaphore()
    partners = (xp, xo, xm, zp, zo, zm, yp, ym, opp, sib)
    for device in partners:
        pl.semaphore_signal(barrier, inc=1, device_id=device, device_id_type=MESH)

    fills = []

    def bring(src, dst):
        copy = pltpu.make_async_copy(src, dst, fill.at[len(fills)])
        copy.start()
        fills.append(copy)
        return copy

    def group(start):
        return rows(2 * start, 2 * SEG)

    PART, ARECV, CRECV, BRECV = (512 * k for k in range(4))
    part_in = [
        bring(pq.at[group(other_at + 128 * j + SEG * c), :], xb.at[pl.ds(PART + 128 * j, 128), :]) for j in range(4)
    ]
    ff_in = bring(grads, ff)
    pl.semaphore_wait(barrier, len(partners))

    links = Links(sends, recvs)
    ax, az, ay = (x, xp, xo, xm), (z, zp, zo, zm), (y, yp, opp, ym)

    def with_pair(links, data, base, size, land, land_at):
        whole = data.at[rows(base, size), :]
        copy = links.send(whole, land.at[pl.ds(land_at, size), :], pair)
        yield
        links.sent(copy)
        copy.wait_recv()
        add_into(data, base, [(land, land_at)], size, 8)

    def with_ring(axis):
        def last(links, data, base, size, land, land_at):
            yield from sum_of_four(links, data, base, size, axis[0], axis[1:], land, land_at)

        return last

    waited = []

    def ff_loaded():
        if not waited:
            ff_in.wait()
            waited.append(True)

    n = FF_ROWS // 4
    ffs = [
        all_reduce(
            links, ff, n * k, n, (ax, az) if k % 2 == 0 else (az, ax), ffland, n * k,
            with_pair, ffland, n * k + 15 * n // 16, grads, ff_loaded, lambda ref: None, True,
        )
        for k in range(4)
    ]

    a_in = [
        links.send(pq.at[group(other_at + 128 * j + SEG * (1 - c)), :], xb.at[pl.ds(ARECV + 128 * j, 128), :], sib)
        for j in range(4)
    ]
    AFTER, GATE, N2, DH2 = (HALF * k for k in range(4))
    SR, W, RD, A, V, SN, SD = (lax.rem(mine_at + HALF * k, 2 * R_ROWS) for k in range(1, 8))
    lanes = pl.ds(pl.multiple_of(c * HALF_D, 128), HALF_D)
    half = pl.ds(0, HALF)
    b_in = {}
    c_in = []
    fin_in = []

    def other_half():
        for j in (0, 3, 2, 1):
            part_in[j].wait()
            a_in[j].wait_recv()
            for at in (128 * j, 128 * j + SEG):
                add_into(xb, PART + at, [(xb, ARECV + at)], SEG)
                b_in[at] = links.send(xb.at[pl.ds(PART + at, SEG), :], xb.at[pl.ds(BRECV + at, SEG), :], opp)
                yield

    seg0 = h * (HALF // SEG)
    not_last = (1 - h).astype(F32)

    def fold(v):
        return jnp.sum(v.reshape(-1, 8, D), axis=0)

    def tally(k, v):
        acc[pl.ds(8 * k, 8), :] += fold(v)

    GAIN1, BIAS1, MIXK, MIXV, MIXR, LOGD, REW, GAIN2, BIAS2, CMIXK, CMIXR = range(NVEC)

    def take(j):
        fin_in[j].wait()
        c_in[j].wait_recv()
        b_in[128 * j].wait_recv()
        b_in[128 * j + SEG].wait_recv()
        add_into(fin, 2 * (128 * j + SEG * c), [(xb, CRECV + 128 * j), (xb, BRECV + 128 * j)], 128)
        mine = fin.at[group(128 * j + SEG * c), :]
        links.sent(b_in[128 * j])
        links.sent(b_in[128 * j + SEG])
        return links.send(mine, mine, sib)

    def gate_part(j):
        lo = 128 * j
        for seg in range(2):
            live = flags[1, seg0 + 2 * j + seg]

            def body(r, seg=seg, live=live):
                at = lo + SEG * seg + r
                gate = front4[rows(GATE + at, SUB), :]
                co = fin[rows(2 * (lo + SEG * seg) + r, SUB), :]
                res = live * (front4[rows(AFTER + at, SUB), :] + gate * co)
                front4[rows(AFTER + at, SUB), :] = res.astype(BF16).astype(F32)
                go = adj[rows(at, SUB), :].astype(F32) * live
                gg[rows(at, SUB), :] = (go * co * gate * (1.0 - gate)).astype(BF16)

            each(SEG // SUB, SUB, body)
        t0[...] = nt(gg[pl.ds(lo, 128), :], wg[...])
        for seg in range(2):

            def body2(r, seg=seg):
                at = 2 * (lo + SEG * seg) + r
                qk = fin[rows(at + SEG, SUB), :]
                qr = t0[rows(SEG * seg + r, SUB), :]
                dh2 = front4[rows(DH2 + lo + SEG * seg + r, SUB), :]
                tally(CMIXK, qk * dh2)
                tally(CMIXR, qr * dh2)
                base = qk * ck[...] + qr * cr[...]
                fin[rows(at, SUB), :] = base
                fin[rows(at + SEG, SUB), :] = (qk + qr) - base

            each(SEG // SUB, SUB, body2)

    def lifted(nxt, u):
        row = lax.broadcasted_iota(jnp.int32, u.shape, 0)
        return jnp.where(row == u.shape[0] - 1, nxt, pltpu.roll(u, u.shape[0] - 1, 0))

    def norm_back(e, n, r, gain):
        f = e * gain
        return r * (f - jnp.mean(f, axis=-1, keepdims=True) - n * jnp.mean(f * n, axis=-1, keepdims=True))

    def keep_next(seg):
        return 1.0 - flags[0, jnp.minimum(seg0 + seg + 1, NSEG - 1)]

    def walk_rows(j, edge_row, sub_body):
        for seg in (1, 0):
            s = 2 * j + seg
            live = flags[1, seg0 + s]
            for k in reversed(range(SEG // SUB)):
                lo = SEG * s + SUB * k
                at = 2 * SEG * s + SUB * k
                if lo + SUB == HALF:
                    nxt = edge_row[0:1, :] * (not_last * keep_next(s))
                elif k == SEG // SUB - 1:
                    nxt = fin[2 * SEG * (s + 1) + SEG : 2 * SEG * (s + 1) + SEG + 1, :] * keep_next(s)
                else:
                    nxt = fin[at + SEG + SUB : at + SEG + SUB + 1, :]
                sub_body(lo, at, live, nxt)

    def after_rows(lo, at, live, nxt):
        e = fin[pl.ds(at, SUB), :] + lifted(nxt, fin[pl.ds(at + SEG, SUB), :])
        n = front4[pl.ds(N2 + lo, SUB), :]
        tally(GAIN2, e * n)
        tally(BIAS2, e)
        go = adj[pl.ds(lo, SUB), :].astype(F32) * live
        ga = go + norm_back(e, n, r2[pl.ds(lo, SUB), 0:1], g2[...])
        front4[pl.ds(N2 + lo, SUB), :] = ga
        gb[pl.ds(lo, SUB), :] = ga.astype(BF16)

    def mixed_chunk(j):
        t0[...] = nt(gb[pl.ds(128 * j, 128), :], wo[...])
        for seg in (1, 0):
            total = 16 * (2 * j + seg)
            sums[pl.ds(total, 16), :] = jnp.zeros((16, D), F32)

            def body(r, seg=seg, total=total):
                at = 128 * j + SEG * seg + r
                gm = t0[rows(SEG * seg + r, SUB), :]
                sr = red[rows(SR + at, SUB), :]
                w = red[rows(W + at, SUB), :]
                gw = gm * sr
                q = gw * red[rows(RD + at, SUB), :]
                red[rows(RD + at, SUB), :] = q
                gp[rows(at, SUB), :] = (gw * w * (1.0 - sr)).astype(BF16)
                fq = fade[rows(r, SUB), :] * q
                sums[pl.ds(total, 8), :] += fold(fq)
                sums[pl.ds(total + 8, 8), :] += fold(fq * w)

            each(SEG // SUB, SUB, body)

    def chain():
        first = jnp.zeros((1, D), F32)
        second = jnp.zeros((1, D), F32)
        th = through[...]
        for s in reversed(range(8)):
            q = jnp.sum(sums[pl.ds(16 * s, 8), :], axis=0, keepdims=True)
            qw = jnp.sum(sums[pl.ds(16 * s + 8, 8), :], axis=0, keepdims=True)
            if s < 7:
                q = q + th * (first * keep_next(s))
                qw = qw + th * (second * keep_next(s))
            first, second = q, qw
        sums[0:1, :] = first
        sums[1:2, :] = second

    tri = triangle(True)

    def key_value(k, carry):
        s = 7 - k
        lo = SEG * s
        keep = 1.0 - flags[0, seg0 + s]
        for col in range(D // 128):
            cols = pl.ds(col * 128, 128)
            at = rows(lo, SEG)
            q = red[rows(RD + lo, SEG), cols]
            w = red[rows(W + lo, SEG), cols]
            a = red[rows(A + lo, SEG), cols]
            v = red[rows(V + lo, SEG), cols]
            fq = fade[:, cols] * q
            cum, both = running(tri, fq, fq * w)
            cn = through[:, cols] * gc[0:1, cols]
            cd = through[:, cols] * gc[1:2, cols]
            gn = rise[:, cols] * (cum[:, :128] + cn)
            gd = rise[:, cols] * (cum[:, 128:] + cd)
            gc[0:1, cols] = (both[0:1, :128] + cum[0:1, :128] + cn) * keep
            gc[1:2, cols] = (both[0:1, 128:] + cum[0:1, 128:] + cd) * keep
            eq = expu[:, cols] * a * q
            gvv = a * gn + eq
            gv[at, cols] = gvv.astype(BF16)
            gk[at, cols] = (v * gvv - (a * gd + eq * w)).astype(BF16)
            up = eq * (v - w)
            down = gn * red[rows(SN + lo, SEG), cols] - gd * red[rows(SD + lo, SEG), cols]
            acc[pl.ds(8 * REW, 8), cols] += jnp.sum(up.reshape(-1, 8, 128), axis=0)
            acc[pl.ds(8 * LOGD, 8), cols] += jnp.sum(down.reshape(-1, 8, 128), axis=0)
        return carry

    def weights(k, left, right):
        for col in range(D // 256):
            cols = pl.ds(256 * col, 256)
            red[rows(mine_at + HALF_D * k, HALF_D), cols] = tn(left[...], right[:, cols])

    shared = []

    def share(ref):
        if not shared:
            pl.semaphore_wait(ready_sib, 1)
        shared.append((links.step, links.send(ref, ref, sib)))

    orders = ((ax, az, ay), (az, ax, ay), (ax, az, ay), (az, ax, ay), (ay, ax, az))

    def reduce_weights(k):
        if k == 0:
            pl.semaphore_wait(ready_ring, 6)
        first, second, third = orders[k]
        yield from all_reduce(
            links, red, mine_at + HALF_D * k, HALF_D, (first, second), xb, HALF_D * k,
            with_ring(third), yland, HALF_D // 4 * k, red, None, share, k in NEAR,
        )

    def front_chunk(j):
        at0 = pl.ds(128 * j, 128)
        t0[...] = nt(gk[at0, :], wk[...])
        t1[...] = nt(gv[at0, :], wv[...])
        t2[...] = nt(gp[at0, :], wr[...])
        for seg in range(2):

            def body(r, seg=seg):
                lo = 128 * j + SEG * seg
                pk, pv_, pr = (t[rows(SEG * seg + r, SUB), :] for t in (t0, t1, t2))
                dh1 = front4[rows(DH2 + lo + r, SUB), :]
                tally(MIXK, pk * dh1)
                tally(MIXV, pv_ * dh1)
                tally(MIXR, pr * dh1)
                base = pk * fk[...] + pv_ * fv[...] + pr * fr[...]
                fin[rows(2 * lo + r, SUB), :] = base
                fin[rows(2 * lo + SEG + r, SUB), :] = (pk + pv_ + pr) - base

            each(SEG // SUB, SUB, body)

    def input_rows(lo, at, live, nxt):
        e = fin[pl.ds(at, SUB), :] + lifted(nxt, fin[pl.ds(at + SEG, SUB), :])
        n = front4[pl.ds(GATE + lo, SUB), :]
        tally(GAIN1, e * n)
        tally(BIAS1, e)
        gi[rows(own_at + lo, SUB), :] = front4[pl.ds(N2 + lo, SUB), :] + norm_back(e, n, r1[pl.ds(lo, SUB), 0:1], g1[...])

    def vector_sums():
        scale = -jnp.exp(dec[...]) * jnp.exp(-jnp.exp(dec[...]))
        vec_o[...] = jnp.zeros_like(vec_o)
        for k in range(NVEC):
            total = jnp.sum(acc[pl.ds(8 * k, 8), :], axis=0, keepdims=True)
            vec_o[k : k + 1, :] = total * scale if k == LOGD else total

    def cast_rows(r):
        out_o[rows(own_at + r, SUB), :] = front4[rows(AFTER + r, SUB), :].astype(BF16)
        out_o[rows(other_at + r, SUB), :] = other[rows(r, SUB), :].astype(BF16)

    wk, wv = wg, wo

    def compute():
        fin_in.extend(
            bring(pq.at[group(own_at + 128 * j + SEG * c), :], fin.at[group(128 * j + SEG * c), :]) for j in range(4)
        )
        c_in.extend(
            links.send(pq.at[group(own_at + 128 * j + SEG * (1 - c)), :], xb.at[pl.ds(CRECV + 128 * j, 128), :], sib)
            for j in range(4)
        )
        first_in = [
            bring(s.at[half, :], front4.at[pl.ds(HALF * k, HALF), :]) for k, s in enumerate((after_h, gate_h, n2_h, dh2_h))
        ]
        first_in += [bring(adj_h.at[rows(own_at, HALF), :], adj), bring(wg_h, wg), bring(r2_h.at[half, :], r2)]
        first_in += [bring(wo_h, wo)]
        second_in = [
            bring(s.at[half, :], red.at[rows(spot, HALF), :])
            for s, spot in ((a_h, A), (v_h, V), (sr_h, SR), (w_h, W), (rd_h, RD), (sn_h, SN), (sd_h, SD))
        ]
        third_in = [
            bring(s.at[half, lanes], d)
            for s, d in (
                (mixed_h, mixed), (chrec_h, chrec), (keyed_h, keyed), (valued_h, valued), (recepted_h, recepted),
            )
        ]
        third_in += [bring(r1_h.at[half, :], r1), bring(wr_h, wr)]
        for k, v in enumerate(given):
            pv[k : k + 1, :] = v[...].reshape(1, D)
        through[...] = decay_tables(dec[...], rise, fade)
        expu[...] = jnp.exp(rew[...])
        acc[...] = jnp.zeros_like(acc)
        yield
        for j in (0, 3, 2, 1):
            e_in = take(j)
            if j == 1:
                for device in (xp, xm, zp, zm, yp, ym):
                    pl.semaphore_signal(ready_ring, inc=1, device_id=device, device_id_type=MESH)
            yield
            e_in.wait_recv()
            links.sent(e_in)
            if j == 0:
                for copy in first_in:
                    copy.wait()
            gate_part(j)
            if j == 0:
                gsend[...] = fin[SEG : SEG + 8, :]
                u_in = links.send(gsend, urow, opp)
            yield
            if j == 0:
                continue
            if j == 3:
                u_in.wait_recv()
                for copy in second_in:
                    copy.wait()
            if j == 1:
                wk_in = bring(wk_h, wk)
            walk_rows(j, urow, after_rows)
            mixed_chunk(j)
            yield
        walk_rows(0, urow, after_rows)
        mixed_chunk(0)
        chain()
        g_in = links.send(sums.at[pl.ds(0, 8), :], grecv, opp)
        late = [wk_in, bring(wv_h, wv), bring(n1_h.at[half, :], front4.at[pl.ds(GATE, HALF), :])]
        late.append(bring(dh1_h.at[half, :], front4.at[pl.ds(DH2, HALF), :]))
        yield
        for copy in third_in:
            copy.wait()
        weights(0, mixed, gb)
        yield
        weights(1, chrec, gg)
        yield
        g_in.wait_recv()
        edge = not_last * keep_next(7)
        gc[0:1, :] = grecv[0:1, :] * edge
        gc[1:2, :] = grecv[1:2, :] * edge
        lax.fori_loop(0, 4, key_value, 0)
        yield
        lax.fori_loop(4, 8, key_value, 0)
        pl.semaphore_signal(ready_sib, inc=1, device_id=sib, device_id_type=MESH)
        yield
        weights(2, recepted, gp)
        yield
        weights(3, keyed, gk)
        yield
        weights(4, valued, gv)
        yield
        for copy in late:
            copy.wait()
        for j in range(4):
            front_chunk(j)
            if j == 0:
                u2_in = links.send(fin.at[pl.ds(SEG, 8), :], urow2, opp)
            yield
        u2_in.wait_recv()
        for j in reversed(range(4)):
            walk_rows(j, urow2, input_rows)
            if j == 2:
                yield
        vector_sums()

    def vectors():
        for k, (place, others) in enumerate(((x, (xp, xo, xm)), (z, (zp, zo, zm)), (y, (yp, opp, ym)))):
            yield from sum_of_four(links, vec_o, 0, 16, place, others, vland, 64 * k)

    def swap(src, src_at, dst, dst_at, back_at):
        there = []
        for k in range(2):
            there.append(
                links.send(src.at[rows(src_at + 128 * k, 128), :], dst.at[rows(dst_at + 128 * k, 128), :], opp)
            )
            yield
        onward = []
        for k in range(2):
            there[k].wait_recv()
            theirs = dst.at[rows(back_at + 128 * k, 128), :]
            onward.append(links.send(theirs, theirs, sib))
            yield
        for copy in onward:
            copy.wait_recv()

    def result():
        yield from swap(front4, AFTER + 256 * c, other, 256 * c, 256 * c)
        each(HALF // SUB, SUB, cast_rows)

    def input_grads():
        yield from swap(gi, own_at + 256 * c, gi, own_at + 256 * c, other_at + 256 * c)

    jobs = dict(zip("abcd", ffs))
    jobs.update(zip("pqrst", (reduce_weights(k) for k in range(MATS))))
    jobs.update(M=compute(), B=other_half(), V=vectors(), O=result(), G=input_grads())
    arrived = 0
    for name in "".join(ORDER):
        next(jobs[name], None)
        links.settle(SETTLE)
        while shared[arrived:] and shared[arrived][0] < links.step - SETTLE:
            shared[arrived][1].wait_recv()
            arrived += 1
    for _, copy in shared[arrived:]:
        copy.wait_recv()
    links.finish()


def back(front_outs, adj, vecs, mats):
    g1, b1, fk, fv, fr, dec, rew, g2, b2, ck, cr = vecs
    flags, rest = front_outs[0], front_outs[1:]
    vm = pltpu.VMEM
    anywhere = pl.BlockSpec(memory_space=pl.ANY)
    vmem = pl.BlockSpec(memory_space=pltpu.VMEM)
    half = lambda dt: vm((HALF, D), dt)
    return pl.pallas_call(
        back_kernel,
        in_specs=[pl.BlockSpec(memory_space=pltpu.SMEM)] + [anywhere] * len(rest) + [anywhere]
        + [vmem] * 9 + [anywhere] * 5,
        out_specs=[vmem] * 5,
        out_shape=[vm((T, D), BF16), vm((T, D), F32), vm((16, D), F32), vm((2 * R_ROWS, D), F32), vm((FF_ROWS, D), F32)],
        scratch_shapes=[vm((4 * HALF, D), F32), vm((HALF, 128), F32), vm((HALF, 128), F32)]
        + [vm((HALF, HALF_D), BF16)] * 5 + [half(BF16)] + [vm((D, D), BF16)] * 3
        + [vm((2 * HALF, D), F32), vm((R_ROWS, D), F32)]
        + [half(BF16)] * 5 + [vm((128, D), F32)] * 3 + [half(F32)]
        + [vm((FF_ROWS, D), F32), vm((R_ROWS // 4, D), F32), vm((192, D), F32)]
        + [vm((8, D), F32)] * 4 + [vm((8 * NVEC, D), F32)] + [vm((SEG, D), F32)] * 2
        + [vm((1, D), F32)] * 2 + [vm((128, D), F32), vm((8, D), F32), vm((16, D), F32)]
        + [pltpu.SemaphoreType.DMA((COPIES,)), pltpu.SemaphoreType.DMA((COPIES,)),
           pltpu.SemaphoreType.DMA((48,)), pltpu.SemaphoreType.REGULAR, pltpu.SemaphoreType.REGULAR],
        compiler_params=pltpu.CompilerParams(collective_id=1, has_side_effects=True, vmem_limit_bytes=BACK_VMEM * 2**20),
        cost_estimate=pl.CostEstimate(flops=14 * T * D * D, bytes_accessed=60 * 2**20, transcendentals=0),
        name="back",
    )(flags, *rest, adj, g1, fk, fv, fr, dec, rew, g2, ck, cr, *mats[:5])


def finish_kernel(out, gi, vec, red, ff, *refs):
    out_o, gi_o, mats, ck_o, cv_o, vecs, sems = refs[0], refs[1], refs[2:7], refs[7], refs[8], refs[9:20], refs[20]
    pairs = [(gi, gi_o), (ff.at[pl.ds(0, D), :], ck_o), (ff.at[pl.ds(D, D), :], cv_o), (out, out_o)]
    for k in range(MATS):
        for core in range(2):
            src = red.at[pl.ds(core * R_ROWS + HALF_D * k, HALF_D), :]
            pairs.append((src, mats[(3, 4, 0, 1, 2)[k]].at[pl.ds(HALF_D * core, HALF_D), :]))
    copies = [pltpu.make_async_copy(src, dst, sems.at[k]) for k, (src, dst) in enumerate(pairs)]
    for copy in copies:
        copy.start()
    for k in range(NVEC):
        vecs[k][...] = vec[k : k + 1, :].reshape(D)
    for copy in copies:
        copy.wait()


def finish(out, gi, vec, red, ff):
    sds = jax.ShapeDtypeStruct
    anywhere = pl.BlockSpec(memory_space=pl.ANY)
    vmem = pl.BlockSpec(memory_space=pltpu.VMEM)
    return pl.pallas_call(
        finish_kernel,
        in_specs=[vmem] * 5,
        out_specs=[anywhere] * 9 + [vmem] * NVEC,
        out_shape=[sds((T, D), BF16), sds((T, D), F32)] + [sds((D, D), F32)] * 7 + [sds((D,), F32)] * NVEC,
        scratch_shapes=[pltpu.SemaphoreType.DMA((16,))],
        compiler_params=pltpu.CompilerParams(vmem_limit_bytes=FINISH_VMEM * 2**20),
        name="finish",
    )(out, gi, vec, red, ff)


def body(
    entering_activations, sample_sizes, initial_layernorm_scale, initial_layernorm_offset, temporal_lookup_fraction,
    temporal_content_fraction, temporal_gating_fraction, fading_speed_logarithm, present_reward,
    temporal_gating_matrix, temporal_lookup_matrix, temporal_content_matrix, temporal_emission_matrix,
    latter_layernorm_scale, latter_layernorm_offset, feedforward_lookup_fraction, feedforward_gating_fraction,
    feedforward_gating_matrix, feedforward_lookup_matrix, feedforward_content_matrix, upstream_adjoint,
):
    vecs = (
        initial_layernorm_scale, initial_layernorm_offset, temporal_lookup_fraction, temporal_content_fraction,
        temporal_gating_fraction, fading_speed_logarithm, present_reward, latter_layernorm_scale,
        latter_layernorm_offset, feedforward_lookup_fraction, feedforward_gating_fraction,
    )
    mats = (
        temporal_gating_matrix, temporal_lookup_matrix, temporal_content_matrix, temporal_emission_matrix,
        feedforward_gating_matrix, feedforward_lookup_matrix, feedforward_content_matrix,
    )
    half = (lax.axis_index("tensor") // 2).astype(jnp.int32).reshape(1)
    fronts = front(half, sample_sizes, entering_activations, upstream_adjoint, vecs, mats)
    out, grad_inputs, recw, keyw, valw, outw, chrec, chkey, chval, *g = finish(*back(fronts, upstream_adjoint, vecs, mats))
    return (
        out, grad_inputs, g[0], g[1], g[2], g[3], g[4], g[5], g[6], recw, keyw, valw, outw,
        g[7], g[8], g[9], g[10], chrec, chkey, chval,
    )


def solution(mesh):
    split = P("dp", None)
    in_specs = (split, split) + (P(),) * 16 + (P(None, "tensor"), P("tensor", None), split)
    out_specs = (split, split) + (P(),) * 16 + (P(None, "tensor"), P("tensor", None))
    return jax.shard_map(body, mesh=mesh, in_specs=in_specs, out_specs=out_specs, check_vma=False)
```
